32 devices in a mesh: groups: 2 (over y), shot: 4 (over z), freq: 4 (over x, core).
Axes of the slice: x: 2, y: 2, z: 4, core: 2. Of those that a mesh axis runs over, the one named last changes fastest.
Arguments:
- source_field: bfloat16 [4, 4096, 16, 2, 128], P('freq', ('groups', 'shot')), parts along dimension 1, may hold values from -6 to 6
- receiver_field: bfloat16 [4, 4096, 16, 2, 128], P('freq', ('groups', 'shot')), parts along dimension 1, may hold values from -6 to 6
- operator: bfloat16 [4, 32, 3, 2, 128, 128], P('freq', 'groups'), parts along dimension 1, may hold values from -0.21875 to 0.21875
- band_offsets: int32 [32, 3], P('groups'), parts along dimension 0, may hold values from -2 to 4, as said below
- survey_tiles: int32 [128, 2], P('groups'), parts along dimension 0, may hold values from 0 to 15, as said below
- survey_data: bfloat16 [4, 128, 2, 128, 128], P('freq', ('groups', 'shot')), parts along dimension 1, may hold values from -0.1875 to 0.1875
Outputs:
- image: float32 [2, 4096, 128], P(None, ('groups', 'shot', 'freq')), parts along dimension 1
The draws below stay inside these ranges and needn't reach their ends.
There are 2 independent parts, one for each index of `groups`. The reference program is written for one: setup_inputs(seed, part) draws one part's arguments, and reference() takes and returns one part's arrays. A program takes and returns all parts, laid end to end along the dimension named above; each array names one. Nothing has to cross between parts.
Inputs may be any that keep to these rules, and one draw needn't show every extreme that they name: `band_offsets`: in each row the offsets rise strictly; band k of row block i acts on cell block (i + offset) mod 16. `survey_tiles`: tile t has source block t div (4), so each source block has 4 tiles; the receiver blocks of one source block's tiles differ.
All inputs are finite; a program needn't handle non-finite values.
Results may differ from the reference program's by a relative error of at most 0.005.
Values may be sent and summed in bfloat16 or wider, within the bound.
No kernel may reach another device: no remote copies, remote signals or barrier semaphores. Data moves between devices by JAX's collectives and lax.ppermute only.
A program may use at most 256 MiB of HBM per device.

```python
import math
import jax
import jax.numpy as jnp
from jax import lax

X = 2048
NS = 2048
NR = 2048
B = 128
NBAND = 3
FREQS = 4
XB = 16
SB = 16
RB = 16
NTILE = 64


def draw_band_offsets(key, part):
    key = jax.random.fold_in(key, 11)
    keys = jax.random.split(key, 5)
    rows = jnp.arange(XB, dtype=jnp.int32)
    first = jax.random.randint(keys[0], (XB,), -2, 1)
    second = first + jax.random.randint(keys[1], (XB,), 1, 3)
    third = second + jax.random.randint(keys[2], (XB,), 1, 3)
    widest = jax.random.randint(keys[3], (), 0, XB)
    lowest = (widest + jax.random.randint(keys[4], (), 1, XB)) % XB
    first = jnp.where(rows == widest, 0, jnp.where(rows == lowest, -2, first))
    second = jnp.where(rows == widest, 2, second)
    third = jnp.where(rows == widest, 4, third)
    return jnp.stack([first, second, third], axis=1).astype(jnp.int32)


def receiver_order(one_key):
    return jax.random.permutation(one_key, RB)


def draw_survey_tiles(key, part):
    key = jax.random.fold_in(key, 23)
    keys = jax.random.split(key, SB)
    chosen = jax.vmap(receiver_order)(keys)[:, :RB // 4]
    source_blocks = jnp.broadcast_to(jnp.arange(SB, dtype=jnp.int32)[:, None], (SB, RB // 4))
    return jnp.stack([source_blocks.reshape(-1), chosen.reshape(-1)], axis=1).astype(jnp.int32)


def shard_levels(own_key, extent, cuts, smallest, largest):
    def one(dim, parts):
        heights = jax.random.uniform(jax.random.fold_in(jax.random.fold_in(own_key, 6), dim), (parts,), jnp.float32, smallest / len(cuts), largest / len(cuts))
        return jnp.repeat(jnp.exp(heights), extent[dim] // parts).reshape((-1,) + (1,) * (len(extent) - dim - 1))

    level = one(*cuts[0])
    for cut in cuts[1:]:
        level = level * one(*cut)
    return level


def bell_draw(stream_key, extent, spread, reach, cuts=(), kind=jnp.bfloat16):
    level = shard_levels(stream_key, extent, cuts, -0.22, 0.18) if cuts else 1.0
    values = jax.random.normal(stream_key, extent, jnp.float32) * spread * level
    return jnp.minimum(jnp.maximum(values, -reach), reach).astype(kind)


def setup_inputs(seed: int = 0, part: int = 0) -> dict:
    key_of = jax.random.split(jax.random.key(seed), 7)
    own_keys = jax.random.split(jax.random.fold_in(key_of[6], part), 7)
    source_field = bell_draw(own_keys[0], (FREQS, NS, XB, 2, B), 1.0, 6.0, ((0, 4), (1, 4)))
    receiver_field = bell_draw(own_keys[1], (FREQS, NR, XB, 2, B), 1.0, 6.0, ((0, 4), (1, 4)))
    operator = bell_draw(own_keys[2], (FREQS, XB, NBAND, 2, B, B), (2 * NBAND * B) ** -0.5, 0.21875, ((0, 4),))
    band_offsets = draw_band_offsets(jax.random.fold_in(jax.random.fold_in(key_of[6], part), 71), part)
    survey_tiles = draw_survey_tiles(jax.random.fold_in(jax.random.fold_in(key_of[6], part), 71), part)
    survey_data = bell_draw(own_keys[5], (FREQS, NTILE, 2, B, B), (8 * B) ** -0.5, 0.1875, ((0, 4), (1, 4)))
    return dict(source_field=source_field, receiver_field=receiver_field, operator=operator, band_offsets=band_offsets, survey_tiles=survey_tiles, survey_data=survey_data)


def cell_columns(band_offsets):
    rows = jnp.arange(XB, dtype=jnp.int32)[:, None]
    return ((rows + band_offsets) % XB).astype(jnp.int32)

def extrapolate(wavefield, operator, columns):
    row_count = wavefield.shape[0]
    real_part = operator[:, :, 0].astype(jnp.float32)
    imag_part = operator[:, :, 1].astype(jnp.float32)
    upper_rows = jnp.concatenate([real_part, imag_part], -1)
    lower_rows = jnp.concatenate([-imag_part, real_part], -1)
    real_block = jnp.concatenate([upper_rows, lower_rows], -2)
    chosen = jnp.take(wavefield, columns, axis=1).reshape(row_count, XB, NBAND, 2 * B).astype(jnp.float32)
    result = jnp.einsum('sikc,ikcd->sid', chosen, real_block, precision=lax.Precision.HIGHEST)
    return result.astype(jnp.bfloat16).reshape(row_count, XB, 2, B)

def data_product(source_cells, tile_data, survey_tiles):
    blocks = source_cells.reshape(SB, B, 2, X)

    def add_tile(running, item):
        one_tile, tile_pair = item
        chosen = blocks[tile_pair[0]]
        source_real = chosen[:, 0]
        source_imag = chosen[:, 1]
        data_real = one_tile[0].T
        data_imag = one_tile[1].T
        real_part = jnp.dot(data_real, source_real, preferred_element_type=jnp.float32) - jnp.dot(data_imag, source_imag, preferred_element_type=jnp.float32)
        imag_part = jnp.dot(data_real, source_imag, preferred_element_type=jnp.float32) + jnp.dot(data_imag, source_real, preferred_element_type=jnp.float32)
        return (running.at[tile_pair[1]].add(jnp.stack([real_part, imag_part], 1)), None)
    running = jnp.zeros((RB, B, 2, X), jnp.float32)
    running, _ = lax.scan(add_tile, running, (tile_data, survey_tiles))
    return running.reshape(NR, 2, X).astype(jnp.bfloat16)

def image_term(product, receiver_cells):
    left = product.reshape(NR, 2, XB, B).astype(jnp.float32)
    right = receiver_cells.reshape(NR, 2, XB, B).astype(jnp.float32)
    turned = jnp.stack([-right[:, 1], right[:, 0]], 1)
    both = jnp.stack([right, turned], 1)
    result = jnp.einsum('rctx,rocty->otxy', left, both, precision=lax.Precision.HIGHEST)
    return result.reshape(2, X, B)

def reference(source_field, receiver_field, operator, band_offsets, survey_tiles, survey_data):
    columns = cell_columns(band_offsets)
    image_sum = jnp.zeros((2, X, B), jnp.float32)
    for freq_slot in range(FREQS):
        source_next = extrapolate(source_field[freq_slot], operator[freq_slot], columns)
        receiver_next = extrapolate(receiver_field[freq_slot], operator[freq_slot], columns)
        source_cells = source_next.transpose(0, 2, 1, 3).reshape(NS, 2, X)
        receiver_cells = receiver_next.transpose(0, 2, 1, 3).reshape(NR, 2, X)
        product = data_product(source_cells, survey_data[freq_slot], survey_tiles)
        image_sum = image_sum + image_term(product, receiver_cells)
    return image_sum * (1.0 / math.sqrt(2.0 * NR * FREQS))
```

```python
import functools
import math

import jax
import jax.numpy as jnp
from jax import lax
from jax.experimental import pallas as pl
from jax.experimental.pallas import tpu as pltpu
from jax.sharding import PartitionSpec as P

NR = 2048
LIMIT = 48 * 1024 * 1024


def extrapolate(wavefield, operator, columns):
    row_count, blocks_x, components, block_size = wavefield.shape
    bands = columns.shape[1]
    real_part = operator[:, :, 0]
    imag_part = operator[:, :, 1]
    upper_rows = jnp.concatenate([real_part, imag_part], -1)
    lower_rows = jnp.concatenate([-imag_part, real_part], -1)
    real_block = jnp.concatenate([upper_rows, lower_rows], -2)
    real_block = real_block.reshape(blocks_x, bands, 2 * block_size, 2, block_size)
    chosen = jnp.take(wavefield, columns, axis=1).reshape(
        row_count, blocks_x, bands, 2 * block_size
    )
    result = jnp.einsum("sikc,ikcoy->soiy", chosen, real_block, preferred_element_type=jnp.float32)
    return result.astype(jnp.bfloat16)


def to_owners(wavefield, shot_count, own_cells):
    row_count = wavefield.shape[0]
    return wavefield.reshape(row_count, 2, shot_count, own_cells)


def to_tiles(wavefield, shot_count, own_cells):
    row_count, components, blocks_x, block_size = wavefield.shape
    if own_cells >= block_size:
        return to_owners(wavefield, shot_count, own_cells)
    factor = block_size // own_cells
    copies = jnp.broadcast_to(
        wavefield[:, :, :, None, :], (row_count, components, blocks_x, factor, block_size)
    )
    return copies.reshape(row_count, components, shot_count, block_size)


def data_product(source_cells, data_shard, survey_tiles, block_size, own_cells):
    source_count = source_cells.shape[0]
    receiver_blocks = NR // block_size
    blocks = source_cells.reshape(source_count // block_size, block_size, 2 * own_cells)
    block_ids = jnp.arange(receiver_blocks, dtype=jnp.int32)
    chosen = jnp.take(blocks, survey_tiles[:, 0], axis=0)
    products = jnp.einsum(
        "ncsr,nsk->ncrk",
        lax.all_gather(data_shard, "shot", axis=0, tiled=True),
        chosen,
        preferred_element_type=jnp.float32,
    )
    real_part = products[:, 0, :, :own_cells] - products[:, 1, :, own_cells:]
    imag_part = products[:, 0, :, own_cells:] + products[:, 1, :, :own_cells]
    contribution = jnp.concatenate([real_part, imag_part], -1)
    onehot = (survey_tiles[:, 1][:, None] == block_ids[None, :]).astype(jnp.float32)
    summed = jnp.einsum("nq,nrk->qrk", onehot, contribution, precision=lax.Precision.HIGHEST)
    return summed.reshape(NR, 2, own_cells).astype(jnp.bfloat16)


def image_tile(product, receiver_tile, block_size):
    row_count, components, own_cells = product.shape
    tiles_here = max(own_cells // block_size, 1)
    inner_cells = own_cells // tiles_here
    left = product.reshape(row_count, 2, tiles_here, inner_cells)
    right = receiver_tile.reshape(row_count, 2, tiles_here, block_size)
    turned = jnp.stack([-right[:, 1], right[:, 0]], 1)
    both = jnp.stack([right, turned], 1)
    result = jnp.einsum("rctx,rocty->otxy", left, both, preferred_element_type=jnp.float32)
    return result.reshape(2, own_cells, block_size)


def general_body(source_field, receiver_field, operator, band_offsets, survey_tiles, survey_data):
    shot_count = lax.axis_size("shot")
    freq_local = source_field.shape[0]
    blocks_x = source_field.shape[2]
    block_size = source_field.shape[4]
    own_cells = blocks_x * block_size // shot_count
    block_rows = jnp.arange(blocks_x, dtype=jnp.int32)[:, None]
    columns = (block_rows + band_offsets) % blocks_x
    source_next = extrapolate(source_field[0], operator[0], columns)
    receiver_next = extrapolate(receiver_field[0], operator[0], columns)
    source_send = to_owners(source_next, shot_count, own_cells)
    receiver_send = to_tiles(receiver_next, shot_count, own_cells)
    source_cells = lax.all_to_all(source_send, "shot", split_axis=2, concat_axis=0, tiled=True)
    receiver_tile = lax.all_to_all(receiver_send, "shot", split_axis=2, concat_axis=0, tiled=True)
    source_cells = source_cells.reshape(source_cells.shape[0], 2 * own_cells)
    product = data_product(source_cells, survey_data[0], survey_tiles, block_size, own_cells)
    receiver_tile = receiver_tile.reshape(receiver_tile.shape[0], 2, -1)
    image_sum = image_tile(product, receiver_tile, block_size)
    total_freqs = freq_local * lax.axis_size("freq")
    scaled = image_sum * (1.0 / math.sqrt(2.0 * NR * total_freqs))
    return lax.psum_scatter(scaled, "freq", scatter_dimension=1, tiled=True)


def params():
    return pltpu.CompilerParams(vmem_limit_bytes=LIMIT)


def extrapolate_kernel(order, columns, field, operator, first, second, stage, apart, *, rows, blocks, chunk):
    step = pl.program_id(0)
    lines = 2 * blocks
    half = blocks // 2

    @pl.when(step == 0)
    def _():
        def split(n, carry):
            start = pl.multiple_of(n * (chunk * lines), chunk * lines)
            stage[...] = field[pl.ds(start, chunk * lines), :].astype(jnp.float32)
            to = pl.ds(pl.multiple_of(n * chunk, chunk), chunk)
            for block in range(blocks):
                for part in range(2):
                    picked = stage[pl.ds(2 * block + part, chunk, stride=lines), :]
                    apart[block, to, part * 128:(part + 1) * 128] = picked.astype(jnp.bfloat16)
            return carry

        lax.fori_loop(0, rows // chunk, split, 0)

    block = order[step]
    inputs = []
    weights = []
    for band in range(operator.shape[1]):
        inputs.append(apart[columns[block, band]])
        real = operator[0, band, 0]
        imag = operator[0, band, 1]
        weights.append(jnp.concatenate([real, imag], 1))
        weights.append(jnp.concatenate([-imag, real], 1))
    result = jnp.dot(
        jnp.concatenate(inputs, 1), jnp.concatenate(weights, 0), preferred_element_type=jnp.float32
    ).astype(jnp.bfloat16)

    @pl.when(step < half)
    def _():
        first[0] = result

    @pl.when(step >= half)
    def _():
        second[0] = result


def extrapolate_blocks(field, operator, columns, order):
    rows, blocks, _, size = field.shape
    half = blocks // 2
    bands = columns.shape[1]
    chunk = 32
    flat = field.reshape(rows * blocks * 2, size)
    out = jax.ShapeDtypeStruct((half, rows, 2 * size), jnp.bfloat16)
    return pl.pallas_call(
        functools.partial(extrapolate_kernel, rows=rows, blocks=blocks, chunk=chunk),
        grid_spec=pltpu.PrefetchScalarGridSpec(
            num_scalar_prefetch=2,
            grid=(blocks,),
            in_specs=[
                pl.BlockSpec((rows * blocks * 2, size), lambda j, o, c: (0, 0)),
                pl.BlockSpec((1, bands, 2, size, size), lambda j, o, c: (o[j], 0, 0, 0, 0)),
            ],
            out_specs=[
                pl.BlockSpec((1, rows, 2 * size), lambda j, o, c: (jnp.minimum(j, half - 1), 0, 0)),
                pl.BlockSpec((1, rows, 2 * size), lambda j, o, c: (jnp.maximum(j - half, 0), 0, 0)),
            ],
            scratch_shapes=[
                pltpu.VMEM((chunk * blocks * 2, size), jnp.float32),
                pltpu.VMEM((blocks, rows, 2 * size), jnp.bfloat16),
            ],
        ),
        out_shape=[out, out],
        compiler_params=params(),
        cost_estimate=pl.CostEstimate(
            flops=2 * rows * blocks * bands * 4 * size * size,
            bytes_accessed=16 * 1024 * 1024,
            transcendentals=0,
        ),
        name="extrapolate",
    )(order, columns, flat, operator)


def product_kernel(near_ids, far_ids, near, far, near_data, far_data, out, turned, total):
    size = near_data.shape[2]
    tiles = near_data.shape[0]
    sources = near.shape[1] // size
    per_source = tiles // sources

    @pl.when(pl.program_id(0) == 0)
    def _():
        for side, data in enumerate((near_data, far_data)):
            for tile in range(tiles):
                for part in range(2):
                    turned[side * tiles + tile, :, part * size:(part + 1) * size] = data[tile, part].T

    total[...] = jnp.zeros_like(total)
    for side, (field, ids) in enumerate(((near, near_ids), (far, far_ids))):
        for source in range(sources):
            upper = field[0, source * size:(source + 1) * size, :]
            lower = jnp.concatenate([-upper[:, size:], upper[:, :size]], 1)
            both = jnp.concatenate([upper, lower], 0)
            first = side * tiles + source * per_source
            left = turned[first:first + per_source].reshape(per_source * size, 2 * size)
            result = jnp.dot(left, both, preferred_element_type=jnp.float32)
            for tile in range(per_source):
                total[ids[source * per_source + tile]] += result[tile * size:(tile + 1) * size]
    for block in range(total.shape[0]):
        out[0, :, block * size:(block + 1) * size] = total[block].T.astype(jnp.bfloat16)


def product_blocks(near, far, near_data, far_data, near_ids, far_ids):
    blocks, rows, width = near.shape
    tiles, _, size, _ = near_data.shape
    receivers = NR // size
    field_spec = pl.BlockSpec((1, rows, width), lambda j, a, b: (j, 0, 0))
    data_spec = pl.BlockSpec(near_data.shape, lambda j, a, b: (0, 0, 0, 0))
    return pl.pallas_call(
        product_kernel,
        grid_spec=pltpu.PrefetchScalarGridSpec(
            num_scalar_prefetch=2,
            grid=(blocks,),
            in_specs=[field_spec, field_spec, data_spec, data_spec],
            out_specs=pl.BlockSpec((1, width, NR), lambda j, a, b: (j, 0, 0)),
            scratch_shapes=[
                pltpu.VMEM((2 * tiles, size, width), jnp.bfloat16),
                pltpu.VMEM((receivers, size, width), jnp.float32),
            ],
        ),
        out_shape=jax.ShapeDtypeStruct((blocks, width, NR), jnp.bfloat16),
        compiler_params=params(),
        cost_estimate=pl.CostEstimate(
            flops=2 * blocks * 2 * tiles * size * width * width,
            bytes_accessed=16 * 1024 * 1024,
            transcendentals=0,
        ),
        name="product",
    )(near_ids, far_ids, near, far, near_data, far_data)


def image_kernel(origin, product, field, before, out, *, size):
    both = jnp.dot(product[0], field[0], preferred_element_type=jnp.float32)
    out[0, 0] = before[0, 0] + both[:size, :size] + both[size:, size:]
    out[0, 1] = before[0, 1] + both[size:, :size] - both[:size, size:]


def first_image_kernel(origin, product, field, out, *, size):
    both = jnp.dot(product[0], field[0], preferred_element_type=jnp.float32)
    out[0, 0] = both[:size, :size] + both[size:, size:]
    out[0, 1] = both[size:, :size] - both[:size, size:]


def image_blocks(product, field, origin, before=None):
    blocks, rows, width = field.shape
    size = width // 2
    image_spec = pl.BlockSpec((1, 2, size, size), lambda j, o: (j, 0, 0, 0))
    specs = [
        pl.BlockSpec((1, width, rows), lambda j, o: (j, 0, o[0])),
        pl.BlockSpec((1, rows, width), lambda j, o: (j, 0, 0)),
    ]
    values = [product, field]
    kernel = first_image_kernel
    if before is not None:
        specs.append(image_spec)
        values.append(before)
        kernel = image_kernel
    return pl.pallas_call(
        functools.partial(kernel, size=size),
        grid_spec=pltpu.PrefetchScalarGridSpec(
            num_scalar_prefetch=1, grid=(blocks,), in_specs=specs, out_specs=image_spec
        ),
        out_shape=jax.ShapeDtypeStruct((blocks, 2, size, size), jnp.float32),
        compiler_params=params(),
        cost_estimate=pl.CostEstimate(
            flops=2 * blocks * rows * width * width,
            bytes_accessed=6 * 1024 * 1024,
            transcendentals=0,
        ),
        name="image",
    )(origin, *values)


def exchange(value, axis, bit):
    count = lax.axis_size(axis)
    return lax.ppermute(value, axis, [(i, i ^ bit) for i in range(count)])


def keep_and_send(value, bit):
    keep = lax.dynamic_index_in_dim(value, bit, 0, keepdims=False)
    send = lax.dynamic_index_in_dim(value, 1 - bit, 0, keepdims=False)
    return keep, send


def split_body(source_field, receiver_field, operator, band_offsets, survey_tiles, survey_data):
    blocks = source_field.shape[2]
    size = source_field.shape[4]
    tiles = survey_data.shape[1]
    shot = lax.axis_index("shot")
    freq = lax.axis_index("freq")
    place = shot % 2
    per_owner = blocks // lax.axis_size("shot")
    steps = jnp.arange(blocks // 2, dtype=jnp.int32)
    own = steps % per_owner + per_owner * (2 * (steps // per_owner) + place)
    other = steps % per_owner + per_owner * (2 * (steps // per_owner) + 1 - place)
    order = jnp.concatenate([own, other])
    columns = (jnp.arange(blocks, dtype=jnp.int32)[:, None] + band_offsets) % blocks

    far_data = exchange(survey_data[0], "shot", 1)
    receiver_own, receiver_other = extrapolate_blocks(receiver_field[0], operator[0], columns, order)
    receiver_3 = exchange(receiver_other, "shot", 3)
    receiver_2 = exchange(receiver_own, "shot", 2)
    source_own, source_other = extrapolate_blocks(source_field[0], operator[0], columns, order)
    source_far = exchange(source_other, "shot", 1)
    receiver_1 = exchange(receiver_other, "shot", 1)

    ids = survey_tiles[:, 1]
    near_ids = lax.dynamic_slice_in_dim(ids, shot * tiles, tiles)
    far_ids = lax.dynamic_slice_in_dim(ids, (shot ^ 1) * tiles, tiles)
    product = product_blocks(source_own, source_far, survey_data[0], far_data, near_ids, far_ids)
    image = image_blocks(product, receiver_own, shot[None])
    image = image_blocks(product, receiver_1, (shot ^ 1)[None], image)
    image = image_blocks(product, receiver_2, (shot ^ 2)[None], image)
    image = image_blocks(product, receiver_3, (shot ^ 3)[None], image)

    image = image.reshape(2, 2, 2, 2, size, size)
    keep, send = keep_and_send(image.transpose(2, 0, 1, 3, 4, 5), freq % 2)
    image = keep + exchange(send, "freq", 1)
    keep, send = keep_and_send(image.transpose(1, 0, 2, 3, 4), freq // 2)
    image = keep + exchange(send, "freq", 2)
    keep, send = keep_and_send(image, shot // 2)
    image = keep + exchange(send, "shot", 2)
    total_freqs = source_field.shape[0] * lax.axis_size("freq")
    return image * (1.0 / math.sqrt(2.0 * NR * total_freqs))


def body(source_field, *rest):
    fits = (
        lax.axis_size("shot") == 4
        and lax.axis_size("freq") == 4
        and source_field.shape[1:] == (512, 16, 2, 128)
    )
    return (split_body if fits else general_body)(source_field, *rest)


def solution(mesh):
    return jax.shard_map(
        body,
        mesh=mesh,
        in_specs=(
            P("freq", ("groups", "shot"), None, None, None),
            P("freq", ("groups", "shot"), None, None, None),
            P("freq", "groups", None, None, None, None),
            P("groups", None),
            P("groups", None),
            P("freq", ("groups", "shot"), None, None, None),
        ),
        out_specs=P(None, ("groups", "shot", "freq"), None),
        check_vma=False,
    )
```

```python
import functools
import math

import jax
import jax.numpy as jnp
from jax import lax
from jax.experimental import pallas as pl
from jax.experimental.pallas import tpu as pltpu
from jax.sharding import PartitionSpec as P

NR = 2048
PARTS = 2
LIMIT = 48 * 1024 * 1024
SMALL = pl.CostEstimate(flops=1000, bytes_accessed=1000, transcendentals=0)


def extrapolate(wavefield, operator, columns):
    row_count, blocks_x, components, block_size = wavefield.shape
    bands = columns.shape[1]
    real_part = operator[:, :, 0]
    imag_part = operator[:, :, 1]
    upper_rows = jnp.concatenate([real_part, imag_part], -1)
    lower_rows = jnp.concatenate([-imag_part, real_part], -1)
    real_block = jnp.concatenate([upper_rows, lower_rows], -2)
    real_block = real_block.reshape(blocks_x, bands, 2 * block_size, 2, block_size)
    chosen = jnp.take(wavefield, columns, axis=1).reshape(
        row_count, blocks_x, bands, 2 * block_size
    )
    result = jnp.einsum("sikc,ikcoy->soiy", chosen, real_block, preferred_element_type=jnp.float32)
    return result.astype(jnp.bfloat16)


def to_owners(wavefield, shot_count, own_cells):
    row_count = wavefield.shape[0]
    return wavefield.reshape(row_count, 2, shot_count, own_cells)


def to_tiles(wavefield, shot_count, own_cells):
    row_count, components, blocks_x, block_size = wavefield.shape
    if own_cells >= block_size:
        return to_owners(wavefield, shot_count, own_cells)
    factor = block_size // own_cells
    copies = jnp.broadcast_to(
        wavefield[:, :, :, None, :], (row_count, components, blocks_x, factor, block_size)
    )
    return copies.reshape(row_count, components, shot_count, block_size)


def data_product(source_cells, data_shard, survey_tiles, block_size, own_cells):
    source_count = source_cells.shape[0]
    receiver_blocks = NR // block_size
    blocks = source_cells.reshape(source_count // block_size, block_size, 2 * own_cells)
    block_ids = jnp.arange(receiver_blocks, dtype=jnp.int32)
    chosen = jnp.take(blocks, survey_tiles[:, 0], axis=0)
    products = jnp.einsum(
        "ncsr,nsk->ncrk",
        lax.all_gather(data_shard, "shot", axis=0, tiled=True),
        chosen,
        preferred_element_type=jnp.float32,
    )
    real_part = products[:, 0, :, :own_cells] - products[:, 1, :, own_cells:]
    imag_part = products[:, 0, :, own_cells:] + products[:, 1, :, :own_cells]
    contribution = jnp.concatenate([real_part, imag_part], -1)
    onehot = (survey_tiles[:, 1][:, None] == block_ids[None, :]).astype(jnp.float32)
    summed = jnp.einsum("nq,nrk->qrk", onehot, contribution, precision=lax.Precision.HIGHEST)
    return summed.reshape(NR, 2, own_cells).astype(jnp.bfloat16)


def image_tile(product, receiver_tile, block_size):
    row_count, components, own_cells = product.shape
    tiles_here = max(own_cells // block_size, 1)
    inner_cells = own_cells // tiles_here
    left = product.reshape(row_count, 2, tiles_here, inner_cells)
    right = receiver_tile.reshape(row_count, 2, tiles_here, block_size)
    turned = jnp.stack([-right[:, 1], right[:, 0]], 1)
    both = jnp.stack([right, turned], 1)
    result = jnp.einsum("rctx,rocty->otxy", left, both, preferred_element_type=jnp.float32)
    return result.reshape(2, own_cells, block_size)


def general_body(source_field, receiver_field, operator, band_offsets, survey_tiles, survey_data):
    shot_count = lax.axis_size("shot")
    freq_local = source_field.shape[0]
    blocks_x = source_field.shape[2]
    block_size = source_field.shape[4]
    own_cells = blocks_x * block_size // shot_count
    block_rows = jnp.arange(blocks_x, dtype=jnp.int32)[:, None]
    columns = (block_rows + band_offsets) % blocks_x
    source_next = extrapolate(source_field[0], operator[0], columns)
    receiver_next = extrapolate(receiver_field[0], operator[0], columns)
    source_send = to_owners(source_next, shot_count, own_cells)
    receiver_send = to_tiles(receiver_next, shot_count, own_cells)
    source_cells = lax.all_to_all(source_send, "shot", split_axis=2, concat_axis=0, tiled=True)
    receiver_tile = lax.all_to_all(receiver_send, "shot", split_axis=2, concat_axis=0, tiled=True)
    source_cells = source_cells.reshape(source_cells.shape[0], 2 * own_cells)
    product = data_product(source_cells, survey_data[0], survey_tiles, block_size, own_cells)
    receiver_tile = receiver_tile.reshape(receiver_tile.shape[0], 2, -1)
    image_sum = image_tile(product, receiver_tile, block_size)
    total_freqs = freq_local * lax.axis_size("freq")
    scaled = image_sum * (1.0 / math.sqrt(2.0 * NR * total_freqs))
    return lax.psum_scatter(scaled, "freq", scatter_dimension=1, tiled=True)


def params():
    return pltpu.CompilerParams(vmem_limit_bytes=LIMIT)


def extrapolate_kernel(order, columns, field, operator, *refs, rows, blocks, chunk):
    first, second, stage, apart = refs[-4:]
    step = pl.program_id(0)
    lines = 2 * blocks
    half = blocks // 2

    @pl.when(step == 0)
    def _():
        def split(n, carry):
            start = pl.multiple_of(n * (chunk * lines), chunk * lines)
            stage[...] = field[pl.ds(start, chunk * lines), :].astype(jnp.float32)
            to = pl.ds(pl.multiple_of(n * chunk, chunk), chunk)
            for block in range(blocks):
                for part in range(2):
                    picked = stage[pl.ds(2 * block + part, chunk, stride=lines), :]
                    apart[block, to, part * 128:(part + 1) * 128] = picked.astype(jnp.bfloat16)
            return carry

        lax.fori_loop(0, rows // chunk, split, 0)

    block = order[step]
    inputs = []
    weights = []
    for band in range(operator.shape[1]):
        inputs.append(apart[columns[block, band]])
        real = operator[0, band, 0]
        imag = operator[0, band, 1]
        weights.append(jnp.concatenate([real, imag], 1))
        weights.append(jnp.concatenate([-imag, real], 1))
    result = jnp.dot(
        jnp.concatenate(inputs, 1), jnp.concatenate(weights, 0), preferred_element_type=jnp.float32
    ).astype(jnp.bfloat16)

    @pl.when(step < half)
    def _():
        first[0] = result

    @pl.when(step >= half)
    def _():
        second[0] = result


def extrapolate_rows(field, operator, columns, order, part, parts, after=()):
    rows, blocks, _, size = field.shape
    rows = rows // parts
    half = blocks // 2
    bands = columns.shape[1]
    chunk = 32
    flat = field.reshape(parts * rows * blocks * 2, size)
    out = jax.ShapeDtypeStruct((half, rows, 2 * size), jnp.bfloat16)
    return pl.pallas_call(
        functools.partial(extrapolate_kernel, rows=rows, blocks=blocks, chunk=chunk),
        grid_spec=pltpu.PrefetchScalarGridSpec(
            num_scalar_prefetch=2,
            grid=(blocks,),
            in_specs=[
                pl.BlockSpec((rows * blocks * 2, size), lambda j, o, c: (part, 0)),
                pl.BlockSpec((1, bands, 2, size, size), lambda j, o, c: (o[j], 0, 0, 0, 0)),
            ]
            + [pl.BlockSpec(memory_space=pl.ANY)] * len(after),
            out_specs=[
                pl.BlockSpec((1, rows, 2 * size), lambda j, o, c: (jnp.minimum(j, half - 1), 0, 0)),
                pl.BlockSpec((1, rows, 2 * size), lambda j, o, c: (jnp.maximum(j - half, 0), 0, 0)),
            ],
            scratch_shapes=[
                pltpu.VMEM((chunk * blocks * 2, size), jnp.float32),
                pltpu.VMEM((blocks, rows, 2 * size), jnp.bfloat16),
            ],
        ),
        out_shape=[out, out],
        compiler_params=params(),
        cost_estimate=SMALL,
        name="extrapolate",
    )(order, columns, flat, operator, *after)


def product_kernel(near_ids, far_ids, *refs, parts):
    near = refs[:parts]
    far = refs[parts:2 * parts]
    near_data, far_data, out, turned, total = refs[2 * parts:]
    size = near_data.shape[2]
    tiles = near_data.shape[0]
    part_sources = near[0].shape[1] // size
    per_source = tiles // (parts * part_sources)

    @pl.when(pl.program_id(0) == 0)
    def _():
        for side, data in enumerate((near_data, far_data)):
            for tile in range(tiles):
                for part in range(2):
                    turned[side * tiles + tile, :, part * size:(part + 1) * size] = data[tile, part].T

    total[...] = jnp.zeros_like(total)
    for side, (fields, ids) in enumerate(((near, near_ids), (far, far_ids))):
        for source in range(parts * part_sources):
            place = (source % part_sources) * size
            upper = fields[source // part_sources][0, place:place + size, :]
            lower = jnp.concatenate([-upper[:, size:], upper[:, :size]], 1)
            both = jnp.concatenate([upper, lower], 0)
            first = side * tiles + source * per_source
            left = turned[first:first + per_source].reshape(per_source * size, 2 * size)
            result = jnp.dot(left, both, preferred_element_type=jnp.float32)
            for tile in range(per_source):
                total[ids[source * per_source + tile]] += result[tile * size:(tile + 1) * size]
    for block in range(total.shape[0]):
        out[0, :, block * size:(block + 1) * size] = total[block].T.astype(jnp.bfloat16)


def product_blocks(near, far, near_data, far_data, near_ids, far_ids):
    blocks, rows, width = near[0].shape
    tiles, _, size, _ = near_data.shape
    receivers = NR // size
    field_spec = pl.BlockSpec((1, rows, width), lambda j, a, b: (j, 0, 0))
    data_spec = pl.BlockSpec(near_data.shape, lambda j, a, b: (0, 0, 0, 0))
    return pl.pallas_call(
        functools.partial(product_kernel, parts=len(near)),
        grid_spec=pltpu.PrefetchScalarGridSpec(
            num_scalar_prefetch=2,
            grid=(blocks,),
            in_specs=[field_spec] * (2 * len(near)) + [data_spec, data_spec],
            out_specs=pl.BlockSpec((1, width, NR), lambda j, a, b: (j, 0, 0)),
            scratch_shapes=[
                pltpu.VMEM((2 * tiles, size, width), jnp.bfloat16),
                pltpu.VMEM((receivers, size, width), jnp.float32),
            ],
        ),
        out_shape=jax.ShapeDtypeStruct((blocks, width, NR), jnp.bfloat16),
        compiler_params=params(),
        cost_estimate=SMALL,
        name="product",
    )(near_ids, far_ids, *near, *far, near_data, far_data)


def image_kernel(places, *refs, pieces, size):
    out = refs[-1]
    both = jnp.dot(refs[0][0], refs[pieces][0], preferred_element_type=jnp.float32)
    for n in range(1, pieces):
        both += jnp.dot(refs[n][0], refs[pieces + n][0], preferred_element_type=jnp.float32)
    real = both[:size, :size] + both[size:, size:]
    imag = both[size:, :size] - both[:size, size:]
    if len(refs) > 2 * pieces + 1:
        real += refs[2 * pieces][0, 0]
        imag += refs[2 * pieces][0, 1]
    out[0, 0] = real
    out[0, 1] = imag


def image_blocks(product, fields, places, before=None):
    blocks, rows, width = fields[0].shape
    size = width // 2
    pieces = len(fields)
    image_spec = pl.BlockSpec((1, 2, size, size), lambda j, o: (j, 0, 0, 0))
    specs = [pl.BlockSpec((1, width, rows), lambda j, o, n=n: (j, 0, o[n])) for n in range(pieces)]
    specs += [pl.BlockSpec((1, rows, width), lambda j, o: (j, 0, 0))] * pieces
    values = [product] * pieces + list(fields)
    if before is not None:
        specs.append(image_spec)
        values.append(before)
    return pl.pallas_call(
        functools.partial(image_kernel, pieces=pieces, size=size),
        grid_spec=pltpu.PrefetchScalarGridSpec(
            num_scalar_prefetch=1, grid=(blocks,), in_specs=specs, out_specs=image_spec
        ),
        out_shape=jax.ShapeDtypeStruct((blocks, 2, size, size), jnp.float32),
        compiler_params=params(),
        cost_estimate=SMALL,
        name="image",
    )(places, *values)


def exchange(value, axis, bit):
    count = lax.axis_size(axis)
    return lax.ppermute(value, axis, [(i, i ^ bit) for i in range(count)])


def following(value, earlier):
    return lax.optimization_barrier((value,) + earlier)[0] if earlier else value


def keep_and_send(value, bit):
    keep = lax.dynamic_index_in_dim(value, bit, 0, keepdims=False)
    send = lax.dynamic_index_in_dim(value, 1 - bit, 0, keepdims=False)
    return keep, send


def split_body(source_field, receiver_field, operator, band_offsets, survey_tiles, survey_data):
    blocks = source_field.shape[2]
    size = source_field.shape[4]
    tiles = survey_data.shape[1]
    shot = lax.axis_index("shot")
    freq = lax.axis_index("freq")
    place = shot % 2
    per_owner = blocks // lax.axis_size("shot")
    steps = jnp.arange(blocks // 2, dtype=jnp.int32)
    own = steps % per_owner + per_owner * (2 * (steps // per_owner) + place)
    other = steps % per_owner + per_owner * (2 * (steps // per_owner) + 1 - place)
    order = jnp.concatenate([own, other])
    columns = (jnp.arange(blocks, dtype=jnp.int32)[:, None] + band_offsets) % blocks

    far_data = exchange(survey_data[0], "shot", 1)
    make = functools.partial(extrapolate_rows, operator=operator[0], columns=columns, order=order, parts=PARTS)
    receiver = []
    last = ()
    for part in range(PARTS):
        receiver.append(make(receiver_field[0], part=part, after=last))
        last = tuple(receiver[-1])
    source = []
    for part in range(PARTS):
        source.append(make(source_field[0], part=part, after=last + (far_data,) * (part == PARTS - 1)))
        last = tuple(source[-1])
    source_far = [exchange(source[part][1], "shot", 1) for part in range(PARTS)]
    ahead = {2: (), 3: (), 1: (far_data,)}
    arrived = []
    for part in range(PARTS):
        own_rows, other_rows = receiver[part]
        sent = {}
        for bit, rows in ((2, own_rows), (3, other_rows), (1, other_rows)):
            sent[bit] = exchange(following(rows, ahead[bit]), "shot", bit)
        ahead = {2: (sent[2],), 3: (sent[3],), 1: (sent[2], sent[3])}
        arrived.append(sent)

    ids = survey_tiles[:, 1]
    near_ids = lax.dynamic_slice_in_dim(ids, shot * tiles, tiles)
    far_ids = lax.dynamic_slice_in_dim(ids, (shot ^ 1) * tiles, tiles)
    product = product_blocks(
        [rows[0] for rows in source], source_far, survey_data[0], far_data, near_ids, far_ids
    )
    places = jnp.stack([shot * PARTS + part for part in range(PARTS)])
    image = image_blocks(product, [rows[0] for rows in receiver], places)
    for part in range(PARTS):
        places = jnp.stack([(shot ^ bit) * PARTS + part for bit in (1, 2, 3)])
        image = image_blocks(product, [arrived[part][bit] for bit in (1, 2, 3)], places, image)

    image = image.reshape(2, 2, 2, 2, size, size)
    keep, send = keep_and_send(image.transpose(2, 0, 1, 3, 4, 5), freq % 2)
    image = keep + exchange(send, "freq", 1)
    keep, send = keep_and_send(image.transpose(1, 0, 2, 3, 4), freq // 2)
    image = keep + exchange(send, "freq", 2)
    keep, send = keep_and_send(image, shot // 2)
    image = keep + exchange(send, "shot", 2)
    total_freqs = source_field.shape[0] * lax.axis_size("freq")
    return image * (1.0 / math.sqrt(2.0 * NR * total_freqs))


def body(source_field, *rest):
    fits = (
        lax.axis_size("shot") == 4
        and lax.axis_size("freq") == 4
        and source_field.shape[1:] == (512, 16, 2, 128)
    )
    return (split_body if fits else general_body)(source_field, *rest)


def solution(mesh):
    return jax.shard_map(
        body,
        mesh=mesh,
        in_specs=(
            P("freq", ("groups", "shot"), None, None, None),
            P("freq", ("groups", "shot"), None, None, None),
            P("freq", "groups", None, None, None, None),
            P("groups", None),
            P("groups", None),
            P("freq", ("groups", "shot"), None, None, None),
        ),
        out_specs=P(None, ("groups", "shot", "freq"), None),
        check_vma=False,
    )
```

```python
import functools
import math

import jax
import jax.numpy as jnp
from jax import lax
from jax.experimental import pallas as pl
from jax.experimental.pallas import tpu as pltpu
from jax.sharding import PartitionSpec as P

NR = 2048
LIMIT = 24 * 1024 * 1024
SMALL = pl.CostEstimate(flops=1000, bytes_accessed=1000, transcendentals=0)


def extrapolate(wavefield, operator, columns):
    row_count, blocks_x, components, block_size = wavefield.shape
    bands = columns.shape[1]
    real_part = operator[:, :, 0]
    imag_part = operator[:, :, 1]
    upper_rows = jnp.concatenate([real_part, imag_part], -1)
    lower_rows = jnp.concatenate([-imag_part, real_part], -1)
    real_block = jnp.concatenate([upper_rows, lower_rows], -2)
    real_block = real_block.reshape(blocks_x, bands, 2 * block_size, 2, block_size)
    chosen = jnp.take(wavefield, columns, axis=1).reshape(
        row_count, blocks_x, bands, 2 * block_size
    )
    result = jnp.einsum("sikc,ikcoy->soiy", chosen, real_block, preferred_element_type=jnp.float32)
    return result.astype(jnp.bfloat16)


def to_owners(wavefield, shot_count, own_cells):
    row_count = wavefield.shape[0]
    return wavefield.reshape(row_count, 2, shot_count, own_cells)


def to_tiles(wavefield, shot_count, own_cells):
    row_count, components, blocks_x, block_size = wavefield.shape
    if own_cells >= block_size:
        return to_owners(wavefield, shot_count, own_cells)
    factor = block_size // own_cells
    copies = jnp.broadcast_to(
        wavefield[:, :, :, None, :], (row_count, components, blocks_x, factor, block_size)
    )
    return copies.reshape(row_count, components, shot_count, block_size)


def data_product(source_cells, data_shard, survey_tiles, block_size, own_cells):
    source_count = source_cells.shape[0]
    receiver_blocks = NR // block_size
    blocks = source_cells.reshape(source_count // block_size, block_size, 2 * own_cells)
    block_ids = jnp.arange(receiver_blocks, dtype=jnp.int32)
    chosen = jnp.take(blocks, survey_tiles[:, 0], axis=0)
    products = jnp.einsum(
        "ncsr,nsk->ncrk",
        lax.all_gather(data_shard, "shot", axis=0, tiled=True),
        chosen,
        preferred_element_type=jnp.float32,
    )
    real_part = products[:, 0, :, :own_cells] - products[:, 1, :, own_cells:]
    imag_part = products[:, 0, :, own_cells:] + products[:, 1, :, :own_cells]
    contribution = jnp.concatenate([real_part, imag_part], -1)
    onehot = (survey_tiles[:, 1][:, None] == block_ids[None, :]).astype(jnp.float32)
    summed = jnp.einsum("nq,nrk->qrk", onehot, contribution, precision=lax.Precision.HIGHEST)
    return summed.reshape(NR, 2, own_cells).astype(jnp.bfloat16)


def image_tile(product, receiver_tile, block_size):
    row_count, components, own_cells = product.shape
    tiles_here = max(own_cells // block_size, 1)
    inner_cells = own_cells // tiles_here
    left = product.reshape(row_count, 2, tiles_here, inner_cells)
    right = receiver_tile.reshape(row_count, 2, tiles_here, block_size)
    turned = jnp.stack([-right[:, 1], right[:, 0]], 1)
    both = jnp.stack([right, turned], 1)
    result = jnp.einsum("rctx,rocty->otxy", left, both, preferred_element_type=jnp.float32)
    return result.reshape(2, own_cells, block_size)


def general_body(source_field, receiver_field, operator, band_offsets, survey_tiles, survey_data):
    shot_count = lax.axis_size("shot")
    freq_local = source_field.shape[0]
    blocks_x = source_field.shape[2]
    block_size = source_field.shape[4]
    own_cells = blocks_x * block_size // shot_count
    block_rows = jnp.arange(blocks_x, dtype=jnp.int32)[:, None]
    columns = (block_rows + band_offsets) % blocks_x
    source_next = extrapolate(source_field[0], operator[0], columns)
    receiver_next = extrapolate(receiver_field[0], operator[0], columns)
    source_send = to_owners(source_next, shot_count, own_cells)
    receiver_send = to_tiles(receiver_next, shot_count, own_cells)
    source_cells = lax.all_to_all(source_send, "shot", split_axis=2, concat_axis=0, tiled=True)
    receiver_tile = lax.all_to_all(receiver_send, "shot", split_axis=2, concat_axis=0, tiled=True)
    source_cells = source_cells.reshape(source_cells.shape[0], 2 * own_cells)
    product = data_product(source_cells, survey_data[0], survey_tiles, block_size, own_cells)
    receiver_tile = receiver_tile.reshape(receiver_tile.shape[0], 2, -1)
    image_sum = image_tile(product, receiver_tile, block_size)
    total_freqs = freq_local * lax.axis_size("freq")
    scaled = image_sum * (1.0 / math.sqrt(2.0 * NR * total_freqs))
    return lax.psum_scatter(scaled, "freq", scatter_dimension=1, tiled=True)


def params():
    return pltpu.CompilerParams(vmem_limit_bytes=LIMIT)


def extrapolate_kernel(order, columns, field, operator, *refs, sizes, rows, blocks, chunk, listed):
    stage, apart = refs[-2:]
    outs = refs[-2 - len(sizes):-2]
    step = pl.program_id(0)
    lines = 2 * blocks
    bands = operator.shape[1]

    @pl.when(step == 0)
    def _():
        if listed:
            wanted = [columns[order[n // bands], n % bands] for n in range(sum(sizes) * bands)]
        else:
            wanted = list(range(blocks))

        def split(n, carry):
            start = pl.multiple_of(n * (chunk * lines), chunk * lines)
            stage[...] = field[pl.ds(start, chunk * lines), :].astype(jnp.float32)
            to = pl.ds(pl.multiple_of(n * chunk, chunk), chunk)
            for slot, block in enumerate(wanted):
                for part in range(2):
                    picked = stage[pl.ds(2 * block + part, chunk, stride=lines), :]
                    apart[slot, to, part * 128:(part + 1) * 128] = picked.astype(jnp.bfloat16)
            return carry

        lax.fori_loop(0, rows // chunk, split, 0)

    block = order[step]
    inputs = []
    weights = []
    for band in range(bands):
        inputs.append(apart[step * bands + band if listed else columns[block, band]])
        real = operator[0, band, 0]
        imag = operator[0, band, 1]
        weights.append(jnp.concatenate([real, imag], 1))
        weights.append(jnp.concatenate([-imag, real], 1))
    result = jnp.dot(
        jnp.concatenate(inputs, 1), jnp.concatenate(weights, 0), preferred_element_type=jnp.float32
    ).astype(jnp.bfloat16)
    first = 0
    for out, count in zip(outs, sizes):
        if len(sizes) == 1:
            out[0] = result
        else:
            @pl.when((step >= first) & (step < first + count))
            def _(out=out):
                out[0] = result
        first += count


def extrapolate_blocks(field, operator, columns, sets, listed=False, after=()):
    rows, blocks, _, size = field.shape
    bands = columns.shape[1]
    chunk = 32
    sizes = [len(one) for one in sets]
    order = jnp.concatenate(sets)
    firsts = [sum(sizes[:n]) for n in range(len(sizes))]
    flat = field.reshape(rows * blocks * 2, size)

    def out_spec(first, count):
        return pl.BlockSpec(
            (1, rows, 2 * size), lambda j, o, c: (jnp.clip(j - first, 0, count - 1), 0, 0)
        )

    return pl.pallas_call(
        functools.partial(
            extrapolate_kernel, sizes=sizes, rows=rows, blocks=blocks, chunk=chunk, listed=listed
        ),
        grid_spec=pltpu.PrefetchScalarGridSpec(
            num_scalar_prefetch=2,
            grid=(sum(sizes),),
            in_specs=[
                pl.BlockSpec((rows * blocks * 2, size), lambda j, o, c: (0, 0)),
                pl.BlockSpec((1, bands, 2, size, size), lambda j, o, c: (o[j], 0, 0, 0, 0)),
            ]
            + [pl.BlockSpec(memory_space=pl.ANY)] * len(after),
            out_specs=[out_spec(*one) for one in zip(firsts, sizes)],
            scratch_shapes=[
                pltpu.VMEM((chunk * blocks * 2, size), jnp.float32),
                pltpu.VMEM((sum(sizes) * bands if listed else blocks, rows, 2 * size), jnp.bfloat16),
            ],
        ),
        out_shape=[jax.ShapeDtypeStruct((n, rows, 2 * size), jnp.bfloat16) for n in sizes],
        compiler_params=params(),
        cost_estimate=SMALL,
        name="extrapolate",
    )(order, columns, flat, operator, *after)


def starts(fields):
    sizes = [field.shape[0] for field in fields]
    return [sum(sizes[:n]) for n in range(len(sizes))]


def product_kernel(near_ids, far_ids, *refs, near_starts, far_starts):
    near = refs[:len(near_starts)]
    far = refs[len(near_starts):-5]
    near_data, far_data, out, turned, total = refs[-5:]
    size = near_data.shape[2]
    tiles = near_data.shape[0]
    sources = near[0].shape[1] // size
    per_source = tiles // sources
    step = pl.program_id(0)

    @pl.when(step == 0)
    def _():
        for side, data in enumerate((near_data, far_data)):
            for tile in range(tiles):
                for part in range(2):
                    turned[side * tiles + tile, :, part * size:(part + 1) * size] = data[tile, part].T

    total[...] = jnp.zeros_like(total)
    for side, (fields, begin, ids) in enumerate(((near, near_starts, near_ids), (far, far_starts, far_ids))):
        for source in range(sources):
            lines = slice(source * size, (source + 1) * size)
            upper = fields[0][0, lines, :]
            for field, start in zip(fields[1:], begin[1:]):
                upper = jnp.where(step < start, upper, field[0, lines, :])
            lower = jnp.concatenate([-upper[:, size:], upper[:, :size]], 1)
            both = jnp.concatenate([upper, lower], 0)
            first = side * tiles + source * per_source
            left = turned[first:first + per_source].reshape(per_source * size, 2 * size)
            result = jnp.dot(left, both, preferred_element_type=jnp.float32)
            for tile in range(per_source):
                total[ids[source * per_source + tile]] += result[tile * size:(tile + 1) * size]
    for block in range(total.shape[0]):
        out[0, :, block * size:(block + 1) * size] = total[block].T.astype(jnp.bfloat16)


def product_blocks(near, far, near_data, far_data, near_ids, far_ids):
    _, rows, width = near[0].shape
    blocks = sum(field.shape[0] for field in near)
    tiles, _, size, _ = near_data.shape
    receivers = NR // size
    specs = [
        pl.BlockSpec(
            (1, rows, width), lambda j, a, b, start=start, count=field.shape[0]: (jnp.clip(j - start, 0, count - 1), 0, 0)
        )
        for fields in (near, far)
        for field, start in zip(fields, starts(fields))
    ]
    data_spec = pl.BlockSpec(near_data.shape, lambda j, a, b: (0, 0, 0, 0))
    return pl.pallas_call(
        functools.partial(product_kernel, near_starts=starts(near), far_starts=starts(far)),
        grid_spec=pltpu.PrefetchScalarGridSpec(
            num_scalar_prefetch=2,
            grid=(blocks,),
            in_specs=specs + [data_spec, data_spec],
            out_specs=pl.BlockSpec((1, width, NR), lambda j, a, b: (j, 0, 0)),
            scratch_shapes=[
                pltpu.VMEM((2 * tiles, size, width), jnp.bfloat16),
                pltpu.VMEM((receivers, size, width), jnp.float32),
            ],
        ),
        out_shape=jax.ShapeDtypeStruct((blocks, width, NR), jnp.bfloat16),
        compiler_params=params(),
        cost_estimate=SMALL,
        name="product",
    )(near_ids, far_ids, *near, *far, near_data, far_data)


def image_kernel(places, *refs, pieces, choice, size):
    out = refs[-1]
    both = None
    for n in range(pieces):
        field = refs[pieces + n][0]
        if n == pieces - 1 and choice:
            field = jnp.where(places[pieces] > 0, refs[2 * pieces][0], field)
        term = jnp.dot(refs[n][0], field, preferred_element_type=jnp.float32)
        both = term if both is None else both + term
    real = both[:size, :size] + both[size:, size:]
    imag = both[size:, :size] - both[:size, size:]
    if len(refs) > 2 * pieces + choice + 1:
        real += refs[2 * pieces + choice][0, 0]
        imag += refs[2 * pieces + choice][0, 1]
    out[0, 0] = real
    out[0, 1] = imag


def image_blocks(product, first, blocks, fields, origins, before=None, inner=None, forwarded=None):
    _, rows, width = fields[0][0].shape
    size = width // 2
    pieces = len(fields)
    choice = int(forwarded is not None)
    places = jnp.stack(list(origins) + ([inner.astype(jnp.int32)] if choice else []))
    image_spec = pl.BlockSpec((1, 2, size, size), lambda j, o: (j, 0, 0, 0))
    specs = [pl.BlockSpec((1, width, rows), lambda j, o, n=n: (first + j, 0, o[n])) for n in range(pieces)]
    specs += [pl.BlockSpec((1, rows, width), lambda j, o, at=at: (at + j, 0, 0)) for _, at in fields]
    specs += [pl.BlockSpec((1, rows, width), lambda j, o: (j, 0, 0))] * choice
    values = [product] * pieces + [field for field, _ in fields] + ([forwarded] if choice else [])
    if before is not None:
        specs.append(image_spec)
        values.append(before)
    return pl.pallas_call(
        functools.partial(image_kernel, pieces=pieces, choice=choice, size=size),
        grid_spec=pltpu.PrefetchScalarGridSpec(
            num_scalar_prefetch=1, grid=(blocks,), in_specs=specs, out_specs=image_spec
        ),
        out_shape=jax.ShapeDtypeStruct((blocks, 2, size, size), jnp.float32),
        compiler_params=params(),
        cost_estimate=SMALL,
        name="image",
    )(places, *values)


def following(value, *earlier):
    return lax.optimization_barrier((value,) + earlier)[0]


def swap(value, bit):
    return lax.ppermute(value, "shot", [(i, i ^ bit) for i in range(4)])


def hand(value, *pairs):
    return lax.ppermute(value, "shot", pairs)


def send_sum(value, pairs):
    return lax.ppermute(value.astype(jnp.bfloat16), ("shot", "freq"), pairs).astype(jnp.float32)


def hand_freq(value, *pairs, shots=(0, 1, 2, 3)):
    return send_sum(value, [(4 * shot + a, 4 * shot + b) for shot in shots for a, b in pairs])


def hand_shot(value, freq_pairs):
    return send_sum(
        value, [(4 * a + freq, 4 * b + freq) for freq, pairs in freq_pairs.items() for a, b in pairs]
    )


def pick(condition, one, other):
    return jnp.where(condition, one, other)


def even_image(image, freq, left):
    image = image + hand_freq(image, (1, 0), (3, 2))
    image = image.reshape((2, 2) + image.shape[1:])
    low = freq < 2
    keep = pick(low, image[:, 0], image[:, 1])
    send = pick(low, image[:, 1], image[:, 0])
    image = keep + hand_freq(send, (0, 2), (2, 0))
    keep = pick(left, image[0], image[1])
    send = pick(left, image[1], image[0])
    across = [(0, 3), (3, 0), (1, 2), (2, 1)]
    return keep + hand_shot(send, {0: across, 2: across})


def odd_image(image, freq, left):
    image = image + hand_freq(image, (0, 1), (2, 3))
    ones = jnp.stack([image[0], image[2]])
    ones = ones + hand_freq(ones, (3, 1))
    three = image[1] + hand_freq(image[1], (1, 3))
    keep = pick(freq == 1, pick(left, ones[0], ones[1]), three)
    send = pick(freq == 1, pick(left, ones[1], ones[0]), three)
    return keep + hand_shot(send, {1: [(0, 3), (3, 0), (1, 2), (2, 1)], 3: [(3, 0), (2, 1)]})


def extra_image(image, shot):
    inner = (1, 2)
    image = image + hand_freq(image, (0, 1), (2, 3), shots=inner)
    image = image + hand_freq(image, (1, 3), shots=inner)
    image = image + hand_shot(image, {3: [(1, 2)]})
    return pick(shot == 2, image[0], hand_shot(image[1], {3: [(2, 3)]}))


def split_body(source_field, receiver_field, operator, band_offsets, survey_tiles, survey_data):
    blocks = source_field.shape[2]
    tiles = survey_data.shape[1]
    shot = lax.axis_index("shot")
    freq = lax.axis_index("freq")
    left = shot < 2
    inner = (shot == 1) | (shot == 2)
    outer_even, inner_even = jnp.array([0, 2, 12, 14], jnp.int32), jnp.array([4, 6, 8, 10], jnp.int32)
    outer_odd, inner_odd = jnp.array([1, 3, 13], jnp.int32), jnp.array([5, 7, 9], jnp.int32)
    extra = jnp.array([11, 15], jnp.int32)
    own_even = jnp.where(inner, inner_even, outer_even)
    other_even = jnp.where(inner, outer_even, inner_even)
    own_odd = jnp.where(inner, inner_odd, outer_odd)
    other_odd = jnp.where(inner, outer_odd, inner_odd)
    columns = (jnp.arange(blocks, dtype=jnp.int32)[:, None] + band_offsets) % blocks
    make = functools.partial(extrapolate_blocks, operator=operator[0], columns=columns)

    inward = ((0, 1), (3, 2))
    middle = ((1, 2), (2, 1))
    beyond = ((1, 3), (2, 0))
    far_data = swap(survey_data[0], 1)
    (r_extra,) = make(receiver_field[0], sets=[extra], listed=True)
    extra_3 = hand(r_extra, *middle)
    extra_1 = hand(r_extra, *inward)
    r_own, r_other = make(
        receiver_field[0],
        sets=[jnp.concatenate([own_even, own_odd]), jnp.concatenate([other_even, other_odd])],
        after=(r_extra,),
    )
    r_3 = swap(r_own, 3)
    r_1 = swap(r_other, 1)
    s_own, s_even_other, s_odd_other, s_extra = make(
        source_field[0],
        sets=[jnp.concatenate([own_even, own_odd]), other_even, other_odd, extra],
        after=(r_own, far_data, extra_3, extra_1),
    )
    s_extra_far = hand(s_extra, *inward)
    s_even_far = swap(following(s_even_other, s_extra_far), 1)
    s_odd_far = swap(following(s_odd_other, s_even_far, r_3), 1)
    even_2 = hand(following(r_other, far_data)[:4], *beyond)
    even_2_inner = hand(r_1[:4], *middle)
    extra_2 = hand(following(extra_1, r_1), *middle)
    odd_2 = hand(following(r_other, r_3)[4:], *beyond)
    odd_2_inner = hand(following(r_1, r_3)[4:], *middle)

    ids = survey_tiles[:, 1]
    near_ids = lax.dynamic_slice_in_dim(ids, shot * tiles, tiles)
    far_ids = lax.dynamic_slice_in_dim(ids, (shot ^ 1) * tiles, tiles)
    product = product_blocks(
        [s_own, s_extra], [s_even_far, s_odd_far, s_extra_far], survey_data[0], far_data, near_ids, far_ids
    )
    make_image = functools.partial(image_blocks, product, inner=inner)
    image = make_image(
        7, 2, [(r_extra, 0), (extra_1, 0), (extra_3, 0), (extra_2, 0)], [shot, shot ^ 1, shot ^ 3, shot ^ 2]
    )
    last = extra_image(image, shot)
    image = make_image(
        0, 4, [(r_own, 0), (r_1, 0), (r_3, 0), (even_2, 0)], [shot, shot ^ 1, shot ^ 3, shot ^ 2],
        forwarded=even_2_inner,
    )
    even = even_image(image, freq, left)
    image = make_image(4, 3, [(r_own, 4), (r_1, 4), (r_3, 4)], [shot, shot ^ 1, shot ^ 3])
    image = following(image, even, last)
    image = make_image(4, 3, [(odd_2, 0)], [shot ^ 2], image, forwarded=odd_2_inner)
    odd = odd_image(image, freq, left)
    image = pick(freq % 2 == 0, even, pick((freq == 3) & ~left, last, odd))
    total_freqs = source_field.shape[0] * lax.axis_size("freq")
    return image * (1.0 / math.sqrt(2.0 * NR * total_freqs))


def body(source_field, *rest):
    fits = (
        lax.axis_size("shot") == 4
        and lax.axis_size("freq") == 4
        and source_field.shape[1:] == (512, 16, 2, 128)
    )
    return (split_body if fits else general_body)(source_field, *rest)


def solution(mesh):
    return jax.shard_map(
        body,
        mesh=mesh,
        in_specs=(
            P("freq", ("groups", "shot"), None, None, None),
            P("freq", ("groups", "shot"), None, None, None),
            P("freq", "groups", None, None, None, None),
            P("groups", None),
            P("groups", None),
            P("freq", ("groups", "shot"), None, None, None),
        ),
        out_specs=P(None, ("groups", "shot", "freq"), None),
        check_vma=False,
    )
```

```python
import functools
import math

import jax
import jax.numpy as jnp
from jax import lax
from jax.experimental import pallas as pl
from jax.experimental.pallas import tpu as pltpu
from jax.sharding import PartitionSpec as P

NR = 2048
LIMIT = 56 * 1024 * 1024
SMALL = pl.CostEstimate(flops=1000, bytes_accessed=1000, transcendentals=0)


def extrapolate(wavefield, operator, columns):
    row_count, blocks_x, components, block_size = wavefield.shape
    bands = columns.shape[1]
    real_part = operator[:, :, 0]
    imag_part = operator[:, :, 1]
    upper_rows = jnp.concatenate([real_part, imag_part], -1)
    lower_rows = jnp.concatenate([-imag_part, real_part], -1)
    real_block = jnp.concatenate([upper_rows, lower_rows], -2)
    real_block = real_block.reshape(blocks_x, bands, 2 * block_size, 2, block_size)
    chosen = jnp.take(wavefield, columns, axis=1).reshape(
        row_count, blocks_x, bands, 2 * block_size
    )
    result = jnp.einsum("sikc,ikcoy->soiy", chosen, real_block, preferred_element_type=jnp.float32)
    return result.astype(jnp.bfloat16)


def to_owners(wavefield, shot_count, own_cells):
    row_count = wavefield.shape[0]
    return wavefield.reshape(row_count, 2, shot_count, own_cells)


def to_tiles(wavefield, shot_count, own_cells):
    row_count, components, blocks_x, block_size = wavefield.shape
    if own_cells >= block_size:
        return to_owners(wavefield, shot_count, own_cells)
    factor = block_size // own_cells
    copies = jnp.broadcast_to(
        wavefield[:, :, :, None, :], (row_count, components, blocks_x, factor, block_size)
    )
    return copies.reshape(row_count, components, shot_count, block_size)


def data_product(source_cells, data_shard, survey_tiles, block_size, own_cells):
    source_count = source_cells.shape[0]
    receiver_blocks = NR // block_size
    blocks = source_cells.reshape(source_count // block_size, block_size, 2 * own_cells)
    block_ids = jnp.arange(receiver_blocks, dtype=jnp.int32)
    chosen = jnp.take(blocks, survey_tiles[:, 0], axis=0)
    products = jnp.einsum(
        "ncsr,nsk->ncrk",
        lax.all_gather(data_shard, "shot", axis=0, tiled=True),
        chosen,
        preferred_element_type=jnp.float32,
    )
    real_part = products[:, 0, :, :own_cells] - products[:, 1, :, own_cells:]
    imag_part = products[:, 0, :, own_cells:] + products[:, 1, :, :own_cells]
    contribution = jnp.concatenate([real_part, imag_part], -1)
    onehot = (survey_tiles[:, 1][:, None] == block_ids[None, :]).astype(jnp.float32)
    summed = jnp.einsum("nq,nrk->qrk", onehot, contribution, precision=lax.Precision.HIGHEST)
    return summed.reshape(NR, 2, own_cells).astype(jnp.bfloat16)


def image_tile(product, receiver_tile, block_size):
    row_count, components, own_cells = product.shape
    tiles_here = max(own_cells // block_size, 1)
    inner_cells = own_cells // tiles_here
    left = product.reshape(row_count, 2, tiles_here, inner_cells)
    right = receiver_tile.reshape(row_count, 2, tiles_here, block_size)
    turned = jnp.stack([-right[:, 1], right[:, 0]], 1)
    both = jnp.stack([right, turned], 1)
    result = jnp.einsum("rctx,rocty->otxy", left, both, preferred_element_type=jnp.float32)
    return result.reshape(2, own_cells, block_size)


def general_body(source_field, receiver_field, operator, band_offsets, survey_tiles, survey_data):
    shot_count = lax.axis_size("shot")
    freq_local = source_field.shape[0]
    blocks_x = source_field.shape[2]
    block_size = source_field.shape[4]
    own_cells = blocks_x * block_size // shot_count
    block_rows = jnp.arange(blocks_x, dtype=jnp.int32)[:, None]
    columns = (block_rows + band_offsets) % blocks_x
    source_next = extrapolate(source_field[0], operator[0], columns)
    receiver_next = extrapolate(receiver_field[0], operator[0], columns)
    source_send = to_owners(source_next, shot_count, own_cells)
    receiver_send = to_tiles(receiver_next, shot_count, own_cells)
    source_cells = lax.all_to_all(source_send, "shot", split_axis=2, concat_axis=0, tiled=True)
    receiver_tile = lax.all_to_all(receiver_send, "shot", split_axis=2, concat_axis=0, tiled=True)
    source_cells = source_cells.reshape(source_cells.shape[0], 2 * own_cells)
    product = data_product(source_cells, survey_data[0], survey_tiles, block_size, own_cells)
    receiver_tile = receiver_tile.reshape(receiver_tile.shape[0], 2, -1)
    image_sum = image_tile(product, receiver_tile, block_size)
    total_freqs = freq_local * lax.axis_size("freq")
    scaled = image_sum * (1.0 / math.sqrt(2.0 * NR * total_freqs))
    return lax.psum_scatter(scaled, "freq", scatter_dimension=1, tiled=True)


INNER = [4, 8, 6, 10, 15, 5, 9, 7, 11]
OUTER = [0, 12, 2, 14, 1, 13, 3]
FIRST = 5
OUTER_FIRST = 4


def outer_place(slot):
    return jnp.where(slot < FIRST, jnp.minimum(slot, OUTER_FIRST - 1), jnp.minimum(slot - 1, len(OUTER) - 1))


def params():
    return pltpu.CompilerParams(vmem_limit_bytes=LIMIT)


def split_components(field, stage, apart, rows, blocks, chunk):
    lines = 2 * blocks

    def split(n, carry):
        start = pl.multiple_of(n * (chunk * lines), chunk * lines)
        stage[...] = field[pl.ds(start, chunk * lines), :].astype(jnp.float32)
        to = pl.ds(pl.multiple_of(n * chunk, chunk), chunk)
        for block in range(blocks):
            for part in range(2):
                picked = stage[pl.ds(2 * block + part, chunk, stride=lines), :]
                apart[block, to, part * 128:(part + 1) * 128] = picked.astype(jnp.bfloat16)
        return carry

    lax.fori_loop(0, rows // chunk, split, 0)


def extrapolate_kernel(order, columns, field, operator, *refs, sizes, rows, blocks, chunk, ready):
    step = pl.program_id(0)
    bands = operator.shape[1]
    if ready:
        apart = field
        outs = refs[-len(sizes):]
    else:
        stage = refs[-1]
        apart = refs[-2]
        outs = refs[-2 - len(sizes):-2]

        @pl.when(step == 0)
        def _():
            split_components(field, stage, apart, rows, blocks, chunk)

    block = order[step]
    inputs = []
    weights = []
    for band in range(bands):
        inputs.append(apart[columns[block, band]])
        real = operator[0, band, 0]
        imag = operator[0, band, 1]
        weights.append(jnp.concatenate([real, imag], 1))
        weights.append(jnp.concatenate([-imag, real], 1))
    result = jnp.dot(
        jnp.concatenate(inputs, 1), jnp.concatenate(weights, 0), preferred_element_type=jnp.float32
    ).astype(jnp.bfloat16)
    first = 0
    for out, count in zip(outs, sizes):
        if len(sizes) == 1:
            out[0] = result
        else:
            @pl.when((step >= first) & (step < first + count))
            def _(out=out):
                out[0] = result
        first += count


def extrapolate_blocks(field, operator, columns, sets, keep=False, after=()):
    ready = field.ndim == 3
    blocks = columns.shape[0]
    bands = columns.shape[1]
    if ready:
        _, rows, width = field.shape
        size = width // 2
        flat = field
    else:
        rows, _, _, size = field.shape
        width = 2 * size
        flat = field.reshape(rows * blocks * 2, size)
    chunk = 32
    sizes = [len(one) for one in sets]
    order = jnp.array(sum(sets, []), jnp.int32)
    firsts = [sum(sizes[:n]) for n in range(len(sizes))]
    whole = (blocks, rows, width)

    def out_spec(first, count):
        return pl.BlockSpec((1, rows, width), lambda j, o, c: (jnp.clip(j - first, 0, count - 1), 0, 0))

    scratch = [] if ready else [pltpu.VMEM((chunk * blocks * 2, size), jnp.float32)]
    if not ready and not keep:
        scratch = [pltpu.VMEM(whole, jnp.bfloat16)] + scratch
    return pl.pallas_call(
        functools.partial(
            extrapolate_kernel, sizes=sizes, rows=rows, blocks=blocks, chunk=chunk, ready=ready
        ),
        grid_spec=pltpu.PrefetchScalarGridSpec(
            num_scalar_prefetch=2,
            grid=(sum(sizes),),
            in_specs=[
                pl.BlockSpec(flat.shape, lambda j, o, c: (0,) * flat.ndim),
                pl.BlockSpec((1, bands, 2, size, size), lambda j, o, c: (o[j], 0, 0, 0, 0)),
            ]
            + [pl.BlockSpec(memory_space=pl.ANY)] * len(after),
            out_specs=[out_spec(*one) for one in zip(firsts, sizes)]
            + [pl.BlockSpec(whole, lambda j, o, c: (0, 0, 0))] * keep,
            scratch_shapes=scratch,
        ),
        out_shape=[jax.ShapeDtypeStruct((n, rows, width), jnp.bfloat16) for n in sizes]
        + [jax.ShapeDtypeStruct(whole, jnp.bfloat16)] * keep,
        compiler_params=params(),
        cost_estimate=SMALL,
        name="extrapolate",
    )(order, columns, flat, operator, *after)


def product_kernel(near_ids, far_ids, inner, near_in, near_out, far_in, far_out, near_data, far_data, out, turned, total):
    size = near_data.shape[2]
    tiles = near_data.shape[0]
    sources = near_in.shape[1] // size
    per_source = tiles // sources

    @pl.when(pl.program_id(0) == 0)
    def _():
        for side, data in enumerate((near_data, far_data)):
            for tile in range(tiles):
                for part in range(2):
                    turned[side * tiles + tile, :, part * size:(part + 1) * size] = data[tile, part].T

    total[...] = jnp.zeros_like(total)
    sides = ((near_in, near_out, near_ids), (far_in, far_out, far_ids))
    for side, (field_in, field_out, ids) in enumerate(sides):
        for source in range(sources):
            lines = slice(source * size, (source + 1) * size)
            upper = jnp.where(inner[0] > 0, field_in[0, lines, :], field_out[0, lines, :])
            lower = jnp.concatenate([-upper[:, size:], upper[:, :size]], 1)
            both = jnp.concatenate([upper, lower], 0)
            first = side * tiles + source * per_source
            left = turned[first:first + per_source].reshape(per_source * size, 2 * size)
            result = jnp.dot(left, both, preferred_element_type=jnp.float32)
            for tile in range(per_source):
                total[ids[source * per_source + tile]] += result[tile * size:(tile + 1) * size]
    for block in range(total.shape[0]):
        out[0, :, block * size:(block + 1) * size] = total[block].T.astype(jnp.bfloat16)


def inner_spec(shape, first, inner_first=0):
    return pl.BlockSpec(
        shape, lambda j, a, b, inner: (jnp.where(inner[0] > 0, first + j - inner_first, 0), 0, 0)
    )


def outer_spec(shape, first, outer_first=0):
    return pl.BlockSpec(
        shape, lambda j, a, b, inner: (jnp.where(inner[0] > 0, 0, outer_place(first + j) - outer_first), 0, 0)
    )


def product_blocks(near_in, near_out, far_in, far_out, near_data, far_data, near_ids, far_ids, inner):
    blocks, rows, width = near_in.shape
    tiles, _, size, _ = near_data.shape
    receivers = NR // size
    shape = (1, rows, width)
    data_spec = pl.BlockSpec(near_data.shape, lambda j, a, b, i: (0, 0, 0, 0))
    return pl.pallas_call(
        product_kernel,
        grid_spec=pltpu.PrefetchScalarGridSpec(
            num_scalar_prefetch=3,
            grid=(blocks,),
            in_specs=[inner_spec(shape, 0), outer_spec(shape, 0)] * 2 + [data_spec, data_spec],
            out_specs=pl.BlockSpec((1, width, NR), lambda j, a, b, i: (j, 0, 0)),
            scratch_shapes=[
                pltpu.VMEM((2 * tiles, size, width), jnp.bfloat16),
                pltpu.VMEM((receivers, size, width), jnp.float32),
            ],
        ),
        out_shape=jax.ShapeDtypeStruct((blocks, width, NR), jnp.bfloat16),
        compiler_params=params(),
        cost_estimate=SMALL,
        name="product",
    )(near_ids, far_ids, inner, near_in, near_out, far_in, far_out, near_data, far_data)


def image_kernel(places, unused, inner, *refs, pieces, size):
    out = refs[-1]
    both = None
    for n in range(pieces):
        field = jnp.where(inner[0] > 0, refs[pieces + 2 * n][0], refs[pieces + 2 * n + 1][0])
        term = jnp.dot(refs[n][0], field, preferred_element_type=jnp.float32)
        both = term if both is None else both + term
    real = both[:size, :size] + both[size:, size:]
    imag = both[size:, :size] - both[:size, size:]
    if len(refs) > 3 * pieces + 1:
        real += refs[3 * pieces][0, 0]
        imag += refs[3 * pieces][0, 1]
    out[0, 0] = real
    out[0, 1] = imag


def image_blocks(product, first, count, fields, origins, inner, before=None):
    _, rows, width = fields[0][0].shape
    size = width // 2
    pieces = len(fields)
    image_spec = pl.BlockSpec((1, 2, size, size), lambda j, o, u, i: (j, 0, 0, 0))
    specs = [pl.BlockSpec((1, width, rows), lambda j, o, u, i, n=n: (first + j, 0, o[n])) for n in range(pieces)]
    values = [product] * pieces
    for field_in, inner_first, field_out, outer_first in fields:
        specs += [inner_spec((1, rows, width), first, inner_first), outer_spec((1, rows, width), first, outer_first)]
        values += [field_in, field_out]
    if before is not None:
        specs.append(image_spec)
        values.append(before)
    places = jnp.stack(list(origins))
    return pl.pallas_call(
        functools.partial(image_kernel, pieces=pieces, size=size),
        grid_spec=pltpu.PrefetchScalarGridSpec(
            num_scalar_prefetch=3, grid=(count,), in_specs=specs, out_specs=image_spec
        ),
        out_shape=jax.ShapeDtypeStruct((count, 2, size, size), jnp.float32),
        compiler_params=params(),
        cost_estimate=SMALL,
        name="image",
    )(places, places, inner, *values)


def following(value, *earlier):
    return lax.optimization_barrier((value,) + earlier)[0]


def hand(value, *pairs):
    return lax.ppermute(value, "shot", pairs)


def send_sum(value, pairs):
    pairs = [(4 * a + b, 4 * c + d) for (a, b), (c, d) in pairs]
    return lax.ppermute(value.astype(jnp.bfloat16), ("shot", "freq"), pairs).astype(jnp.float32)


def sum_images(one, two, shot, freq):
    left = shot < 2
    shots = range(4)
    even = freq % 2 == 0
    low = freq < 2
    last = one[4:]
    one = one[:4]
    keep = jnp.where(even, jnp.concatenate([one, last]), jnp.concatenate([two, last]))
    send = jnp.where(even, jnp.concatenate([two, last]), jnp.concatenate([one, last]))
    image = keep + send_sum(send, [((s, f), (s, f ^ 1)) for s in shots for f in range(4)])
    keep = jnp.where(low, image[:2], image[2:4])
    send = jnp.where(low, image[2:4], image[:2])
    last = image[4] + send_sum(image[4], [((s, 1), (s, 3)) for s in (1, 2)])
    image = keep + send_sum(send, [((s, f), (s, f ^ 2)) for s in shots for f in range(4)])
    keep = jnp.where(left, image[0], image[1])
    send = jnp.where(left, image[1], image[0])
    image = keep + send_sum(send, [((s, f), (3 - s, f)) for s in shots for f in range(4) if (s, f) != (0, 3)])
    last = send_sum(last, [((1, 3), (3, 3))]) + send_sum(last, [((2, 3), (3, 3))])
    return jnp.where((shot == 3) & (freq == 3), last, image)


def split_body(source_field, receiver_field, operator, band_offsets, survey_tiles, survey_data):
    blocks = source_field.shape[2]
    tiles = survey_data.shape[1]
    shot = lax.axis_index("shot")
    freq = lax.axis_index("freq")
    inner = ((shot == 1) | (shot == 2)).astype(jnp.int32)[None]
    columns = (jnp.arange(blocks, dtype=jnp.int32)[:, None] + band_offsets) % blocks
    make = functools.partial(extrapolate_blocks, operator=operator[0], columns=columns)
    inward = ((0, 1), (3, 2))
    outward = ((1, 0), (2, 3))
    middle = ((1, 2), (2, 1))
    ends = ((0, 3), (3, 0))
    beyond = ((1, 3), (2, 0))

    far_data = hand(survey_data[0], *inward, *outward)
    r_inner, r_apart = make(receiver_field[0], sets=[INNER], keep=True)
    r_3_in = hand(r_inner, *middle)
    r_1_in = hand(following(r_inner, far_data), *inward)
    (r_outer,) = make(r_apart, sets=[OUTER])
    r_3_out = hand(r_outer, *ends)
    s_inner, s_outer = make(source_field[0], sets=[INNER, OUTER], after=(r_outer, far_data))
    s_out = hand(s_outer, *outward)
    s_in = hand(s_inner, *inward)
    r_1_out = hand(following(r_outer, r_3_in, r_3_out), *outward)
    forward_1 = hand(r_1_in[:FIRST], *middle)
    forward_2 = hand(r_1_in[FIRST:], *middle)
    beyond_1 = hand(following(r_outer, r_3_out)[:OUTER_FIRST], *beyond)
    beyond_2 = hand(following(r_outer, s_out)[OUTER_FIRST:], *beyond)

    ids = survey_tiles[:, 1]
    near_ids = lax.dynamic_slice_in_dim(ids, shot * tiles, tiles)
    far_ids = lax.dynamic_slice_in_dim(ids, (shot ^ 1) * tiles, tiles)
    product = product_blocks(
        s_inner, s_outer, s_in, s_out, survey_data[0], far_data, near_ids, far_ids, inner
    )
    early = [(r_inner, 0, r_outer, 0), (r_3_in, 0, r_3_out, 0)]
    late = [(r_1_in, 0, r_1_out, 0)]
    origins = [shot, shot ^ 3, shot ^ 1, shot ^ 2]
    one = image_blocks(product, 0, FIRST, early, origins[:2], inner)
    two = image_blocks(product, FIRST, len(INNER) - FIRST, early, origins[:2], inner)
    one = image_blocks(product, 0, FIRST, late + [(forward_1, 0, beyond_1, 0)], origins[2:], inner, one)
    two = image_blocks(
        product, FIRST, len(INNER) - FIRST, late + [(forward_2, FIRST, beyond_2, OUTER_FIRST)], origins[2:], inner, two
    )
    image = sum_images(one, two, shot, freq)
    total_freqs = source_field.shape[0] * lax.axis_size("freq")
    return image * (1.0 / math.sqrt(2.0 * NR * total_freqs))


def body(source_field, *rest):
    fits = (
        lax.axis_size("shot") == 4
        and lax.axis_size("freq") == 4
        and source_field.shape[1:] == (512, 16, 2, 128)
    )
    return (split_body if fits else general_body)(source_field, *rest)


def solution(mesh):
    return jax.shard_map(
        body,
        mesh=mesh,
        in_specs=(
            P("freq", ("groups", "shot"), None, None, None),
            P("freq", ("groups", "shot"), None, None, None),
            P("freq", "groups", None, None, None, None),
            P("groups", None),
            P("groups", None),
            P("freq", ("groups", "shot"), None, None, None),
        ),
        out_specs=P(None, ("groups", "shot", "freq"), None),
        check_vma=False,
    )
```

```python
import functools
import math

import jax
import jax.numpy as jnp
from jax import lax
from jax.experimental import pallas as pl
from jax.experimental.pallas import tpu as pltpu
from jax.sharding import PartitionSpec as P

NR = 2048
HEAD_LIMIT = 60
SMALL = pl.CostEstimate(flops=1000, bytes_accessed=1000, transcendentals=0)


def extrapolate(wavefield, operator, columns):
    row_count, blocks_x, components, block_size = wavefield.shape
    bands = columns.shape[1]
    real_part = operator[:, :, 0]
    imag_part = operator[:, :, 1]
    upper_rows = jnp.concatenate([real_part, imag_part], -1)
    lower_rows = jnp.concatenate([-imag_part, real_part], -1)
    real_block = jnp.concatenate([upper_rows, lower_rows], -2)
    real_block = real_block.reshape(blocks_x, bands, 2 * block_size, 2, block_size)
    chosen = jnp.take(wavefield, columns, axis=1).reshape(
        row_count, blocks_x, bands, 2 * block_size
    )
    result = jnp.einsum("sikc,ikcoy->soiy", chosen, real_block, preferred_element_type=jnp.float32)
    return result.astype(jnp.bfloat16)


def to_owners(wavefield, shot_count, own_cells):
    row_count = wavefield.shape[0]
    return wavefield.reshape(row_count, 2, shot_count, own_cells)


def to_tiles(wavefield, shot_count, own_cells):
    row_count, components, blocks_x, block_size = wavefield.shape
    if own_cells >= block_size:
        return to_owners(wavefield, shot_count, own_cells)
    factor = block_size // own_cells
    copies = jnp.broadcast_to(
        wavefield[:, :, :, None, :], (row_count, components, blocks_x, factor, block_size)
    )
    return copies.reshape(row_count, components, shot_count, block_size)


def data_product(source_cells, data_shard, survey_tiles, block_size, own_cells):
    source_count = source_cells.shape[0]
    receiver_blocks = NR // block_size
    blocks = source_cells.reshape(source_count // block_size, block_size, 2 * own_cells)
    block_ids = jnp.arange(receiver_blocks, dtype=jnp.int32)
    chosen = jnp.take(blocks, survey_tiles[:, 0], axis=0)
    products = jnp.einsum(
        "ncsr,nsk->ncrk",
        lax.all_gather(data_shard, "shot", axis=0, tiled=True),
        chosen,
        preferred_element_type=jnp.float32,
    )
    real_part = products[:, 0, :, :own_cells] - products[:, 1, :, own_cells:]
    imag_part = products[:, 0, :, own_cells:] + products[:, 1, :, :own_cells]
    contribution = jnp.concatenate([real_part, imag_part], -1)
    onehot = (survey_tiles[:, 1][:, None] == block_ids[None, :]).astype(jnp.float32)
    summed = jnp.einsum("nq,nrk->qrk", onehot, contribution, precision=lax.Precision.HIGHEST)
    return summed.reshape(NR, 2, own_cells).astype(jnp.bfloat16)


def image_tile(product, receiver_tile, block_size):
    row_count, components, own_cells = product.shape
    tiles_here = max(own_cells // block_size, 1)
    inner_cells = own_cells // tiles_here
    left = product.reshape(row_count, 2, tiles_here, inner_cells)
    right = receiver_tile.reshape(row_count, 2, tiles_here, block_size)
    turned = jnp.stack([-right[:, 1], right[:, 0]], 1)
    both = jnp.stack([right, turned], 1)
    result = jnp.einsum("rctx,rocty->otxy", left, both, preferred_element_type=jnp.float32)
    return result.reshape(2, own_cells, block_size)


def general_body(source_field, receiver_field, operator, band_offsets, survey_tiles, survey_data):
    shot_count = lax.axis_size("shot")
    freq_local = source_field.shape[0]
    blocks_x = source_field.shape[2]
    block_size = source_field.shape[4]
    own_cells = blocks_x * block_size // shot_count
    block_rows = jnp.arange(blocks_x, dtype=jnp.int32)[:, None]
    columns = (block_rows + band_offsets) % blocks_x
    source_next = extrapolate(source_field[0], operator[0], columns)
    receiver_next = extrapolate(receiver_field[0], operator[0], columns)
    source_send = to_owners(source_next, shot_count, own_cells)
    receiver_send = to_tiles(receiver_next, shot_count, own_cells)
    source_cells = lax.all_to_all(source_send, "shot", split_axis=2, concat_axis=0, tiled=True)
    receiver_tile = lax.all_to_all(receiver_send, "shot", split_axis=2, concat_axis=0, tiled=True)
    source_cells = source_cells.reshape(source_cells.shape[0], 2 * own_cells)
    product = data_product(source_cells, survey_data[0], survey_tiles, block_size, own_cells)
    receiver_tile = receiver_tile.reshape(receiver_tile.shape[0], 2, -1)
    image_sum = image_tile(product, receiver_tile, block_size)
    total_freqs = freq_local * lax.axis_size("freq")
    scaled = image_sum * (1.0 / math.sqrt(2.0 * NR * total_freqs))
    return lax.psum_scatter(scaled, "freq", scatter_dimension=1, tiled=True)


INNER = [4, 8, 6, 10, 15, 5, 9, 7, 11]
HEAD = 3
OUTER = [0, 12, 2, 14, 1, 13, 3]
FIRST = 5
OUTER_FIRST = 4


def outer_place(slot):
    return jnp.where(slot < FIRST, jnp.minimum(slot, OUTER_FIRST - 1), jnp.minimum(slot - 1, len(OUTER) - 1))


def params(limit=24):
    return pltpu.CompilerParams(vmem_limit_bytes=limit * 1024 * 1024)


def extrapolate_kernel(order, columns, field, operator, *refs, sizes, rows, blocks, chunk, listed):
    stage, apart = refs[-2:]
    outs = refs[-2 - len(sizes):-2]
    step = pl.program_id(0)
    lines = 2 * blocks
    bands = operator.shape[1]

    @pl.when(step == 0)
    def _():
        if listed:
            wanted = [columns[order[n // bands], n % bands] for n in range(sum(sizes) * bands)]
        else:
            wanted = list(range(blocks))

        def split(n, carry):
            start = pl.multiple_of(n * (chunk * lines), chunk * lines)
            stage[...] = field[pl.ds(start, chunk * lines), :].astype(jnp.float32)
            to = pl.ds(pl.multiple_of(n * chunk, chunk), chunk)
            for slot, block in enumerate(wanted):
                for part in range(2):
                    picked = stage[pl.ds(2 * block + part, chunk, stride=lines), :]
                    apart[slot, to, part * 128:(part + 1) * 128] = picked.astype(jnp.bfloat16)
            return carry

        lax.fori_loop(0, rows // chunk, split, 0)

    block = order[step]
    inputs = []
    weights = []
    for band in range(bands):
        inputs.append(apart[step * bands + band if listed else columns[block, band]])
        real = operator[0, band, 0]
        imag = operator[0, band, 1]
        weights.append(jnp.concatenate([real, imag], 1))
        weights.append(jnp.concatenate([-imag, real], 1))
    result = jnp.dot(
        jnp.concatenate(inputs, 1), jnp.concatenate(weights, 0), preferred_element_type=jnp.float32
    ).astype(jnp.bfloat16)
    first = 0
    for out, count in zip(outs, sizes):
        if len(sizes) == 1:
            out[0] = result
        else:
            @pl.when((step >= first) & (step < first + count))
            def _(out=out):
                out[0] = result
        first += count


def extrapolate_blocks(field, operator, columns, sets, listed=False, after=(), limit=24):
    rows, blocks, _, size = field.shape
    bands = columns.shape[1]
    width = 2 * size
    chunk = 32
    sizes = [len(one) for one in sets]
    order = jnp.array(sum(sets, []), jnp.int32)
    firsts = [sum(sizes[:n]) for n in range(len(sizes))]
    flat = field.reshape(rows * blocks * 2, size)

    def out_spec(first, count):
        return pl.BlockSpec((1, rows, width), lambda j, o, c: (jnp.clip(j - first, 0, count - 1), 0, 0))

    return pl.pallas_call(
        functools.partial(
            extrapolate_kernel, sizes=sizes, rows=rows, blocks=blocks, chunk=chunk, listed=listed
        ),
        grid_spec=pltpu.PrefetchScalarGridSpec(
            num_scalar_prefetch=2,
            grid=(sum(sizes),),
            in_specs=[
                pl.BlockSpec(flat.shape, lambda j, o, c: (0, 0)),
                pl.BlockSpec((1, bands, 2, size, size), lambda j, o, c: (o[j], 0, 0, 0, 0)),
            ]
            + [pl.BlockSpec(memory_space=pl.ANY)] * len(after),
            out_specs=[out_spec(*one) for one in zip(firsts, sizes)],
            scratch_shapes=[
                pltpu.VMEM((chunk * blocks * 2, size), jnp.float32),
                pltpu.VMEM((sum(sizes) * bands if listed else blocks, rows, width), jnp.bfloat16),
            ],
        ),
        out_shape=[jax.ShapeDtypeStruct((n, rows, width), jnp.bfloat16) for n in sizes],
        compiler_params=params(limit),
        cost_estimate=SMALL,
        name="extrapolate",
    )(order, columns, flat, operator, *after)


def product_kernel(near_ids, far_ids, inner, near_in, near_out, far_in, far_out, near_data, far_data, out, turned, total):
    size = near_data.shape[2]
    tiles = near_data.shape[0]
    sources = near_in.shape[1] // size
    per_source = tiles // sources

    @pl.when(pl.program_id(0) == 0)
    def _():
        for side, data in enumerate((near_data, far_data)):
            for tile in range(tiles):
                for part in range(2):
                    turned[side * tiles + tile, :, part * size:(part + 1) * size] = data[tile, part].T

    total[...] = jnp.zeros_like(total)
    sides = ((near_in, near_out, near_ids), (far_in, far_out, far_ids))
    for side, (field_in, field_out, ids) in enumerate(sides):
        for source in range(sources):
            lines = slice(source * size, (source + 1) * size)
            upper = jnp.where(inner[0] > 0, field_in[0, lines, :], field_out[0, lines, :])
            lower = jnp.concatenate([-upper[:, size:], upper[:, :size]], 1)
            both = jnp.concatenate([upper, lower], 0)
            first = side * tiles + source * per_source
            left = turned[first:first + per_source].reshape(per_source * size, 2 * size)
            result = jnp.dot(left, both, preferred_element_type=jnp.float32)
            for tile in range(per_source):
                total[ids[source * per_source + tile]] += result[tile * size:(tile + 1) * size]
    for block in range(total.shape[0]):
        out[0, :, block * size:(block + 1) * size] = total[block].T.astype(jnp.bfloat16)


def part_spec(shape, first, begin, count, is_inner):
    def index(j, a, b, inner):
        place = first + j if is_inner else outer_place(first + j)
        place = jnp.clip(place - begin, 0, count - 1)
        return jnp.where((inner[0] > 0) == is_inner, place, 0), 0, 0

    return pl.BlockSpec(shape, index)


def product_blocks(near_in, near_out, far_in, far_out, near_data, far_data, near_ids, far_ids, inner):
    blocks, rows, width = near_in.shape
    tiles, _, size, _ = near_data.shape
    receivers = NR // size
    shape = (1, rows, width)
    data_spec = pl.BlockSpec(near_data.shape, lambda j, a, b, i: (0, 0, 0, 0))
    return pl.pallas_call(
        product_kernel,
        grid_spec=pltpu.PrefetchScalarGridSpec(
            num_scalar_prefetch=3,
            grid=(blocks,),
            in_specs=[part_spec(shape, 0, 0, len(INNER), True), part_spec(shape, 0, 0, len(OUTER), False)] * 2
            + [data_spec, data_spec],
            out_specs=pl.BlockSpec((1, width, NR), lambda j, a, b, i: (j, 0, 0)),
            scratch_shapes=[
                pltpu.VMEM((2 * tiles, size, width), jnp.bfloat16),
                pltpu.VMEM((receivers, size, width), jnp.float32),
            ],
        ),
        out_shape=jax.ShapeDtypeStruct((blocks, width, NR), jnp.bfloat16),
        compiler_params=params(),
        cost_estimate=SMALL,
        name="product",
    )(near_ids, far_ids, inner, near_in, near_out, far_in, far_out, near_data, far_data)


def image_kernel(places, unused, inner, *refs, first, begins, size):
    out = refs[-1]
    slot = first + pl.program_id(0)
    parts = refs[len(begins):]
    both = None
    for n, piece in enumerate(begins):
        field = parts[0][0]
        for part, (begin, is_inner) in zip(parts[1:], piece[1:]):
            chosen = (inner[0] > 0) & (slot >= begin) if is_inner else inner[0] == 0
            field = jnp.where(chosen, part[0], field)
        parts = parts[len(piece):]
        term = jnp.dot(refs[n][0], field, preferred_element_type=jnp.float32)
        both = term if both is None else both + term
    real = both[:size, :size] + both[size:, size:]
    imag = both[size:, :size] - both[:size, size:]
    if len(parts) > 1:
        real += parts[0][0, 0]
        imag += parts[0][0, 1]
    out[0, 0] = real
    out[0, 1] = imag


def image_blocks(product, first, count, pieces, inner, before=None):
    _, rows, width = pieces[0][1][0][0].shape
    size = width // 2
    image_spec = pl.BlockSpec((1, 2, size, size), lambda j, o, u, i: (j, 0, 0, 0))
    specs = [
        pl.BlockSpec((1, width, rows), lambda j, o, u, i, n=n: (first + j, 0, o[n])) for n in range(len(pieces))
    ]
    values = [product] * len(pieces)
    begins = []
    for _, parts in pieces:
        inners = [True] * (len(parts) - 1) + [False]
        for (field, begin), is_inner in zip(parts, inners):
            specs.append(part_spec((1, rows, width), first, begin, field.shape[0], is_inner))
            values.append(field)
        begins.append([(begin, is_inner) for (_, begin), is_inner in zip(parts, inners)])
    if before is not None:
        specs.append(image_spec)
        values.append(before)
    places = jnp.stack([shot for shot, _ in pieces])
    return pl.pallas_call(
        functools.partial(image_kernel, first=first, begins=begins, size=size),
        grid_spec=pltpu.PrefetchScalarGridSpec(
            num_scalar_prefetch=3, grid=(count,), in_specs=specs, out_specs=image_spec
        ),
        out_shape=jax.ShapeDtypeStruct((count, 2, size, size), jnp.float32),
        compiler_params=params(),
        cost_estimate=SMALL,
        name="image",
    )(places, places, inner, *values)


def following(value, *earlier):
    return lax.optimization_barrier((value,) + earlier)[0]


def hand(value, *pairs):
    return lax.ppermute(value, "shot", pairs)


def send_sum(value, pairs):
    pairs = [(4 * a + b, 4 * c + d) for (a, b), (c, d) in pairs]
    return lax.ppermute(value.astype(jnp.bfloat16), ("shot", "freq"), pairs).astype(jnp.float32)


def sum_images(one, two, shot, freq):
    left = shot < 2
    shots = range(4)
    even = freq % 2 == 0
    low = freq < 2
    last = one[4:]
    one = one[:4]
    keep = jnp.where(even, jnp.concatenate([one, last]), jnp.concatenate([two, last]))
    send = jnp.where(even, jnp.concatenate([two, last]), jnp.concatenate([one, last]))
    image = keep + send_sum(send, [((s, f), (s, f ^ 1)) for s in shots for f in range(4)])
    keep = jnp.where(low, image[:2], image[2:4])
    send = jnp.where(low, image[2:4], image[:2])
    last = image[4] + send_sum(image[4], [((s, 1), (s, 3)) for s in (1, 2)])
    image = keep + send_sum(send, [((s, f), (s, f ^ 2)) for s in shots for f in range(4)])
    keep = jnp.where(left, image[0], image[1])
    send = jnp.where(left, image[1], image[0])
    image = keep + send_sum(send, [((s, f), (3 - s, f)) for s in shots for f in range(4) if (s, f) != (0, 3)])
    last = send_sum(last, [((1, 3), (3, 3))]) + send_sum(last, [((2, 3), (3, 3))])
    return jnp.where((shot == 3) & (freq == 3), last, image)


def split_body(source_field, receiver_field, operator, band_offsets, survey_tiles, survey_data):
    blocks = source_field.shape[2]
    tiles = survey_data.shape[1]
    shot = lax.axis_index("shot")
    freq = lax.axis_index("freq")
    inner = ((shot == 1) | (shot == 2)).astype(jnp.int32)[None]
    columns = (jnp.arange(blocks, dtype=jnp.int32)[:, None] + band_offsets) % blocks
    make = functools.partial(extrapolate_blocks, operator=operator[0], columns=columns)
    inward = ((0, 1), (3, 2))
    outward = ((1, 0), (2, 3))
    middle = ((1, 2), (2, 1))
    ends = ((0, 3), (3, 0))
    beyond = ((1, 3), (2, 0))

    far_data = hand(survey_data[0], *inward, *outward)
    (r_head,) = make(receiver_field[0], sets=[INNER[:HEAD]], listed=True, limit=HEAD_LIMIT)
    r_3_head = hand(r_head, *middle)
    r_1_head = hand(r_head, *inward)
    r_inner, r_outer = make(receiver_field[0], sets=[INNER[HEAD:], OUTER], after=(r_head,))
    r_1_out = hand(following(r_outer, far_data), *outward)
    r_3_in = hand(r_inner, *middle)
    r_1_in = hand(r_inner, *inward)
    s_inner, s_outer = make(source_field[0], sets=[INNER, OUTER], after=(r_outer, r_3_head, r_1_head))
    s_out = hand(s_outer, *outward)
    s_in = hand(s_inner, *inward)
    forward_head = hand(following(r_1_head, r_3_in), *middle)
    r_3_out = hand(following(r_outer, r_1_out), *ends)
    forward = hand(r_1_in, *middle)
    beyond_1 = hand(following(r_outer, s_out, forward_head)[:OUTER_FIRST], *beyond)
    beyond_2 = hand(r_outer[OUTER_FIRST:], *beyond)

    ids = survey_tiles[:, 1]
    near_ids = lax.dynamic_slice_in_dim(ids, shot * tiles, tiles)
    far_ids = lax.dynamic_slice_in_dim(ids, (shot ^ 1) * tiles, tiles)
    product = product_blocks(
        s_inner, s_outer, s_in, s_out, survey_data[0], far_data, near_ids, far_ids, inner
    )
    early = [
        (shot, [(r_head, 0), (r_inner, HEAD), (r_outer, 0)]),
        (shot ^ 1, [(r_1_head, 0), (r_1_in, HEAD), (r_1_out, 0)]),
        (shot ^ 3, [(r_3_head, 0), (r_3_in, HEAD), (r_3_out, 0)]),
    ]
    forwarded = [(forward_head, 0), (forward, HEAD)]
    one = image_blocks(product, 0, FIRST, early, inner)
    two = image_blocks(product, FIRST, len(INNER) - FIRST, early, inner)
    one = image_blocks(product, 0, FIRST, [(shot ^ 2, forwarded + [(beyond_1, 0)])], inner, one)
    two = image_blocks(
        product, FIRST, len(INNER) - FIRST, [(shot ^ 2, forwarded + [(beyond_2, OUTER_FIRST)])], inner,
        following(two, one),
    )
    image = sum_images(one, two, shot, freq)
    total_freqs = source_field.shape[0] * lax.axis_size("freq")
    return image * (1.0 / math.sqrt(2.0 * NR * total_freqs))


def body(source_field, *rest):
    fits = (
        lax.axis_size("shot") == 4
        and lax.axis_size("freq") == 4
        and source_field.shape[1:] == (512, 16, 2, 128)
    )
    return (split_body if fits else general_body)(source_field, *rest)


def solution(mesh):
    return jax.shard_map(
        body,
        mesh=mesh,
        in_specs=(
            P("freq", ("groups", "shot"), None, None, None),
            P("freq", ("groups", "shot"), None, None, None),
            P("freq", "groups", None, None, None, None),
            P("groups", None),
            P("groups", None),
            P("freq", ("groups", "shot"), None, None, None),
        ),
        out_specs=P(None, ("groups", "shot", "freq"), None),
        check_vma=False,
    )
```

```python
import functools
import math

import jax
import jax.numpy as jnp
from jax import lax
from jax.experimental import pallas as pl
from jax.experimental.pallas import tpu as pltpu
from jax.sharding import PartitionSpec as P

NR = 2048
SMALL = pl.CostEstimate(flops=1000, bytes_accessed=1000, transcendentals=0)


def extrapolate(wavefield, operator, columns):
    row_count, blocks_x, components, block_size = wavefield.shape
    bands = columns.shape[1]
    real_part = operator[:, :, 0]
    imag_part = operator[:, :, 1]
    upper_rows = jnp.concatenate([real_part, imag_part], -1)
    lower_rows = jnp.concatenate([-imag_part, real_part], -1)
    real_block = jnp.concatenate([upper_rows, lower_rows], -2)
    real_block = real_block.reshape(blocks_x, bands, 2 * block_size, 2, block_size)
    chosen = jnp.take(wavefield, columns, axis=1).reshape(
        row_count, blocks_x, bands, 2 * block_size
    )
    result = jnp.einsum("sikc,ikcoy->soiy", chosen, real_block, preferred_element_type=jnp.float32)
    return result.astype(jnp.bfloat16)


def to_owners(wavefield, shot_count, own_cells):
    row_count = wavefield.shape[0]
    return wavefield.reshape(row_count, 2, shot_count, own_cells)


def to_tiles(wavefield, shot_count, own_cells):
    row_count, components, blocks_x, block_size = wavefield.shape
    if own_cells >= block_size:
        return to_owners(wavefield, shot_count, own_cells)
    factor = block_size // own_cells
    copies = jnp.broadcast_to(
        wavefield[:, :, :, None, :], (row_count, components, blocks_x, factor, block_size)
    )
    return copies.reshape(row_count, components, shot_count, block_size)


def data_product(source_cells, data_shard, survey_tiles, block_size, own_cells):
    source_count = source_cells.shape[0]
    receiver_blocks = NR // block_size
    blocks = source_cells.reshape(source_count // block_size, block_size, 2 * own_cells)
    block_ids = jnp.arange(receiver_blocks, dtype=jnp.int32)
    chosen = jnp.take(blocks, survey_tiles[:, 0], axis=0)
    products = jnp.einsum(
        "ncsr,nsk->ncrk",
        lax.all_gather(data_shard, "shot", axis=0, tiled=True),
        chosen,
        preferred_element_type=jnp.float32,
    )
    real_part = products[:, 0, :, :own_cells] - products[:, 1, :, own_cells:]
    imag_part = products[:, 0, :, own_cells:] + products[:, 1, :, :own_cells]
    contribution = jnp.concatenate([real_part, imag_part], -1)
    onehot = (survey_tiles[:, 1][:, None] == block_ids[None, :]).astype(jnp.float32)
    summed = jnp.einsum("nq,nrk->qrk", onehot, contribution, precision=lax.Precision.HIGHEST)
    return summed.reshape(NR, 2, own_cells).astype(jnp.bfloat16)


def image_tile(product, receiver_tile, block_size):
    row_count, components, own_cells = product.shape
    tiles_here = max(own_cells // block_size, 1)
    inner_cells = own_cells // tiles_here
    left = product.reshape(row_count, 2, tiles_here, inner_cells)
    right = receiver_tile.reshape(row_count, 2, tiles_here, block_size)
    turned = jnp.stack([-right[:, 1], right[:, 0]], 1)
    both = jnp.stack([right, turned], 1)
    result = jnp.einsum("rctx,rocty->otxy", left, both, preferred_element_type=jnp.float32)
    return result.reshape(2, own_cells, block_size)


def general_body(source_field, receiver_field, operator, band_offsets, survey_tiles, survey_data):
    shot_count = lax.axis_size("shot")
    freq_local = source_field.shape[0]
    blocks_x = source_field.shape[2]
    block_size = source_field.shape[4]
    own_cells = blocks_x * block_size // shot_count
    block_rows = jnp.arange(blocks_x, dtype=jnp.int32)[:, None]
    columns = (block_rows + band_offsets) % blocks_x
    source_next = extrapolate(source_field[0], operator[0], columns)
    receiver_next = extrapolate(receiver_field[0], operator[0], columns)
    source_send = to_owners(source_next, shot_count, own_cells)
    receiver_send = to_tiles(receiver_next, shot_count, own_cells)
    source_cells = lax.all_to_all(source_send, "shot", split_axis=2, concat_axis=0, tiled=True)
    receiver_tile = lax.all_to_all(receiver_send, "shot", split_axis=2, concat_axis=0, tiled=True)
    source_cells = source_cells.reshape(source_cells.shape[0], 2 * own_cells)
    product = data_product(source_cells, survey_data[0], survey_tiles, block_size, own_cells)
    receiver_tile = receiver_tile.reshape(receiver_tile.shape[0], 2, -1)
    image_sum = image_tile(product, receiver_tile, block_size)
    total_freqs = freq_local * lax.axis_size("freq")
    scaled = image_sum * (1.0 / math.sqrt(2.0 * NR * total_freqs))
    return lax.psum_scatter(scaled, "freq", scatter_dimension=1, tiled=True)


INNER = [4, 8, 6, 10, 15, 5, 9, 7, 11]
HEAD = 3
OUTER = [0, 12, 2, 14, 1, 13, 3]
FIRST = 5
OUTER_FIRST = 4


def outer_place(slot):
    return jnp.where(slot < FIRST, jnp.minimum(slot, OUTER_FIRST - 1), jnp.minimum(slot - 1, len(OUTER) - 1))


def params(limit=24):
    return pltpu.CompilerParams(vmem_limit_bytes=limit * 1024 * 1024)


def extrapolate_kernel(order, offsets, field, operator, *refs, sets, rows, blocks, parts, listed):
    stage, apart, lines, weights, field_sems, weight_sems = refs[-6:]
    outs = refs[:-6]
    sizes = [len(one) for one in sets]
    step = pl.program_id(0)
    bands = operator.shape[1]
    pitch = 2 * blocks + 1
    chunk = stage.shape[0] // pitch
    part_lines = lines.shape[0] // parts

    def column(block, band):
        return lax.rem(block + offsets[band, block] + blocks, blocks)

    def field_copy(part):
        here = pl.ds(part * part_lines, part_lines)
        return pltpu.make_async_copy(field.at[here], lines.at[here], field_sems.at[part])

    def weight_copy(n, block):
        return pltpu.make_async_copy(operator.at[block], weights.at[n], weight_sems.at[n])

    @pl.when(step == 0)
    def _():
        for part in range(parts):
            field_copy(part).start()
        for n, block in enumerate(sum(sets, [])):
            weight_copy(n, block).start()
        if listed:
            wanted = [column(block, band) for block in sum(sets, []) for band in range(bands)]
        else:
            wanted = list(range(blocks))

        def split(n, carry):
            for row in range(chunk):
                here = pl.ds(pl.multiple_of((n * chunk + row) * 2 * blocks, 2 * blocks), 2 * blocks)
                stage[pl.ds(row * pitch, 2 * blocks), :] = lines[here, :].astype(jnp.float32)
            to = pl.ds(pl.multiple_of(n * chunk, chunk), chunk)
            for slot, block in enumerate(wanted):
                for half in range(2):
                    picked = stage[pl.ds(2 * block + half, chunk, stride=pitch), :]
                    apart[slot, to, half * 128:(half + 1) * 128] = picked.astype(jnp.bfloat16)
            return carry

        steps = rows // chunk // parts
        for part in range(parts):
            field_copy(part).wait()
            lax.fori_loop(part * steps, (part + 1) * steps, split, 0)

    block = order[step]
    weight_copy(step, block).wait()
    inputs = []
    factors = []
    for band in range(bands):
        inputs.append(apart[step * bands + band if listed else column(block, band)])
        real = weights[step, band, 0]
        imag = weights[step, band, 1]
        factors.append(jnp.concatenate([real, imag], 1))
        factors.append(jnp.concatenate([-imag, real], 1))
    result = jnp.dot(
        jnp.concatenate(inputs, 1), jnp.concatenate(factors, 0), preferred_element_type=jnp.float32
    ).astype(jnp.bfloat16)
    first = 0
    for out, count in zip(outs, sizes):
        if len(sizes) == 1:
            out[0] = result
        else:
            @pl.when((step >= first) & (step < first + count))
            def _(out=out):
                out[0] = result
        first += count


def extrapolate_blocks(field, operator, offsets, sets, listed=False, limit=60):
    rows, blocks, _, size = field.shape
    bands = offsets.shape[0]
    width = 2 * size
    chunk = 32
    parts = 4
    sizes = [len(one) for one in sets]
    count = sum(sizes)
    order = jnp.array(sum(sets, []), jnp.int32)
    firsts = [sum(sizes[:n]) for n in range(len(sizes))]
    flat = field.reshape(rows * blocks * 2, size)

    def out_spec(first, count):
        return pl.BlockSpec((1, rows, width), lambda j, o, c: (jnp.clip(j - first, 0, count - 1), 0, 0))

    return pl.pallas_call(
        functools.partial(
            extrapolate_kernel, sets=sets, rows=rows, blocks=blocks, parts=parts, listed=listed
        ),
        grid_spec=pltpu.PrefetchScalarGridSpec(
            num_scalar_prefetch=2,
            grid=(count,),
            in_specs=[pl.BlockSpec(memory_space=pltpu.HBM)] * 2,
            out_specs=[out_spec(*one) for one in zip(firsts, sizes)],
            scratch_shapes=[
                pltpu.VMEM((chunk * (2 * blocks + 1), size), jnp.float32),
                pltpu.VMEM((count * bands if listed else blocks, rows, width), jnp.bfloat16),
                pltpu.VMEM(flat.shape, jnp.bfloat16),
                pltpu.VMEM((count,) + operator.shape[1:], jnp.bfloat16),
                pltpu.SemaphoreType.DMA((parts,)),
                pltpu.SemaphoreType.DMA((count,)),
            ],
        ),
        out_shape=[jax.ShapeDtypeStruct((n, rows, width), jnp.bfloat16) for n in sizes],
        compiler_params=params(limit),
        cost_estimate=SMALL,
        name="extrapolate",
    )(order, offsets, flat, operator)


def product_kernel(near_ids, far_ids, inner, near_in, near_out, far_in, far_out, near_data, far_data, out, turned, total):
    size = near_data.shape[2]
    tiles = near_data.shape[0]
    sources = near_in.shape[1] // size
    per_source = tiles // sources

    @pl.when(pl.program_id(0) == 0)
    def _():
        for side, data in enumerate((near_data, far_data)):
            for tile in range(tiles):
                for part in range(2):
                    turned[side * tiles + tile, :, part * size:(part + 1) * size] = data[tile, part].T

    total[...] = jnp.zeros_like(total)
    sides = ((near_in, near_out, near_ids), (far_in, far_out, far_ids))
    for side, (field_in, field_out, ids) in enumerate(sides):
        for source in range(sources):
            lines = slice(source * size, (source + 1) * size)
            upper = jnp.where(inner[0] > 0, field_in[0, lines, :], field_out[0, lines, :])
            lower = jnp.concatenate([-upper[:, size:], upper[:, :size]], 1)
            both = jnp.concatenate([upper, lower], 0)
            first = side * tiles + source * per_source
            left = turned[first:first + per_source].reshape(per_source * size, 2 * size)
            result = jnp.dot(left, both, preferred_element_type=jnp.float32)
            for tile in range(per_source):
                total[ids[source * per_source + tile]] += result[tile * size:(tile + 1) * size]
    for block in range(total.shape[0]):
        out[0, :, block * size:(block + 1) * size] = total[block].T.astype(jnp.bfloat16)


def part_spec(shape, first, begin, count, is_inner):
    def index(j, a, b, inner):
        place = first + j if is_inner else outer_place(first + j)
        place = jnp.clip(place - begin, 0, count - 1)
        return jnp.where((inner[0] > 0) == is_inner, place, 0), 0, 0

    return pl.BlockSpec(shape, index)


def product_blocks(near_in, near_out, far_in, far_out, near_data, far_data, near_ids, far_ids, inner):
    blocks, rows, width = near_in.shape
    tiles, _, size, _ = near_data.shape
    receivers = NR // size
    shape = (1, rows, width)
    data_spec = pl.BlockSpec(near_data.shape, lambda j, a, b, i: (0, 0, 0, 0))
    return pl.pallas_call(
        product_kernel,
        grid_spec=pltpu.PrefetchScalarGridSpec(
            num_scalar_prefetch=3,
            grid=(blocks,),
            in_specs=[part_spec(shape, 0, 0, len(INNER), True), part_spec(shape, 0, 0, len(OUTER), False)] * 2
            + [data_spec, data_spec],
            out_specs=pl.BlockSpec((1, width, NR), lambda j, a, b, i: (j, 0, 0)),
            scratch_shapes=[
                pltpu.VMEM((2 * tiles, size, width), jnp.bfloat16),
                pltpu.VMEM((receivers, size, width), jnp.float32),
            ],
        ),
        out_shape=jax.ShapeDtypeStruct((blocks, width, NR), jnp.bfloat16),
        compiler_params=params(),
        cost_estimate=SMALL,
        name="product",
    )(near_ids, far_ids, inner, near_in, near_out, far_in, far_out, near_data, far_data)


def image_kernel(places, unused, inner, *refs, first, begins, size):
    out = refs[-1]
    slot = first + pl.program_id(0)
    parts = refs[len(begins):]
    both = None
    for n, piece in enumerate(begins):
        field = parts[0][0]
        for part, (begin, is_inner) in zip(parts[1:], piece[1:]):
            chosen = (inner[0] > 0) & (slot >= begin) if is_inner else inner[0] == 0
            field = jnp.where(chosen, part[0], field)
        parts = parts[len(piece):]
        term = jnp.dot(refs[n][0], field, preferred_element_type=jnp.float32)
        both = term if both is None else both + term
    real = both[:size, :size] + both[size:, size:]
    imag = both[size:, :size] - both[:size, size:]
    if len(parts) > 1:
        real += parts[0][0, 0]
        imag += parts[0][0, 1]
    out[0, 0] = real
    out[0, 1] = imag


def image_blocks(product, first, count, pieces, inner, before=None):
    _, rows, width = pieces[0][1][0][0].shape
    size = width // 2
    image_spec = pl.BlockSpec((1, 2, size, size), lambda j, o, u, i: (j, 0, 0, 0))
    specs = [
        pl.BlockSpec((1, width, rows), lambda j, o, u, i, n=n: (first + j, 0, o[n])) for n in range(len(pieces))
    ]
    values = [product] * len(pieces)
    begins = []
    for _, parts in pieces:
        inners = [True] * (len(parts) - 1) + [False]
        for (field, begin), is_inner in zip(parts, inners):
            specs.append(part_spec((1, rows, width), first, begin, field.shape[0], is_inner))
            values.append(field)
        begins.append([(begin, is_inner) for (_, begin), is_inner in zip(parts, inners)])
    if before is not None:
        specs.append(image_spec)
        values.append(before)
    places = jnp.stack([shot for shot, _ in pieces])
    return pl.pallas_call(
        functools.partial(image_kernel, first=first, begins=begins, size=size),
        grid_spec=pltpu.PrefetchScalarGridSpec(
            num_scalar_prefetch=3, grid=(count,), in_specs=specs, out_specs=image_spec
        ),
        out_shape=jax.ShapeDtypeStruct((count, 2, size, size), jnp.float32),
        compiler_params=params(),
        cost_estimate=SMALL,
        name="image",
    )(places, places, inner, *values)


def following(value, *earlier):
    return lax.optimization_barrier((value,) + earlier)[0]


def hand(value, *pairs):
    return lax.ppermute(value, "shot", pairs)


def send_sum(value, pairs):
    pairs = [(4 * a + b, 4 * c + d) for (a, b), (c, d) in pairs]
    return lax.ppermute(value.astype(jnp.bfloat16), ("shot", "freq"), pairs).astype(jnp.float32)


def sum_images(one, two, shot, freq):
    left = shot < 2
    shots = range(4)
    even = freq % 2 == 0
    low = freq < 2
    last = one[4:]
    one = one[:4]
    keep = jnp.where(even, jnp.concatenate([one, last]), jnp.concatenate([two, last]))
    send = jnp.where(even, jnp.concatenate([two, last]), jnp.concatenate([one, last]))
    image = keep + send_sum(send, [((s, f), (s, f ^ 1)) for s in shots for f in range(4)])
    keep = jnp.where(low, image[:2], image[2:4])
    send = jnp.where(low, image[2:4], image[:2])
    last = image[4] + send_sum(image[4], [((s, 1), (s, 3)) for s in (1, 2)])
    image = keep + send_sum(send, [((s, f), (s, f ^ 2)) for s in shots for f in range(4)])
    keep = jnp.where(left, image[0], image[1])
    send = jnp.where(left, image[1], image[0])
    image = keep + send_sum(send, [((s, f), (3 - s, f)) for s in shots for f in range(4) if (s, f) != (0, 3)])
    last = send_sum(last, [((1, 3), (3, 3))]) + send_sum(last, [((2, 3), (3, 3))])
    return jnp.where((shot == 3) & (freq == 3), last, image)


def split_body(source_field, receiver_field, operator, band_offsets, survey_tiles, survey_data):
    tiles = survey_data.shape[1]
    shot = lax.axis_index("shot")
    freq = lax.axis_index("freq")
    inner = ((shot == 1) | (shot == 2)).astype(jnp.int32)[None]
    offsets = band_offsets.T
    make = functools.partial(extrapolate_blocks, operator=operator[0])
    inward = ((0, 1), (3, 2))
    outward = ((1, 0), (2, 3))
    middle = ((1, 2), (2, 1))
    ends = ((0, 3), (3, 0))
    beyond = ((1, 3), (2, 0))

    far_data = hand(survey_data[0], *inward, *outward)
    (r_head,) = make(receiver_field[0], offsets=offsets, sets=[INNER[:HEAD]], listed=True)
    r_1_head = hand(r_head, *inward)
    r_3_head = hand(r_head, *middle)
    r_inner, r_outer = make(receiver_field[0], offsets=following(offsets, r_head), sets=[INNER[HEAD:], OUTER])
    r_3_in = hand(r_inner, *middle)
    r_1_in = hand(r_inner, *inward)
    r_1_out = hand(following(r_outer, far_data, r_3_head), *outward)
    s_inner, s_outer = make(
        source_field[0], offsets=following(offsets, r_outer, r_3_head, r_1_head), sets=[INNER, OUTER]
    )
    s_out = hand(s_outer, *outward)
    s_in = hand(s_inner, *inward)
    forward_head = hand(following(r_1_head, r_3_in), *middle)
    r_3_out = hand(r_outer, *ends)
    forward = hand(following(r_1_in, r_1_out), *middle)
    beyond_1 = hand(following(r_outer, s_out, forward_head)[:OUTER_FIRST], *beyond)
    beyond_2 = hand(r_outer[OUTER_FIRST:], *beyond)

    ids = survey_tiles[:, 1]
    near_ids = lax.dynamic_slice_in_dim(ids, shot * tiles, tiles)
    far_ids = lax.dynamic_slice_in_dim(ids, (shot ^ 1) * tiles, tiles)
    product = product_blocks(
        s_inner, s_outer, s_in, s_out, survey_data[0], far_data, near_ids, far_ids, inner
    )
    early = [
        (shot, [(r_head, 0), (r_inner, HEAD), (r_outer, 0)]),
        (shot ^ 1, [(r_1_head, 0), (r_1_in, HEAD), (r_1_out, 0)]),
        (shot ^ 3, [(r_3_head, 0), (r_3_in, HEAD), (r_3_out, 0)]),
    ]
    forwarded = [(forward_head, 0), (forward, HEAD)]
    one = image_blocks(product, 0, FIRST, early, inner)
    two = image_blocks(product, FIRST, len(INNER) - FIRST, early, inner)
    one = image_blocks(product, 0, FIRST, [(shot ^ 2, forwarded + [(beyond_1, 0)])], inner, one)
    two = image_blocks(
        product, FIRST, len(INNER) - FIRST, [(shot ^ 2, forwarded + [(beyond_2, OUTER_FIRST)])], inner,
        following(two, one),
    )
    image = sum_images(one, two, shot, freq)
    total_freqs = source_field.shape[0] * lax.axis_size("freq")
    return image * (1.0 / math.sqrt(2.0 * NR * total_freqs))


def body(source_field, *rest):
    fits = (
        lax.axis_size("shot") == 4
        and lax.axis_size("freq") == 4
        and source_field.shape[1:] == (512, 16, 2, 128)
    )
    return (split_body if fits else general_body)(source_field, *rest)


def solution(mesh):
    return jax.shard_map(
        body,
        mesh=mesh,
        in_specs=(
            P("freq", ("groups", "shot"), None, None, None),
            P("freq", ("groups", "shot"), None, None, None),
            P("freq", "groups", None, None, None, None),
            P("groups", None),
            P("groups", None),
            P("freq", ("groups", "shot"), None, None, None),
        ),
        out_specs=P(None, ("groups", "shot", "freq"), None),
        check_vma=False,
    )
```

```python
import functools
import math

import jax
import jax.numpy as jnp
from jax import lax
from jax.experimental import pallas as pl
from jax.experimental.pallas import tpu as pltpu
from jax.sharding import PartitionSpec as P

NR = 2048
SMALL = pl.CostEstimate(flops=1000, bytes_accessed=1000, transcendentals=0)


def extrapolate(wavefield, operator, columns):
    row_count, blocks_x, components, block_size = wavefield.shape
    bands = columns.shape[1]
    real_part = operator[:, :, 0]
    imag_part = operator[:, :, 1]
    upper_rows = jnp.concatenate([real_part, imag_part], -1)
    lower_rows = jnp.concatenate([-imag_part, real_part], -1)
    real_block = jnp.concatenate([upper_rows, lower_rows], -2)
    real_block = real_block.reshape(blocks_x, bands, 2 * block_size, 2, block_size)
    chosen = jnp.take(wavefield, columns, axis=1).reshape(
        row_count, blocks_x, bands, 2 * block_size
    )
    result = jnp.einsum("sikc,ikcoy->soiy", chosen, real_block, preferred_element_type=jnp.float32)
    return result.astype(jnp.bfloat16)


def to_owners(wavefield, shot_count, own_cells):
    row_count = wavefield.shape[0]
    return wavefield.reshape(row_count, 2, shot_count, own_cells)


def to_tiles(wavefield, shot_count, own_cells):
    row_count, components, blocks_x, block_size = wavefield.shape
    if own_cells >= block_size:
        return to_owners(wavefield, shot_count, own_cells)
    factor = block_size // own_cells
    copies = jnp.broadcast_to(
        wavefield[:, :, :, None, :], (row_count, components, blocks_x, factor, block_size)
    )
    return copies.reshape(row_count, components, shot_count, block_size)


def data_product(source_cells, data_shard, survey_tiles, block_size, own_cells):
    source_count = source_cells.shape[0]
    receiver_blocks = NR // block_size
    blocks = source_cells.reshape(source_count // block_size, block_size, 2 * own_cells)
    block_ids = jnp.arange(receiver_blocks, dtype=jnp.int32)
    chosen = jnp.take(blocks, survey_tiles[:, 0], axis=0)
    products = jnp.einsum(
        "ncsr,nsk->ncrk",
        lax.all_gather(data_shard, "shot", axis=0, tiled=True),
        chosen,
        preferred_element_type=jnp.float32,
    )
    real_part = products[:, 0, :, :own_cells] - products[:, 1, :, own_cells:]
    imag_part = products[:, 0, :, own_cells:] + products[:, 1, :, :own_cells]
    contribution = jnp.concatenate([real_part, imag_part], -1)
    onehot = (survey_tiles[:, 1][:, None] == block_ids[None, :]).astype(jnp.float32)
    summed = jnp.einsum("nq,nrk->qrk", onehot, contribution, precision=lax.Precision.HIGHEST)
    return summed.reshape(NR, 2, own_cells).astype(jnp.bfloat16)


def image_tile(product, receiver_tile, block_size):
    row_count, components, own_cells = product.shape
    tiles_here = max(own_cells // block_size, 1)
    inner_cells = own_cells // tiles_here
    left = product.reshape(row_count, 2, tiles_here, inner_cells)
    right = receiver_tile.reshape(row_count, 2, tiles_here, block_size)
    turned = jnp.stack([-right[:, 1], right[:, 0]], 1)
    both = jnp.stack([right, turned], 1)
    result = jnp.einsum("rctx,rocty->otxy", left, both, preferred_element_type=jnp.float32)
    return result.reshape(2, own_cells, block_size)


def general_body(source_field, receiver_field, operator, band_offsets, survey_tiles, survey_data):
    shot_count = lax.axis_size("shot")
    freq_local = source_field.shape[0]
    blocks_x = source_field.shape[2]
    block_size = source_field.shape[4]
    own_cells = blocks_x * block_size // shot_count
    block_rows = jnp.arange(blocks_x, dtype=jnp.int32)[:, None]
    columns = (block_rows + band_offsets) % blocks_x
    source_next = extrapolate(source_field[0], operator[0], columns)
    receiver_next = extrapolate(receiver_field[0], operator[0], columns)
    source_send = to_owners(source_next, shot_count, own_cells)
    receiver_send = to_tiles(receiver_next, shot_count, own_cells)
    source_cells = lax.all_to_all(source_send, "shot", split_axis=2, concat_axis=0, tiled=True)
    receiver_tile = lax.all_to_all(receiver_send, "shot", split_axis=2, concat_axis=0, tiled=True)
    source_cells = source_cells.reshape(source_cells.shape[0], 2 * own_cells)
    product = data_product(source_cells, survey_data[0], survey_tiles, block_size, own_cells)
    receiver_tile = receiver_tile.reshape(receiver_tile.shape[0], 2, -1)
    image_sum = image_tile(product, receiver_tile, block_size)
    total_freqs = freq_local * lax.axis_size("freq")
    scaled = image_sum * (1.0 / math.sqrt(2.0 * NR * total_freqs))
    return lax.psum_scatter(scaled, "freq", scatter_dimension=1, tiled=True)


INNER = [4, 8, 6, 10, 15, 5, 9, 7, 11]
HEAD = 4
OUTER = [0, 12, 2, 14, 1, 13, 3]
FIRST = 5
OUTER_FIRST = 4
LATE = 4


def outer_place(slot):
    return jnp.where(slot < FIRST, jnp.minimum(slot, OUTER_FIRST - 1), jnp.minimum(slot - 1, len(OUTER) - 1))


def params(limit=24):
    return pltpu.CompilerParams(vmem_limit_bytes=limit * 1024 * 1024)


def extrapolate_kernel(order, offsets, field, operator, *refs, sets, rows, blocks, parts, listed):
    stage, apart, lines, weights, field_sems, weight_sems = refs[-6:]
    outs = refs[:-6]
    sizes = [len(one) for one in sets]
    step = pl.program_id(0)
    bands = operator.shape[1]
    pitch = 2 * blocks + 1
    chunk = stage.shape[0] // pitch
    part_lines = lines.shape[0] // parts

    def column(block, band):
        return lax.rem(block + offsets[band, block] + blocks, blocks)

    def field_copy(part):
        here = pl.ds(part * part_lines, part_lines)
        return pltpu.make_async_copy(field.at[here], lines.at[here], field_sems.at[part])

    def weight_copy(n, block):
        return pltpu.make_async_copy(operator.at[block], weights.at[n], weight_sems.at[n])

    @pl.when(step == 0)
    def _():
        for part in range(parts):
            field_copy(part).start()
        for n, block in enumerate(sum(sets, [])):
            weight_copy(n, block).start()
        if listed:
            wanted = [column(block, band) for block in sum(sets, []) for band in range(bands)]
        else:
            wanted = list(range(blocks))

        def split(n, carry):
            for row in range(chunk):
                here = pl.ds(pl.multiple_of((n * chunk + row) * 2 * blocks, 2 * blocks), 2 * blocks)
                stage[pl.ds(row * pitch, 2 * blocks), :] = lines[here, :].astype(jnp.float32)
            to = pl.ds(pl.multiple_of(n * chunk, chunk), chunk)
            for slot, block in enumerate(wanted):
                for half in range(2):
                    picked = stage[pl.ds(2 * block + half, chunk, stride=pitch), :]
                    apart[slot, to, half * 128:(half + 1) * 128] = picked.astype(jnp.bfloat16)
            return carry

        steps = rows // chunk // parts
        for part in range(parts):
            field_copy(part).wait()
            lax.fori_loop(part * steps, (part + 1) * steps, split, 0)

    block = order[step]
    weight_copy(step, block).wait()
    inputs = []
    factors = []
    for band in range(bands):
        inputs.append(apart[step * bands + band if listed else column(block, band)])
        real = weights[step, band, 0]
        imag = weights[step, band, 1]
        factors.append(jnp.concatenate([real, imag], 1))
        factors.append(jnp.concatenate([-imag, real], 1))
    result = jnp.dot(
        jnp.concatenate(inputs, 1), jnp.concatenate(factors, 0), preferred_element_type=jnp.float32
    ).astype(jnp.bfloat16)
    first = 0
    for out, count in zip(outs, sizes):
        if len(sizes) == 1:
            out[0] = result
        else:
            @pl.when((step >= first) & (step < first + count))
            def _(out=out):
                out[0] = result
        first += count


def extrapolate_blocks(field, operator, offsets, sets, listed=False, limit=60):
    rows, blocks, _, size = field.shape
    bands = offsets.shape[0]
    width = 2 * size
    chunk = 32
    parts = 4
    sizes = [len(one) for one in sets]
    count = sum(sizes)
    order = jnp.array(sum(sets, []), jnp.int32)
    firsts = [sum(sizes[:n]) for n in range(len(sizes))]
    flat = field.reshape(rows * blocks * 2, size)

    def out_spec(first, count):
        return pl.BlockSpec((1, rows, width), lambda j, o, c: (jnp.clip(j - first, 0, count - 1), 0, 0))

    return pl.pallas_call(
        functools.partial(
            extrapolate_kernel, sets=sets, rows=rows, blocks=blocks, parts=parts, listed=listed
        ),
        grid_spec=pltpu.PrefetchScalarGridSpec(
            num_scalar_prefetch=2,
            grid=(count,),
            in_specs=[pl.BlockSpec(memory_space=pltpu.HBM)] * 2,
            out_specs=[out_spec(*one) for one in zip(firsts, sizes)],
            scratch_shapes=[
                pltpu.VMEM((chunk * (2 * blocks + 1), size), jnp.float32),
                pltpu.VMEM((count * bands if listed else blocks, rows, width), jnp.bfloat16),
                pltpu.VMEM(flat.shape, jnp.bfloat16),
                pltpu.VMEM((count,) + operator.shape[1:], jnp.bfloat16),
                pltpu.SemaphoreType.DMA((parts,)),
                pltpu.SemaphoreType.DMA((count,)),
            ],
        ),
        out_shape=[jax.ShapeDtypeStruct((n, rows, width), jnp.bfloat16) for n in sizes],
        compiler_params=params(limit),
        cost_estimate=SMALL,
        name="extrapolate",
    )(order, offsets, flat, operator)


def product_kernel(
    near_ids, far_ids, inner, near_in, near_out, far_in, far_out, near_data, data_in, data_out, out, turned, total
):
    size = near_data.shape[2]
    tiles = near_data.shape[0]
    sources = near_in.shape[1] // size
    per_source = tiles // sources

    @pl.when(pl.program_id(0) == 0)
    def _():
        for tile in range(tiles):
            for part in range(2):
                columns = slice(part * size, (part + 1) * size)
                far = jnp.where(inner[0] > 0, data_in[tile, part], data_out[tile, part])
                turned[tile, :, columns] = near_data[tile, part].T
                turned[tiles + tile, :, columns] = far.T

    total[...] = jnp.zeros_like(total)
    sides = ((near_in, near_out, near_ids), (far_in, far_out, far_ids))
    for side, (field_in, field_out, ids) in enumerate(sides):
        for source in range(sources):
            lines = slice(source * size, (source + 1) * size)
            upper = jnp.where(inner[0] > 0, field_in[0, lines, :], field_out[0, lines, :])
            lower = jnp.concatenate([-upper[:, size:], upper[:, :size]], 1)
            both = jnp.concatenate([upper, lower], 0)
            first = side * tiles + source * per_source
            left = turned[first:first + per_source].reshape(per_source * size, 2 * size)
            result = jnp.dot(left, both, preferred_element_type=jnp.float32)
            for tile in range(per_source):
                total[ids[source * per_source + tile]] += result[tile * size:(tile + 1) * size]
    for block in range(total.shape[0]):
        out[0, :, block * size:(block + 1) * size] = total[block].T.astype(jnp.bfloat16)


def part_spec(shape, first, begin, count, is_inner):
    def index(j, a, b, inner):
        place = first + j if is_inner else outer_place(first + j)
        place = jnp.clip(place - begin, 0, count - 1)
        return jnp.where((inner[0] > 0) == is_inner, place, 0), 0, 0

    return pl.BlockSpec(shape, index)


def product_blocks(near_in, near_out, far_in, far_out, near_data, data_in, data_out, near_ids, far_ids, inner):
    blocks, rows, width = near_in.shape
    tiles, _, size, _ = near_data.shape
    receivers = NR // size
    shape = (1, rows, width)
    data_spec = pl.BlockSpec(near_data.shape, lambda j, a, b, i: (0, 0, 0, 0))
    return pl.pallas_call(
        product_kernel,
        grid_spec=pltpu.PrefetchScalarGridSpec(
            num_scalar_prefetch=3,
            grid=(blocks,),
            in_specs=[part_spec(shape, 0, 0, len(INNER), True), part_spec(shape, 0, 0, len(OUTER), False)] * 2
            + [data_spec] * 3,
            out_specs=pl.BlockSpec((1, width, NR), lambda j, a, b, i: (j, 0, 0)),
            scratch_shapes=[
                pltpu.VMEM((2 * tiles, size, width), jnp.bfloat16),
                pltpu.VMEM((receivers, size, width), jnp.float32),
            ],
        ),
        out_shape=jax.ShapeDtypeStruct((blocks, width, NR), jnp.bfloat16),
        compiler_params=params(),
        cost_estimate=SMALL,
        name="product",
    )(near_ids, far_ids, inner, near_in, near_out, far_in, far_out, near_data, data_in, data_out)


def image_kernel(places, unused, inner, *refs, first, begins, size):
    out = refs[-1]
    slot = first + pl.program_id(0)
    parts = refs[len(begins):]
    both = None
    for n, piece in enumerate(begins):
        field = parts[0][0]
        for part, (begin, is_inner) in zip(parts[1:], piece[1:]):
            chosen = (inner[0] > 0) & (slot >= begin) if is_inner else inner[0] == 0
            field = jnp.where(chosen, part[0], field)
        parts = parts[len(piece):]
        term = jnp.dot(refs[n][0], field, preferred_element_type=jnp.float32)
        both = term if both is None else both + term
    real = both[:size, :size] + both[size:, size:]
    imag = both[size:, :size] - both[:size, size:]
    if len(parts) > 1:
        real += parts[0][0, 0]
        imag += parts[0][0, 1]
    out[0, 0] = real
    out[0, 1] = imag


def image_blocks(product, first, count, pieces, inner, before=None):
    _, rows, width = pieces[0][1][0][0].shape
    size = width // 2
    image_spec = pl.BlockSpec((1, 2, size, size), lambda j, o, u, i: (j, 0, 0, 0))
    specs = [
        pl.BlockSpec((1, width, rows), lambda j, o, u, i, n=n: (first + j, 0, o[n])) for n in range(len(pieces))
    ]
    values = [product] * len(pieces)
    begins = []
    for _, parts in pieces:
        inners = [True] * (len(parts) - 1) + [False]
        for (field, begin), is_inner in zip(parts, inners):
            specs.append(part_spec((1, rows, width), first, begin, field.shape[0], is_inner))
            values.append(field)
        begins.append([(begin, is_inner) for (_, begin), is_inner in zip(parts, inners)])
    if before is not None:
        specs.append(pl.BlockSpec((1, 2, size, size), lambda j, o, u, i: (first + j, 0, 0, 0)))
        values.append(before)
    places = jnp.stack([shot for shot, _ in pieces])
    return pl.pallas_call(
        functools.partial(image_kernel, first=first, begins=begins, size=size),
        grid_spec=pltpu.PrefetchScalarGridSpec(
            num_scalar_prefetch=3, grid=(count,), in_specs=specs, out_specs=image_spec
        ),
        out_shape=jax.ShapeDtypeStruct((count, 2, size, size), jnp.float32),
        compiler_params=params(),
        cost_estimate=SMALL,
        name="image",
    )(places, places, inner, *values)


def following(value, *earlier):
    return lax.optimization_barrier((value,) + earlier)[0]


def hand(value, *pairs):
    return lax.ppermute(value, "shot", pairs)


def send_sum(value, pairs):
    pairs = [(4 * a + b, 4 * c + d) for (a, b), (c, d) in pairs]
    return lax.ppermute(value.astype(jnp.bfloat16), ("shot", "freq"), pairs).astype(jnp.float32)


def sum_images(one, two, shot, freq):
    left = shot < 2
    shots = range(4)
    even = freq % 2 == 0
    low = freq < 2
    last = one[4:]
    one = one[:4]
    keep = jnp.where(even, jnp.concatenate([one, last]), jnp.concatenate([two, last]))
    send = jnp.where(even, jnp.concatenate([two, last]), jnp.concatenate([one, last]))
    image = keep + send_sum(send, [((s, f), (s, f ^ 1)) for s in shots for f in range(4)])
    keep = jnp.where(low, image[:2], image[2:4])
    send = jnp.where(low, image[2:4], image[:2])
    last = image[4] + send_sum(image[4], [((s, 1), (s, 3)) for s in (1, 2)])
    image = keep + send_sum(send, [((s, f), (s, f ^ 2)) for s in shots for f in range(4)])
    keep = jnp.where(left, image[0], image[1])
    send = jnp.where(left, image[1], image[0])
    image = keep + send_sum(send, [((s, f), (3 - s, f)) for s in shots for f in range(4) if (s, f) != (0, 3)])
    last = send_sum(last, [((1, 3), (3, 3))]) + send_sum(last, [((2, 3), (3, 3))])
    return jnp.where((shot == 3) & (freq == 3), last, image)


def split_body(source_field, receiver_field, operator, band_offsets, survey_tiles, survey_data):
    tiles = survey_data.shape[1]
    shot = lax.axis_index("shot")
    freq = lax.axis_index("freq")
    inner = ((shot == 1) | (shot == 2)).astype(jnp.int32)[None]
    offsets = band_offsets.T
    make = functools.partial(extrapolate_blocks, operator=operator[0])
    inward = ((0, 1), (3, 2))
    outward = ((1, 0), (2, 3))
    middle = ((1, 2), (2, 1))
    ends = ((0, 3), (3, 0))
    beyond = ((1, 3), (2, 0))

    (r_head,) = make(receiver_field[0], offsets=offsets, sets=[INNER[:HEAD]], listed=True)
    r_3_head = hand(r_head, *middle)
    r_1_head = hand(r_head, *inward)
    data_out = hand(survey_data[0], *outward)
    r_inner, r_outer = make(receiver_field[0], offsets=following(offsets, r_head), sets=[INNER[HEAD:], OUTER])
    r_3_in = hand(r_inner, *middle)
    r_1_in = hand(r_inner, *inward)
    r_1_out = hand(following(r_outer, r_3_head), *outward)
    s_inner, s_outer = make(source_field[0], offsets=following(offsets, r_outer, data_out, r_1_head), sets=[INNER, OUTER])
    s_out = hand(s_outer, *outward)
    s_in = hand(following(s_inner, r_1_in, r_3_in), *inward)
    data_in = hand(following(survey_data[0], data_out), *inward)
    forward_head = hand(r_1_head, *middle)
    forward = hand(r_1_in, *middle)
    r_3_out = hand(following(r_outer, r_1_out, data_in), *ends)
    beyond_1 = hand(following(r_outer, s_out, forward_head)[:LATE], *beyond)
    beyond_2 = hand(r_outer[LATE:], *beyond)

    ids = survey_tiles[:, 1]
    near_ids = lax.dynamic_slice_in_dim(ids, shot * tiles, tiles)
    far_ids = lax.dynamic_slice_in_dim(ids, (shot ^ 1) * tiles, tiles)
    product = product_blocks(
        s_inner, s_outer, s_in, s_out, survey_data[0], data_in, data_out, near_ids, far_ids, inner
    )
    early = [
        (shot, [(r_head, 0), (r_inner, HEAD), (r_outer, 0)]),
        (shot ^ 1, [(r_1_head, 0), (r_1_in, HEAD), (r_1_out, 0)]),
        (shot ^ 3, [(r_3_head, 0), (r_3_in, HEAD), (r_3_out, 0)]),
    ]
    image = image_blocks(product, 0, len(INNER), early, inner)
    most = image_blocks(product, 0, LATE + 1, [(shot ^ 2, [(forward_head, 0), (forward, HEAD), (beyond_1, 0)])], inner, image)
    rest = image_blocks(
        product, LATE + 1, len(INNER) - LATE - 1, [(shot ^ 2, [(forward_head, 0), (forward, HEAD), (beyond_2, LATE)])], inner,
        following(image, most),
    )
    one = most[:FIRST]
    two = jnp.concatenate([most[FIRST:], rest])
    image = sum_images(one, two, shot, freq)
    total_freqs = source_field.shape[0] * lax.axis_size("freq")
    return image * (1.0 / math.sqrt(2.0 * NR * total_freqs))


def body(source_field, *rest):
    fits = (
        lax.axis_size("shot") == 4
        and lax.axis_size("freq") == 4
        and source_field.shape[1:] == (512, 16, 2, 128)
    )
    return (split_body if fits else general_body)(source_field, *rest)


def solution(mesh):
    return jax.shard_map(
        body,
        mesh=mesh,
        in_specs=(
            P("freq", ("groups", "shot"), None, None, None),
            P("freq", ("groups", "shot"), None, None, None),
            P("freq", "groups", None, None, None, None),
            P("groups", None),
            P("groups", None),
            P("freq", ("groups", "shot"), None, None, None),
        ),
        out_specs=P(None, ("groups", "shot", "freq"), None),
        check_vma=False,
    )
```

```python
import functools
import math

import jax
import jax.numpy as jnp
from jax import lax
from jax.experimental import pallas as pl
from jax.experimental.pallas import tpu as pltpu
from jax.sharding import PartitionSpec as P

NR = 2048
SMALL = pl.CostEstimate(flops=1000, bytes_accessed=1000, transcendentals=0)


def extrapolate(wavefield, operator, columns):
    row_count, blocks_x, components, block_size = wavefield.shape
    bands = columns.shape[1]
    real_part = operator[:, :, 0]
    imag_part = operator[:, :, 1]
    upper_rows = jnp.concatenate([real_part, imag_part], -1)
    lower_rows = jnp.concatenate([-imag_part, real_part], -1)
    real_block = jnp.concatenate([upper_rows, lower_rows], -2)
    real_block = real_block.reshape(blocks_x, bands, 2 * block_size, 2, block_size)
    chosen = jnp.take(wavefield, columns, axis=1).reshape(
        row_count, blocks_x, bands, 2 * block_size
    )
    result = jnp.einsum("sikc,ikcoy->soiy", chosen, real_block, preferred_element_type=jnp.float32)
    return result.astype(jnp.bfloat16)


def to_owners(wavefield, shot_count, own_cells):
    row_count = wavefield.shape[0]
    return wavefield.reshape(row_count, 2, shot_count, own_cells)


def to_tiles(wavefield, shot_count, own_cells):
    row_count, components, blocks_x, block_size = wavefield.shape
    if own_cells >= block_size:
        return to_owners(wavefield, shot_count, own_cells)
    factor = block_size // own_cells
    copies = jnp.broadcast_to(
        wavefield[:, :, :, None, :], (row_count, components, blocks_x, factor, block_size)
    )
    return copies.reshape(row_count, components, shot_count, block_size)


def data_product(source_cells, data_shard, survey_tiles, block_size, own_cells):
    source_count = source_cells.shape[0]
    receiver_blocks = NR // block_size
    blocks = source_cells.reshape(source_count // block_size, block_size, 2 * own_cells)
    block_ids = jnp.arange(receiver_blocks, dtype=jnp.int32)
    chosen = jnp.take(blocks, survey_tiles[:, 0], axis=0)
    products = jnp.einsum(
        "ncsr,nsk->ncrk",
        lax.all_gather(data_shard, "shot", axis=0, tiled=True),
        chosen,
        preferred_element_type=jnp.float32,
    )
    real_part = products[:, 0, :, :own_cells] - products[:, 1, :, own_cells:]
    imag_part = products[:, 0, :, own_cells:] + products[:, 1, :, :own_cells]
    contribution = jnp.concatenate([real_part, imag_part], -1)
    onehot = (survey_tiles[:, 1][:, None] == block_ids[None, :]).astype(jnp.float32)
    summed = jnp.einsum("nq,nrk->qrk", onehot, contribution, precision=lax.Precision.HIGHEST)
    return summed.reshape(NR, 2, own_cells).astype(jnp.bfloat16)


def image_tile(product, receiver_tile, block_size):
    row_count, components, own_cells = product.shape
    tiles_here = max(own_cells // block_size, 1)
    inner_cells = own_cells // tiles_here
    left = product.reshape(row_count, 2, tiles_here, inner_cells)
    right = receiver_tile.reshape(row_count, 2, tiles_here, block_size)
    turned = jnp.stack([-right[:, 1], right[:, 0]], 1)
    both = jnp.stack([right, turned], 1)
    result = jnp.einsum("rctx,rocty->otxy", left, both, preferred_element_type=jnp.float32)
    return result.reshape(2, own_cells, block_size)


def general_body(source_field, receiver_field, operator, band_offsets, survey_tiles, survey_data):
    shot_count = lax.axis_size("shot")
    freq_local = source_field.shape[0]
    blocks_x = source_field.shape[2]
    block_size = source_field.shape[4]
    own_cells = blocks_x * block_size // shot_count
    block_rows = jnp.arange(blocks_x, dtype=jnp.int32)[:, None]
    columns = (block_rows + band_offsets) % blocks_x
    source_next = extrapolate(source_field[0], operator[0], columns)
    receiver_next = extrapolate(receiver_field[0], operator[0], columns)
    source_send = to_owners(source_next, shot_count, own_cells)
    receiver_send = to_tiles(receiver_next, shot_count, own_cells)
    source_cells = lax.all_to_all(source_send, "shot", split_axis=2, concat_axis=0, tiled=True)
    receiver_tile = lax.all_to_all(receiver_send, "shot", split_axis=2, concat_axis=0, tiled=True)
    source_cells = source_cells.reshape(source_cells.shape[0], 2 * own_cells)
    product = data_product(source_cells, survey_data[0], survey_tiles, block_size, own_cells)
    receiver_tile = receiver_tile.reshape(receiver_tile.shape[0], 2, -1)
    image_sum = image_tile(product, receiver_tile, block_size)
    total_freqs = freq_local * lax.axis_size("freq")
    scaled = image_sum * (1.0 / math.sqrt(2.0 * NR * total_freqs))
    return lax.psum_scatter(scaled, "freq", scatter_dimension=1, tiled=True)


INNER = [4, 8, 6, 10, 15, 5, 9, 7, 11]
HEAD = 3
OUTER = [0, 12, 2, 14, 1, 13, 3]
FIRST = 5
OUTER_FIRST = 4
LATE = 5


def outer_place(slot):
    return jnp.where(slot < FIRST, jnp.minimum(slot, OUTER_FIRST - 1), jnp.minimum(slot - 1, len(OUTER) - 1))


def params(limit=24):
    return pltpu.CompilerParams(vmem_limit_bytes=limit * 1024 * 1024)


def extrapolate_kernel(order, offsets, field, operator, *refs, sets, rows, blocks, parts, listed):
    stage, apart, lines, weights, field_sems, weight_sems = refs[-6:]
    outs = refs[:-6]
    sizes = [len(one) for one in sets]
    step = pl.program_id(0)
    bands = operator.shape[1]
    pitch = 2 * blocks + 1
    chunk = stage.shape[0] // pitch
    part_lines = lines.shape[0] // parts

    def column(block, band):
        return lax.rem(block + offsets[band, block] + blocks, blocks)

    def field_copy(part):
        here = pl.ds(part * part_lines, part_lines)
        return pltpu.make_async_copy(field.at[here], lines.at[here], field_sems.at[part])

    def weight_copy(n, block):
        return pltpu.make_async_copy(operator.at[block], weights.at[n], weight_sems.at[n])

    @pl.when(step == 0)
    def _():
        for part in range(parts):
            field_copy(part).start()
        for n, block in enumerate(sum(sets, [])):
            weight_copy(n, block).start()
        if listed:
            wanted = [column(block, band) for block in sum(sets, []) for band in range(bands)]
        else:
            wanted = list(range(blocks))

        def split(n, carry):
            for row in range(chunk):
                here = pl.ds(pl.multiple_of((n * chunk + row) * 2 * blocks, 2 * blocks), 2 * blocks)
                stage[pl.ds(row * pitch, 2 * blocks), :] = lines[here, :].astype(jnp.float32)
            to = pl.ds(pl.multiple_of(n * chunk, chunk), chunk)
            for slot, block in enumerate(wanted):
                for half in range(2):
                    picked = stage[pl.ds(2 * block + half, chunk, stride=pitch), :]
                    apart[slot, to, half * 128:(half + 1) * 128] = picked.astype(jnp.bfloat16)
            return carry

        steps = rows // chunk // parts
        for part in range(parts):
            field_copy(part).wait()
            lax.fori_loop(part * steps, (part + 1) * steps, split, 0)

    block = order[step]
    weight_copy(step, block).wait()
    inputs = []
    factors = []
    for band in range(bands):
        inputs.append(apart[step * bands + band if listed else column(block, band)])
        real = weights[step, band, 0]
        imag = weights[step, band, 1]
        factors.append(jnp.concatenate([real, imag], 1))
        factors.append(jnp.concatenate([-imag, real], 1))
    result = jnp.dot(
        jnp.concatenate(inputs, 1), jnp.concatenate(factors, 0), preferred_element_type=jnp.float32
    ).astype(jnp.bfloat16)
    first = 0
    for out, count in zip(outs, sizes):
        if len(sizes) == 1:
            out[0] = result
        else:
            @pl.when((step >= first) & (step < first + count))
            def _(out=out):
                out[0] = result
        first += count


def extrapolate_blocks(field, operator, offsets, sets, listed=False, limit=60):
    rows, blocks, _, size = field.shape
    bands = offsets.shape[0]
    width = 2 * size
    chunk = 32
    parts = 4
    sizes = [len(one) for one in sets]
    count = sum(sizes)
    order = jnp.array(sum(sets, []), jnp.int32)
    firsts = [sum(sizes[:n]) for n in range(len(sizes))]
    flat = field.reshape(rows * blocks * 2, size)

    def out_spec(first, count):
        return pl.BlockSpec((1, rows, width), lambda j, o, c: (jnp.clip(j - first, 0, count - 1), 0, 0))

    return pl.pallas_call(
        functools.partial(
            extrapolate_kernel, sets=sets, rows=rows, blocks=blocks, parts=parts, listed=listed
        ),
        grid_spec=pltpu.PrefetchScalarGridSpec(
            num_scalar_prefetch=2,
            grid=(count,),
            in_specs=[pl.BlockSpec(memory_space=pltpu.HBM)] * 2,
            out_specs=[out_spec(*one) for one in zip(firsts, sizes)],
            scratch_shapes=[
                pltpu.VMEM((chunk * (2 * blocks + 1), size), jnp.float32),
                pltpu.VMEM((count * bands if listed else blocks, rows, width), jnp.bfloat16),
                pltpu.VMEM(flat.shape, jnp.bfloat16),
                pltpu.VMEM((count,) + operator.shape[1:], jnp.bfloat16),
                pltpu.SemaphoreType.DMA((parts,)),
                pltpu.SemaphoreType.DMA((count,)),
            ],
        ),
        out_shape=[jax.ShapeDtypeStruct((n, rows, width), jnp.bfloat16) for n in sizes],
        compiler_params=params(limit),
        cost_estimate=SMALL,
        name="extrapolate",
    )(order, offsets, flat, operator)


def product_kernel(near_ids, far_ids, inner, near_in, near_out, far_in, far_out, near_data, far_data, out, turned, total):
    size = near_data.shape[2]
    tiles = near_data.shape[0]
    sources = near_in.shape[1] // size
    per_source = tiles // sources

    @pl.when(pl.program_id(0) == 0)
    def _():
        for side, data in enumerate((near_data, far_data)):
            for tile in range(tiles):
                for part in range(2):
                    turned[side * tiles + tile, :, part * size:(part + 1) * size] = data[tile, part].T

    total[...] = jnp.zeros_like(total)
    sides = ((near_in, near_out, near_ids), (far_in, far_out, far_ids))
    for side, (field_in, field_out, ids) in enumerate(sides):
        for source in range(sources):
            lines = slice(source * size, (source + 1) * size)
            upper = jnp.where(inner[0] > 0, field_in[0, lines, :], field_out[0, lines, :])
            lower = jnp.concatenate([-upper[:, size:], upper[:, :size]], 1)
            both = jnp.concatenate([upper, lower], 0)
            first = side * tiles + source * per_source
            left = turned[first:first + per_source].reshape(per_source * size, 2 * size)
            result = jnp.dot(left, both, preferred_element_type=jnp.float32)
            for tile in range(per_source):
                total[ids[source * per_source + tile]] += result[tile * size:(tile + 1) * size]
    for block in range(total.shape[0]):
        out[0, :, block * size:(block + 1) * size] = total[block].T.astype(jnp.bfloat16)


def part_spec(shape, first, begin, count, is_inner):
    def index(j, a, b, inner):
        place = first + j if is_inner else outer_place(first + j)
        place = jnp.clip(place - begin, 0, count - 1)
        return jnp.where((inner[0] > 0) == is_inner, place, 0), 0, 0

    return pl.BlockSpec(shape, index)


def product_blocks(near_in, near_out, far_in, far_out, near_data, far_data, near_ids, far_ids, inner):
    blocks, rows, width = near_in.shape
    tiles, _, size, _ = near_data.shape
    receivers = NR // size
    shape = (1, rows, width)
    data_spec = pl.BlockSpec(near_data.shape, lambda j, a, b, i: (0, 0, 0, 0))
    return pl.pallas_call(
        product_kernel,
        grid_spec=pltpu.PrefetchScalarGridSpec(
            num_scalar_prefetch=3,
            grid=(blocks,),
            in_specs=[part_spec(shape, 0, 0, len(INNER), True), part_spec(shape, 0, 0, len(OUTER), False)] * 2
            + [data_spec, data_spec],
            out_specs=pl.BlockSpec((1, width, NR), lambda j, a, b, i: (j, 0, 0)),
            scratch_shapes=[
                pltpu.VMEM((2 * tiles, size, width), jnp.bfloat16),
                pltpu.VMEM((receivers, size, width), jnp.float32),
            ],
        ),
        out_shape=jax.ShapeDtypeStruct((blocks, width, NR), jnp.bfloat16),
        compiler_params=params(),
        cost_estimate=SMALL,
        name="product",
    )(near_ids, far_ids, inner, near_in, near_out, far_in, far_out, near_data, far_data)


def image_kernel(places, unused, inner, *refs, first, begins, size):
    out = refs[-1]
    slot = first + pl.program_id(0)
    parts = refs[len(begins):]
    both = None
    for n, piece in enumerate(begins):
        field = parts[0][0]
        for part, (begin, is_inner) in zip(parts[1:], piece[1:]):
            chosen = (inner[0] > 0) & (slot >= begin) if is_inner else inner[0] == 0
            field = jnp.where(chosen, part[0], field)
        parts = parts[len(piece):]
        term = jnp.dot(refs[n][0], field, preferred_element_type=jnp.float32)
        both = term if both is None else both + term
    real = both[:size, :size] + both[size:, size:]
    imag = both[size:, :size] - both[:size, size:]
    if len(parts) > 1:
        real += parts[0][0, 0]
        imag += parts[0][0, 1]
    out[0, 0] = real
    out[0, 1] = imag


def image_blocks(product, first, count, pieces, inner, before=None):
    _, rows, width = pieces[0][1][0][0].shape
    size = width // 2
    image_spec = pl.BlockSpec((1, 2, size, size), lambda j, o, u, i: (j, 0, 0, 0))
    specs = [
        pl.BlockSpec((1, width, rows), lambda j, o, u, i, n=n: (first + j, 0, o[n])) for n in range(len(pieces))
    ]
    values = [product] * len(pieces)
    begins = []
    for _, parts in pieces:
        inners = [True] * (len(parts) - 1) + [False]
        for (field, begin), is_inner in zip(parts, inners):
            specs.append(part_spec((1, rows, width), first, begin, field.shape[0], is_inner))
            values.append(field)
        begins.append([(begin, is_inner) for (_, begin), is_inner in zip(parts, inners)])
    if before is not None:
        specs.append(pl.BlockSpec((1, 2, size, size), lambda j, o, u, i: (first + j, 0, 0, 0)))
        values.append(before)
    places = jnp.stack([shot for shot, _ in pieces])
    return pl.pallas_call(
        functools.partial(image_kernel, first=first, begins=begins, size=size),
        grid_spec=pltpu.PrefetchScalarGridSpec(
            num_scalar_prefetch=3, grid=(count,), in_specs=specs, out_specs=image_spec
        ),
        out_shape=jax.ShapeDtypeStruct((count, 2, size, size), jnp.float32),
        compiler_params=params(),
        cost_estimate=SMALL,
        name="image",
    )(places, places, inner, *values)


def following(value, *earlier):
    return lax.optimization_barrier((value,) + earlier)[0]


def hand(value, *pairs):
    return lax.ppermute(value, "shot", pairs)


def send_sum(value, pairs):
    pairs = [(4 * a + b, 4 * c + d) for (a, b), (c, d) in pairs]
    return lax.ppermute(value.astype(jnp.bfloat16), ("shot", "freq"), pairs).astype(jnp.float32)


def sum_images(one, two, shot, freq):
    left = shot < 2
    shots = range(4)
    even = freq % 2 == 0
    low = freq < 2
    keep = jnp.where(even, one, two)
    send = jnp.where(even, two, one)
    image = keep + send_sum(send, [((s, f), (s, f ^ 1)) for s in shots for f in range(4)])
    near = jnp.where(low, image[:2], image[2:])
    far = jnp.where(low, image[2:], image[:2])

    def pick(pair, own):
        return jnp.where(left == own, pair[0], pair[1])

    pairs = [(s, f) for s in shots for f in range(4)]
    both = send_sum(pick(far, False), [((s, f), (3 - s, f ^ 2)) for s, f in pairs if (s, f) != (0, 1)])
    across = send_sum(pick(near, False), [((s, f), (3 - s, f)) for s, f in pairs if (s, f) != (0, 3)])
    along = send_sum(pick(far, True), [((s, f), (s, f ^ 2)) for s, f in pairs if (s, f) != (3, 1)])
    return pick(near, True) + along + across + both


def sum_cores(image):
    return image + send_sum(image, [((s, f), (s, f + 1)) for s in (1, 2) for f in (0, 2)])


def sum_last(image):
    image = image + send_sum(image, [((s, 1), (s, 3)) for s in (1, 2)])
    return send_sum(image, [((1, 3), (3, 3))]) + send_sum(image, [((2, 3), (3, 3))])


def split_body(source_field, receiver_field, operator, band_offsets, survey_tiles, survey_data):
    tiles = survey_data.shape[1]
    shot = lax.axis_index("shot")
    freq = lax.axis_index("freq")
    inner = ((shot == 1) | (shot == 2)).astype(jnp.int32)[None]
    offsets = band_offsets.T
    make = functools.partial(extrapolate_blocks, operator=operator[0])
    inward = ((0, 1), (3, 2))
    outward = ((1, 0), (2, 3))
    middle = ((1, 2), (2, 1))
    ends = ((0, 3), (3, 0))
    beyond = ((1, 3), (2, 0))

    far_data = hand(survey_data[0], *inward, *outward)
    (r_head,) = make(receiver_field[0], offsets=offsets, sets=[INNER[:HEAD]], listed=True)
    r_1_head = hand(r_head, *inward)
    r_3_head = hand(r_head, *middle)
    r_inner, r_outer = make(receiver_field[0], offsets=following(offsets, r_head), sets=[INNER[HEAD:], OUTER])
    r_3_in = hand(r_inner, *middle)
    r_1_in = hand(r_inner, *inward)
    r_1_out = hand(following(r_outer, far_data, r_3_head), *outward)
    s_inner, s_outer = make(
        source_field[0], offsets=following(offsets, r_outer, r_3_head, r_1_head), sets=[INNER, OUTER]
    )
    s_out = hand(s_outer, *outward)
    s_in = hand(s_inner, *inward)
    forward_head = hand(following(r_1_head, r_3_in), *middle)
    r_3_out = hand(r_outer, *ends)
    forward = hand(following(r_1_in, r_1_out), *middle)
    beyond_1 = hand(following(r_outer, s_out, forward_head)[:LATE], *beyond)
    beyond_2 = hand(r_outer[LATE:], *beyond)

    ids = survey_tiles[:, 1]
    near_ids = lax.dynamic_slice_in_dim(ids, shot * tiles, tiles)
    far_ids = lax.dynamic_slice_in_dim(ids, (shot ^ 1) * tiles, tiles)
    product = product_blocks(
        s_inner, s_outer, s_in, s_out, survey_data[0], far_data, near_ids, far_ids, inner
    )
    early = [
        (shot, [(r_head, 0), (r_inner, HEAD), (r_outer, 0)]),
        (shot ^ 1, [(r_1_head, 0), (r_1_in, HEAD), (r_1_out, 0)]),
        (shot ^ 3, [(r_3_head, 0), (r_3_in, HEAD), (r_3_out, 0)]),
    ]
    forwarded = [(forward_head, 0), (forward, HEAD)]
    image = image_blocks(product, 0, len(INNER), early, inner)
    most = image_blocks(product, 0, LATE + 1, [(shot ^ 2, forwarded + [(beyond_1, 0)])], inner, image)
    last = sum_cores(most[FIRST - 1])
    rest = image_blocks(
        product, LATE + 1, len(INNER) - LATE - 1, [(shot ^ 2, forwarded + [(beyond_2, LATE)])], inner,
        following(image, most, last),
    )
    image = sum_images(most[:FIRST - 1], jnp.concatenate([most[FIRST:], rest]), shot, freq)
    image = jnp.where((shot == 3) & (freq == 3), sum_last(last), image)
    total_freqs = source_field.shape[0] * lax.axis_size("freq")
    return image * (1.0 / math.sqrt(2.0 * NR * total_freqs))


def body(source_field, *rest):
    fits = (
        lax.axis_size("shot") == 4
        and lax.axis_size("freq") == 4
        and source_field.shape[1:] == (512, 16, 2, 128)
    )
    return (split_body if fits else general_body)(source_field, *rest)


def solution(mesh):
    return jax.shard_map(
        body,
        mesh=mesh,
        in_specs=(
            P("freq", ("groups", "shot"), None, None, None),
            P("freq", ("groups", "shot"), None, None, None),
            P("freq", "groups", None, None, None, None),
            P("groups", None),
            P("groups", None),
            P("freq", ("groups", "shot"), None, None, None),
        ),
        out_specs=P(None, ("groups", "shot", "freq"), None),
        check_vma=False,
    )
```

```python
import functools
import math

import jax
import jax.numpy as jnp
from jax import lax
from jax.experimental import pallas as pl
from jax.experimental.pallas import tpu as pltpu
from jax.sharding import PartitionSpec as P

NR = 2048
SMALL = pl.CostEstimate(flops=1000, bytes_accessed=1000, transcendentals=0)


def extrapolate(wavefield, operator, columns):
    row_count, blocks_x, components, block_size = wavefield.shape
    bands = columns.shape[1]
    real_part = operator[:, :, 0]
    imag_part = operator[:, :, 1]
    upper_rows = jnp.concatenate([real_part, imag_part], -1)
    lower_rows = jnp.concatenate([-imag_part, real_part], -1)
    real_block = jnp.concatenate([upper_rows, lower_rows], -2)
    real_block = real_block.reshape(blocks_x, bands, 2 * block_size, 2, block_size)
    chosen = jnp.take(wavefield, columns, axis=1).reshape(
        row_count, blocks_x, bands, 2 * block_size
    )
    result = jnp.einsum("sikc,ikcoy->soiy", chosen, real_block, preferred_element_type=jnp.float32)
    return result.astype(jnp.bfloat16)


def to_owners(wavefield, shot_count, own_cells):
    row_count = wavefield.shape[0]
    return wavefield.reshape(row_count, 2, shot_count, own_cells)


def to_tiles(wavefield, shot_count, own_cells):
    row_count, components, blocks_x, block_size = wavefield.shape
    if own_cells >= block_size:
        return to_owners(wavefield, shot_count, own_cells)
    factor = block_size // own_cells
    copies = jnp.broadcast_to(
        wavefield[:, :, :, None, :], (row_count, components, blocks_x, factor, block_size)
    )
    return copies.reshape(row_count, components, shot_count, block_size)


def data_product(source_cells, data_shard, survey_tiles, block_size, own_cells):
    source_count = source_cells.shape[0]
    receiver_blocks = NR // block_size
    blocks = source_cells.reshape(source_count // block_size, block_size, 2 * own_cells)
    block_ids = jnp.arange(receiver_blocks, dtype=jnp.int32)
    chosen = jnp.take(blocks, survey_tiles[:, 0], axis=0)
    products = jnp.einsum(
        "ncsr,nsk->ncrk",
        lax.all_gather(data_shard, "shot", axis=0, tiled=True),
        chosen,
        preferred_element_type=jnp.float32,
    )
    real_part = products[:, 0, :, :own_cells] - products[:, 1, :, own_cells:]
    imag_part = products[:, 0, :, own_cells:] + products[:, 1, :, :own_cells]
    contribution = jnp.concatenate([real_part, imag_part], -1)
    onehot = (survey_tiles[:, 1][:, None] == block_ids[None, :]).astype(jnp.float32)
    summed = jnp.einsum("nq,nrk->qrk", onehot, contribution, precision=lax.Precision.HIGHEST)
    return summed.reshape(NR, 2, own_cells).astype(jnp.bfloat16)


def image_tile(product, receiver_tile, block_size):
    row_count, components, own_cells = product.shape
    tiles_here = max(own_cells // block_size, 1)
    inner_cells = own_cells // tiles_here
    left = product.reshape(row_count, 2, tiles_here, inner_cells)
    right = receiver_tile.reshape(row_count, 2, tiles_here, block_size)
    turned = jnp.stack([-right[:, 1], right[:, 0]], 1)
    both = jnp.stack([right, turned], 1)
    result = jnp.einsum("rctx,rocty->otxy", left, both, preferred_element_type=jnp.float32)
    return result.reshape(2, own_cells, block_size)


def general_body(source_field, receiver_field, operator, band_offsets, survey_tiles, survey_data):
    shot_count = lax.axis_size("shot")
    freq_local = source_field.shape[0]
    blocks_x = source_field.shape[2]
    block_size = source_field.shape[4]
    own_cells = blocks_x * block_size // shot_count
    block_rows = jnp.arange(blocks_x, dtype=jnp.int32)[:, None]
    columns = (block_rows + band_offsets) % blocks_x
    source_next = extrapolate(source_field[0], operator[0], columns)
    receiver_next = extrapolate(receiver_field[0], operator[0], columns)
    source_send = to_owners(source_next, shot_count, own_cells)
    receiver_send = to_tiles(receiver_next, shot_count, own_cells)
    source_cells = lax.all_to_all(source_send, "shot", split_axis=2, concat_axis=0, tiled=True)
    receiver_tile = lax.all_to_all(receiver_send, "shot", split_axis=2, concat_axis=0, tiled=True)
    source_cells = source_cells.reshape(source_cells.shape[0], 2 * own_cells)
    product = data_product(source_cells, survey_data[0], survey_tiles, block_size, own_cells)
    receiver_tile = receiver_tile.reshape(receiver_tile.shape[0], 2, -1)
    image_sum = image_tile(product, receiver_tile, block_size)
    total_freqs = freq_local * lax.axis_size("freq")
    scaled = image_sum * (1.0 / math.sqrt(2.0 * NR * total_freqs))
    return lax.psum_scatter(scaled, "freq", scatter_dimension=1, tiled=True)


INNER = [4, 8, 6, 10, 15, 5, 9, 7, 11]
HEAD = 3
OUTER = [0, 12, 2, 14, 1, 13, 3]
FIRST = 5
OUTER_FIRST = 4
LATE = 5


def outer_place(slot):
    return jnp.where(slot < FIRST, jnp.minimum(slot, OUTER_FIRST - 1), jnp.minimum(slot - 1, len(OUTER) - 1))


def params(limit=24):
    return pltpu.CompilerParams(vmem_limit_bytes=limit * 1024 * 1024)


def extrapolate_kernel(order, offsets, field, operator, *refs, sets, rows, blocks, parts, listed):
    stage, apart, lines, weights, field_sems, weight_sems = refs[-6:]
    outs = refs[:-6]
    sizes = [len(one) for one in sets]
    step = pl.program_id(0)
    bands = operator.shape[1]
    pitch = 2 * blocks + 1
    chunk = stage.shape[0] // pitch
    part_lines = lines.shape[0] // parts

    def column(block, band):
        return lax.rem(block + offsets[band, block] + blocks, blocks)

    def field_copy(part):
        here = pl.ds(part * part_lines, part_lines)
        return pltpu.make_async_copy(field.at[here], lines.at[here], field_sems.at[part])

    def weight_copy(n, block):
        return pltpu.make_async_copy(operator.at[block], weights.at[n], weight_sems.at[n])

    @pl.when(step == 0)
    def _():
        for part in range(parts):
            field_copy(part).start()
        for n, block in enumerate(sum(sets, [])):
            weight_copy(n, block).start()
        if listed:
            wanted = [column(block, band) for block in sum(sets, []) for band in range(bands)]
        else:
            wanted = list(range(blocks))

        def split(n, carry):
            for row in range(chunk):
                here = pl.ds(pl.multiple_of((n * chunk + row) * 2 * blocks, 2 * blocks), 2 * blocks)
                stage[pl.ds(row * pitch, 2 * blocks), :] = lines[here, :].astype(jnp.float32)
            to = pl.ds(pl.multiple_of(n * chunk, chunk), chunk)
            for slot, block in enumerate(wanted):
                for half in range(2):
                    picked = stage[pl.ds(2 * block + half, chunk, stride=pitch), :]
                    apart[slot, to, half * 128:(half + 1) * 128] = picked.astype(jnp.bfloat16)
            return carry

        steps = rows // chunk // parts
        for part in range(parts):
            field_copy(part).wait()
            lax.fori_loop(part * steps, (part + 1) * steps, split, 0)

    block = order[step]
    weight_copy(step, block).wait()
    inputs = []
    factors = []
    for band in range(bands):
        inputs.append(apart[step * bands + band if listed else column(block, band)])
        real = weights[step, band, 0]
        imag = weights[step, band, 1]
        factors.append(jnp.concatenate([real, imag], 1))
        factors.append(jnp.concatenate([-imag, real], 1))
    result = jnp.dot(
        jnp.concatenate(inputs, 1), jnp.concatenate(factors, 0), preferred_element_type=jnp.float32
    ).astype(jnp.bfloat16)
    first = 0
    for out, count in zip(outs, sizes):
        if len(sizes) == 1:
            out[0] = result
        else:
            @pl.when((step >= first) & (step < first + count))
            def _(out=out):
                out[0] = result
        first += count


def extrapolate_blocks(field, operator, offsets, sets, listed=False, limit=60):
    rows, blocks, _, size = field.shape
    bands = offsets.shape[0]
    width = 2 * size
    chunk = 32
    parts = 4
    sizes = [len(one) for one in sets]
    count = sum(sizes)
    order = jnp.array(sum(sets, []), jnp.int32)
    firsts = [sum(sizes[:n]) for n in range(len(sizes))]
    flat = field.reshape(rows * blocks * 2, size)

    def out_spec(first, count):
        return pl.BlockSpec((1, rows, width), lambda j, o, c: (jnp.clip(j - first, 0, count - 1), 0, 0))

    return pl.pallas_call(
        functools.partial(
            extrapolate_kernel, sets=sets, rows=rows, blocks=blocks, parts=parts, listed=listed
        ),
        grid_spec=pltpu.PrefetchScalarGridSpec(
            num_scalar_prefetch=2,
            grid=(count,),
            in_specs=[pl.BlockSpec(memory_space=pltpu.HBM)] * 2,
            out_specs=[out_spec(*one) for one in zip(firsts, sizes)],
            scratch_shapes=[
                pltpu.VMEM((chunk * (2 * blocks + 1), size), jnp.float32),
                pltpu.VMEM((count * bands if listed else blocks, rows, width), jnp.bfloat16),
                pltpu.VMEM(flat.shape, jnp.bfloat16),
                pltpu.VMEM((count,) + operator.shape[1:], jnp.bfloat16),
                pltpu.SemaphoreType.DMA((parts,)),
                pltpu.SemaphoreType.DMA((count,)),
            ],
        ),
        out_shape=[jax.ShapeDtypeStruct((n, rows, width), jnp.bfloat16) for n in sizes],
        compiler_params=params(limit),
        cost_estimate=SMALL,
        name="extrapolate",
    )(order, offsets, flat, operator)


def product_kernel(near_ids, far_ids, inner, near_in, near_out, far_in, far_out, data, out, turned, total):
    size = data.shape[2]
    tiles = data.shape[0] // 2
    sources = near_in.shape[1] // size
    per_source = tiles // sources

    @pl.when(pl.program_id(0) == 0)
    def _():
        for side in range(2):
            first = (inner[1] ^ side) * tiles
            for tile in range(tiles):
                for part in range(2):
                    turned[side * tiles + tile, :, part * size:(part + 1) * size] = data[first + tile, part].T

    total[...] = jnp.zeros_like(total)
    sides = ((near_in, near_out, near_ids), (far_in, far_out, far_ids))
    for side, (field_in, field_out, ids) in enumerate(sides):
        for source in range(sources):
            lines = slice(source * size, (source + 1) * size)
            upper = jnp.where(inner[0] > 0, field_in[0, lines, :], field_out[0, lines, :])
            lower = jnp.concatenate([-upper[:, size:], upper[:, :size]], 1)
            both = jnp.concatenate([upper, lower], 0)
            first = side * tiles + source * per_source
            left = turned[first:first + per_source].reshape(per_source * size, 2 * size)
            result = jnp.dot(left, both, preferred_element_type=jnp.float32)
            for tile in range(per_source):
                total[ids[source * per_source + tile]] += result[tile * size:(tile + 1) * size]
    for block in range(total.shape[0]):
        out[0, :, block * size:(block + 1) * size] = total[block].T.astype(jnp.bfloat16)


def part_spec(shape, first, begin, count, is_inner):
    def index(j, a, b, inner):
        place = first + j if is_inner else outer_place(first + j)
        place = jnp.clip(place - begin, 0, count - 1)
        return jnp.where((inner[0] > 0) == is_inner, place, 0), 0, 0

    return pl.BlockSpec(shape, index)


def product_blocks(near_in, near_out, far_in, far_out, data, near_ids, far_ids, inner):
    blocks, rows, width = near_in.shape
    tiles, _, size, _ = data.shape
    receivers = NR // size
    shape = (1, rows, width)
    data_spec = pl.BlockSpec(data.shape, lambda j, a, b, i: (0, 0, 0, 0))
    return pl.pallas_call(
        product_kernel,
        grid_spec=pltpu.PrefetchScalarGridSpec(
            num_scalar_prefetch=3,
            grid=(blocks,),
            in_specs=[part_spec(shape, 0, 0, len(INNER), True), part_spec(shape, 0, 0, len(OUTER), False)] * 2
            + [data_spec],
            out_specs=pl.BlockSpec((1, width, NR), lambda j, a, b, i: (j, 0, 0)),
            scratch_shapes=[
                pltpu.VMEM((tiles, size, width), jnp.bfloat16),
                pltpu.VMEM((receivers, size, width), jnp.float32),
            ],
        ),
        out_shape=jax.ShapeDtypeStruct((blocks, width, NR), jnp.bfloat16),
        compiler_params=params(),
        cost_estimate=SMALL,
        name="product",
    )(near_ids, far_ids, inner, near_in, near_out, far_in, far_out, data)


def image_kernel(places, unused, inner, *refs, first, begins, size):
    out = refs[-1]
    slot = first + pl.program_id(0)
    parts = refs[len(begins):]
    both = None
    for n, piece in enumerate(begins):
        field = parts[0][0]
        for part, (begin, is_inner) in zip(parts[1:], piece[1:]):
            chosen = (inner[0] > 0) & (slot >= begin) if is_inner else inner[0] == 0
            field = jnp.where(chosen, part[0], field)
        parts = parts[len(piece):]
        term = jnp.dot(refs[n][0], field, preferred_element_type=jnp.float32)
        both = term if both is None else both + term
    real = both[:size, :size] + both[size:, size:]
    imag = both[size:, :size] - both[:size, size:]
    if len(parts) > 1:
        real += parts[0][0, 0]
        imag += parts[0][0, 1]
    out[0, 0] = real
    out[0, 1] = imag


def image_blocks(product, first, count, pieces, inner, before=None):
    _, rows, width = pieces[0][1][0][0].shape
    size = width // 2
    image_spec = pl.BlockSpec((1, 2, size, size), lambda j, o, u, i: (j, 0, 0, 0))
    specs = [
        pl.BlockSpec((1, width, rows), lambda j, o, u, i, n=n: (first + j, 0, o[n])) for n in range(len(pieces))
    ]
    values = [product] * len(pieces)
    begins = []
    for _, parts in pieces:
        inners = [True] * (len(parts) - 1) + [False]
        for (field, begin), is_inner in zip(parts, inners):
            specs.append(part_spec((1, rows, width), first, begin, field.shape[0], is_inner))
            values.append(field)
        begins.append([(begin, is_inner) for (_, begin), is_inner in zip(parts, inners)])
    if before is not None:
        specs.append(pl.BlockSpec((1, 2, size, size), lambda j, o, u, i: (first + j, 0, 0, 0)))
        values.append(before)
    places = jnp.stack([shot for shot, _ in pieces])
    return pl.pallas_call(
        functools.partial(image_kernel, first=first, begins=begins, size=size),
        grid_spec=pltpu.PrefetchScalarGridSpec(
            num_scalar_prefetch=3, grid=(count,), in_specs=specs, out_specs=image_spec
        ),
        out_shape=jax.ShapeDtypeStruct((count, 2, size, size), jnp.float32),
        compiler_params=params(),
        cost_estimate=SMALL,
        name="image",
    )(places, places, inner, *values)


def following(value, *earlier):
    return lax.optimization_barrier((value,) + earlier)[0]


def hand(value, *pairs):
    return lax.ppermute(value, "shot", pairs)


def send_sum(value, pairs):
    pairs = [(4 * a + b, 4 * c + d) for (a, b), (c, d) in pairs]
    return lax.ppermute(value.astype(jnp.bfloat16), ("shot", "freq"), pairs).astype(jnp.float32)


def sum_images(one, two, shot, freq):
    left = shot < 2
    shots = range(4)
    even = freq % 2 == 0
    low = freq < 2
    last = one[4:]
    one = one[:4]
    keep = jnp.where(even, jnp.concatenate([one, last]), jnp.concatenate([two, last]))
    send = jnp.where(even, jnp.concatenate([two, last]), jnp.concatenate([one, last]))
    image = keep + send_sum(send, [((s, f), (s, f ^ 1)) for s in shots for f in range(4)])
    keep = jnp.where(low, image[:2], image[2:4])
    send = jnp.where(low, image[2:4], image[:2])
    last = image[4] + send_sum(image[4], [((s, 1), (s, 3)) for s in (1, 2)])
    image = keep + send_sum(send, [((s, f), (s, f ^ 2)) for s in shots for f in range(4)])
    keep = jnp.where(left, image[0], image[1])
    send = jnp.where(left, image[1], image[0])
    image = keep + send_sum(send, [((s, f), (3 - s, f)) for s in shots for f in range(4) if (s, f) != (0, 3)])
    last = send_sum(last, [((1, 3), (3, 3))]) + send_sum(last, [((2, 3), (3, 3))])
    return jnp.where((shot == 3) & (freq == 3), last, image)


def split_body(source_field, receiver_field, operator, band_offsets, survey_tiles, survey_data):
    tiles = survey_data.shape[1]
    shot = lax.axis_index("shot")
    freq = lax.axis_index("freq")
    inner = ((shot == 1) | (shot == 2)).astype(jnp.int32)[None]
    offsets = band_offsets.T
    make = functools.partial(extrapolate_blocks, operator=operator[0])
    inward = ((0, 1), (3, 2))
    outward = ((1, 0), (2, 3))
    middle = ((1, 2), (2, 1))
    ends = ((0, 3), (3, 0))
    beyond = ((1, 3), (2, 0))

    data = lax.all_gather(survey_data[0], "shot", axis_index_groups=((0, 1), (2, 3)), tiled=True)
    (r_head,) = make(receiver_field[0], offsets=offsets, sets=[INNER[:HEAD]], listed=True)
    r_1_head = hand(r_head, *inward)
    r_3_head = hand(r_head, *middle)
    r_inner, r_outer = make(receiver_field[0], offsets=following(offsets, r_head), sets=[INNER[HEAD:], OUTER])
    r_3_in = hand(r_inner, *middle)
    r_1_in = hand(r_inner, *inward)
    r_1_out = hand(following(r_outer, r_3_head), *outward)
    s_inner, s_outer = make(
        source_field[0], offsets=following(offsets, r_outer, r_3_head, r_1_head, data), sets=[INNER, OUTER]
    )
    s_out = hand(s_outer, *outward)
    s_in = hand(s_inner, *inward)
    forward_head = hand(following(r_1_head, r_3_in), *middle)
    r_3_out = hand(r_outer, *ends)
    forward = hand(following(r_1_in, r_1_out), *middle)
    beyond_1 = hand(following(r_outer, s_out, forward_head)[:LATE], *beyond)
    beyond_2 = hand(r_outer[LATE:], *beyond)

    ids = survey_tiles[:, 1]
    near_ids = lax.dynamic_slice_in_dim(ids, shot * tiles, tiles)
    far_ids = lax.dynamic_slice_in_dim(ids, (shot ^ 1) * tiles, tiles)
    product = product_blocks(
        s_inner, s_outer, s_in, s_out, data, near_ids, far_ids, jnp.concatenate([inner, shot[None] % 2])
    )
    early = [
        (shot, [(r_head, 0), (r_inner, HEAD), (r_outer, 0)]),
        (shot ^ 1, [(r_1_head, 0), (r_1_in, HEAD), (r_1_out, 0)]),
        (shot ^ 3, [(r_3_head, 0), (r_3_in, HEAD), (r_3_out, 0)]),
    ]
    forwarded = [(forward_head, 0), (forward, HEAD)]
    image = image_blocks(product, 0, len(INNER), early, inner)
    most = image_blocks(product, 0, LATE + 1, [(shot ^ 2, forwarded + [(beyond_1, 0)])], inner, image)
    rest = image_blocks(
        product, LATE + 1, len(INNER) - LATE - 1, [(shot ^ 2, forwarded + [(beyond_2, LATE)])], inner,
        following(image, most),
    )
    one = most[:FIRST]
    two = jnp.concatenate([most[FIRST:], rest])
    image = sum_images(one, two, shot, freq)
    total_freqs = source_field.shape[0] * lax.axis_size("freq")
    return image * (1.0 / math.sqrt(2.0 * NR * total_freqs))


def body(source_field, *rest):
    fits = (
        lax.axis_size("shot") == 4
        and lax.axis_size("freq") == 4
        and source_field.shape[1:] == (512, 16, 2, 128)
    )
    return (split_body if fits else general_body)(source_field, *rest)


def solution(mesh):
    return jax.shard_map(
        body,
        mesh=mesh,
        in_specs=(
            P("freq", ("groups", "shot"), None, None, None),
            P("freq", ("groups", "shot"), None, None, None),
            P("freq", "groups", None, None, None, None),
            P("groups", None),
            P("groups", None),
            P("freq", ("groups", "shot"), None, None, None),
        ),
        out_specs=P(None, ("groups", "shot", "freq"), None),
        check_vma=False,
    )
```

```python
import functools
import math

import jax
import jax.numpy as jnp
from jax import lax
from jax.experimental import pallas as pl
from jax.experimental.pallas import tpu as pltpu
from jax.sharding import PartitionSpec as P

NR = 2048
SMALL = pl.CostEstimate(flops=1000, bytes_accessed=1000, transcendentals=0)


def extrapolate(wavefield, operator, columns):
    row_count, blocks_x, components, block_size = wavefield.shape
    bands = columns.shape[1]
    real_part = operator[:, :, 0]
    imag_part = operator[:, :, 1]
    upper_rows = jnp.concatenate([real_part, imag_part], -1)
    lower_rows = jnp.concatenate([-imag_part, real_part], -1)
    real_block = jnp.concatenate([upper_rows, lower_rows], -2)
    real_block = real_block.reshape(blocks_x, bands, 2 * block_size, 2, block_size)
    chosen = jnp.take(wavefield, columns, axis=1).reshape(
        row_count, blocks_x, bands, 2 * block_size
    )
    result = jnp.einsum("sikc,ikcoy->soiy", chosen, real_block, preferred_element_type=jnp.float32)
    return result.astype(jnp.bfloat16)


def to_owners(wavefield, shot_count, own_cells):
    row_count = wavefield.shape[0]
    return wavefield.reshape(row_count, 2, shot_count, own_cells)


def to_tiles(wavefield, shot_count, own_cells):
    row_count, components, blocks_x, block_size = wavefield.shape
    if own_cells >= block_size:
        return to_owners(wavefield, shot_count, own_cells)
    factor = block_size // own_cells
    copies = jnp.broadcast_to(
        wavefield[:, :, :, None, :], (row_count, components, blocks_x, factor, block_size)
    )
    return copies.reshape(row_count, components, shot_count, block_size)


def data_product(source_cells, data_shard, survey_tiles, block_size, own_cells):
    source_count = source_cells.shape[0]
    receiver_blocks = NR // block_size
    blocks = source_cells.reshape(source_count // block_size, block_size, 2 * own_cells)
    block_ids = jnp.arange(receiver_blocks, dtype=jnp.int32)
    chosen = jnp.take(blocks, survey_tiles[:, 0], axis=0)
    products = jnp.einsum(
        "ncsr,nsk->ncrk",
        lax.all_gather(data_shard, "shot", axis=0, tiled=True),
        chosen,
        preferred_element_type=jnp.float32,
    )
    real_part = products[:, 0, :, :own_cells] - products[:, 1, :, own_cells:]
    imag_part = products[:, 0, :, own_cells:] + products[:, 1, :, :own_cells]
    contribution = jnp.concatenate([real_part, imag_part], -1)
    onehot = (survey_tiles[:, 1][:, None] == block_ids[None, :]).astype(jnp.float32)
    summed = jnp.einsum("nq,nrk->qrk", onehot, contribution, precision=lax.Precision.HIGHEST)
    return summed.reshape(NR, 2, own_cells).astype(jnp.bfloat16)


def image_tile(product, receiver_tile, block_size):
    row_count, components, own_cells = product.shape
    tiles_here = max(own_cells // block_size, 1)
    inner_cells = own_cells // tiles_here
    left = product.reshape(row_count, 2, tiles_here, inner_cells)
    right = receiver_tile.reshape(row_count, 2, tiles_here, block_size)
    turned = jnp.stack([-right[:, 1], right[:, 0]], 1)
    both = jnp.stack([right, turned], 1)
    result = jnp.einsum("rctx,rocty->otxy", left, both, preferred_element_type=jnp.float32)
    return result.reshape(2, own_cells, block_size)


def general_body(source_field, receiver_field, operator, band_offsets, survey_tiles, survey_data):
    shot_count = lax.axis_size("shot")
    freq_local = source_field.shape[0]
    blocks_x = source_field.shape[2]
    block_size = source_field.shape[4]
    own_cells = blocks_x * block_size // shot_count
    block_rows = jnp.arange(blocks_x, dtype=jnp.int32)[:, None]
    columns = (block_rows + band_offsets) % blocks_x
    source_next = extrapolate(source_field[0], operator[0], columns)
    receiver_next = extrapolate(receiver_field[0], operator[0], columns)
    source_send = to_owners(source_next, shot_count, own_cells)
    receiver_send = to_tiles(receiver_next, shot_count, own_cells)
    source_cells = lax.all_to_all(source_send, "shot", split_axis=2, concat_axis=0, tiled=True)
    receiver_tile = lax.all_to_all(receiver_send, "shot", split_axis=2, concat_axis=0, tiled=True)
    source_cells = source_cells.reshape(source_cells.shape[0], 2 * own_cells)
    product = data_product(source_cells, survey_data[0], survey_tiles, block_size, own_cells)
    receiver_tile = receiver_tile.reshape(receiver_tile.shape[0], 2, -1)
    image_sum = image_tile(product, receiver_tile, block_size)
    total_freqs = freq_local * lax.axis_size("freq")
    scaled = image_sum * (1.0 / math.sqrt(2.0 * NR * total_freqs))
    return lax.psum_scatter(scaled, "freq", scatter_dimension=1, tiled=True)


INNER = [4, 8, 6, 10, 15, 5, 9, 7, 11]
HEAD = 3
OUTER = [0, 12, 2, 14, 1, 13, 3]
FIRST = 5
OUTER_FIRST = 4
LATE = 5


def outer_place(slot):
    return jnp.where(slot < FIRST, jnp.minimum(slot, OUTER_FIRST - 1), jnp.minimum(slot - 1, len(OUTER) - 1))


def params(limit=24):
    return pltpu.CompilerParams(vmem_limit_bytes=limit * 1024 * 1024)


def extrapolate_kernel(order, offsets, inner, field, operator, *refs, sets, rows, blocks, parts, listed, swap):
    stage, apart, lines, weights, field_sems, weight_sems = refs[-6:]
    outs = refs[:-6]
    sizes = [len(one) for one in sets]
    step = pl.program_id(0)
    bands = operator.shape[1]
    pitch = 2 * blocks + 1
    chunk = stage.shape[0] // pitch
    part_lines = lines.shape[0] // parts

    def column(block, band):
        return lax.rem(block + offsets[band, block] + blocks, blocks)

    def field_copy(part):
        here = pl.ds(part * part_lines, part_lines)
        return pltpu.make_async_copy(field.at[here], lines.at[here], field_sems.at[part])

    def weight_copy(n, block):
        return pltpu.make_async_copy(operator.at[block], weights.at[n], weight_sems.at[n])

    @pl.when(step == 0)
    def _():
        for part in range(parts):
            field_copy(part).start()
        for n, block in enumerate(sum(sets, [])):
            weight_copy(n, block).start()
        if listed:
            wanted = [column(block, band) for block in sum(sets, []) for band in range(bands)]
        else:
            wanted = list(range(blocks))

        def split(n, carry):
            for row in range(chunk):
                here = pl.ds(pl.multiple_of((n * chunk + row) * 2 * blocks, 2 * blocks), 2 * blocks)
                stage[pl.ds(row * pitch, 2 * blocks), :] = lines[here, :].astype(jnp.float32)
            to = pl.ds(pl.multiple_of(n * chunk, chunk), chunk)
            for slot, block in enumerate(wanted):
                for half in range(2):
                    picked = stage[pl.ds(2 * block + half, chunk, stride=pitch), :]
                    apart[slot, to, half * 128:(half + 1) * 128] = picked.astype(jnp.bfloat16)
            return carry

        steps = rows // chunk // parts
        for part in range(parts):
            field_copy(part).wait()
            lax.fori_loop(part * steps, (part + 1) * steps, split, 0)

    block = order[step]
    weight_copy(step, block).wait()
    inputs = []
    factors = []
    for band in range(bands):
        inputs.append(apart[step * bands + band if listed else column(block, band)])
        real = weights[step, band, 0]
        imag = weights[step, band, 1]
        factors.append(jnp.concatenate([real, imag], 1))
        factors.append(jnp.concatenate([-imag, real], 1))
    result = jnp.dot(
        jnp.concatenate(inputs, 1), jnp.concatenate(factors, 0), preferred_element_type=jnp.float32
    ).astype(jnp.bfloat16)
    first = 0
    for out, count in zip(outs, sizes):
        if len(sizes) == 1:
            out[0] = result
        else:
            @pl.when((step >= first) & (step < first + count))
            def _(out=out):
                out[0] = result
        first += count
    if swap:
        @pl.when(jnp.where(inner[0] > 0, step >= sizes[0], step < sizes[1]))
        def _():
            outs[-1][0] = result


def extrapolate_blocks(field, operator, offsets, inner, sets, listed=False, swap=False, limit=60):
    rows, blocks, _, size = field.shape
    bands = offsets.shape[0]
    width = 2 * size
    chunk = 32
    parts = 4
    sizes = [len(one) for one in sets]
    count = sum(sizes)
    order = jnp.array(sum(sets, []), jnp.int32)
    firsts = [sum(sizes[:n]) for n in range(len(sizes))]
    flat = field.reshape(rows * blocks * 2, size)

    def out_spec(first, count):
        return pl.BlockSpec((1, rows, width), lambda j, o, c, i: (jnp.clip(j - first, 0, count - 1), 0, 0))

    def swap_place(j, o, c, i):
        return jnp.clip(j - jnp.where(i[0] > 0, sizes[0], 0), 0, sizes[1] - 1), 0, 0

    out_specs = [out_spec(*one) for one in zip(firsts, sizes)]
    if swap:
        out_specs.append(pl.BlockSpec((1, rows, width), swap_place))
    return pl.pallas_call(
        functools.partial(
            extrapolate_kernel, sets=sets, rows=rows, blocks=blocks, parts=parts, listed=listed, swap=swap
        ),
        grid_spec=pltpu.PrefetchScalarGridSpec(
            num_scalar_prefetch=3,
            grid=(count,),
            in_specs=[pl.BlockSpec(memory_space=pltpu.HBM)] * 2,
            out_specs=out_specs,
            scratch_shapes=[
                pltpu.VMEM((chunk * (2 * blocks + 1), size), jnp.float32),
                pltpu.VMEM((count * bands if listed else blocks, rows, width), jnp.bfloat16),
                pltpu.VMEM(flat.shape, jnp.bfloat16),
                pltpu.VMEM((count,) + operator.shape[1:], jnp.bfloat16),
                pltpu.SemaphoreType.DMA((parts,)),
                pltpu.SemaphoreType.DMA((count,)),
            ],
        ),
        out_shape=[jax.ShapeDtypeStruct((n, rows, width), jnp.bfloat16) for n in sizes + sizes[1:] * swap],
        compiler_params=params(limit),
        cost_estimate=SMALL,
        name="extrapolate",
    )(order, offsets, inner, flat, operator)


def product_kernel(near_ids, far_ids, inner, near_in, near_out, far_in, far_out, near_data, far_data, out, turned, total):
    size = near_data.shape[2]
    tiles = near_data.shape[0]
    sources = near_in.shape[1] // size
    per_source = tiles // sources

    @pl.when(pl.program_id(0) == 0)
    def _():
        for side, data in enumerate((near_data, far_data)):
            for tile in range(tiles):
                for part in range(2):
                    turned[side * tiles + tile, :, part * size:(part + 1) * size] = data[tile, part].T

    total[...] = jnp.zeros_like(total)
    sides = ((near_in, near_out, near_ids), (far_in, far_out, far_ids))
    for side, (field_in, field_out, ids) in enumerate(sides):
        for source in range(sources):
            lines = slice(source * size, (source + 1) * size)
            upper = jnp.where(inner[0] > 0, field_in[0, lines, :], field_out[0, lines, :])
            lower = jnp.concatenate([-upper[:, size:], upper[:, :size]], 1)
            both = jnp.concatenate([upper, lower], 0)
            first = side * tiles + source * per_source
            left = turned[first:first + per_source].reshape(per_source * size, 2 * size)
            result = jnp.dot(left, both, preferred_element_type=jnp.float32)
            for tile in range(per_source):
                total[ids[source * per_source + tile]] += result[tile * size:(tile + 1) * size]
    for block in range(total.shape[0]):
        out[0, :, block * size:(block + 1) * size] = total[block].T.astype(jnp.bfloat16)


def part_spec(shape, first, begin, count, is_inner):
    def index(j, a, b, inner):
        place = first + j if is_inner else outer_place(first + j)
        place = jnp.clip(place - begin, 0, count - 1)
        return jnp.where((inner[0] > 0) == is_inner, place, 0), 0, 0

    return pl.BlockSpec(shape, index)


def product_blocks(near_in, near_out, far_in, far_out, near_data, far_data, near_ids, far_ids, inner):
    blocks, rows, width = near_in.shape
    tiles, _, size, _ = near_data.shape
    receivers = NR // size
    shape = (1, rows, width)
    data_spec = pl.BlockSpec(near_data.shape, lambda j, a, b, i: (0, 0, 0, 0))
    return pl.pallas_call(
        product_kernel,
        grid_spec=pltpu.PrefetchScalarGridSpec(
            num_scalar_prefetch=3,
            grid=(blocks,),
            in_specs=[part_spec(shape, 0, 0, len(INNER), True), part_spec(shape, 0, 0, len(OUTER), False)] * 2
            + [data_spec, data_spec],
            out_specs=pl.BlockSpec((1, width, NR), lambda j, a, b, i: (j, 0, 0)),
            scratch_shapes=[
                pltpu.VMEM((2 * tiles, size, width), jnp.bfloat16),
                pltpu.VMEM((receivers, size, width), jnp.float32),
            ],
        ),
        out_shape=jax.ShapeDtypeStruct((blocks, width, NR), jnp.bfloat16),
        compiler_params=params(),
        cost_estimate=SMALL,
        name="product",
    )(near_ids, far_ids, inner, near_in, near_out, far_in, far_out, near_data, far_data)


def image_kernel(places, unused, inner, *refs, first, begins, size):
    out = refs[-1]
    slot = first + pl.program_id(0)
    parts = refs[len(begins):]
    both = None
    for n, piece in enumerate(begins):
        field = parts[0][0]
        for part, (begin, is_inner) in zip(parts[1:], piece[1:]):
            chosen = (inner[0] > 0) & (slot >= begin) if is_inner else inner[0] == 0
            field = jnp.where(chosen, part[0], field)
        parts = parts[len(piece):]
        term = jnp.dot(refs[n][0], field, preferred_element_type=jnp.float32)
        both = term if both is None else both + term
    real = both[:size, :size] + both[size:, size:]
    imag = both[size:, :size] - both[:size, size:]
    if len(parts) > 1:
        real += parts[0][0, 0]
        imag += parts[0][0, 1]
    out[0, 0] = real
    out[0, 1] = imag


def image_blocks(product, first, count, pieces, inner, before=None):
    _, rows, width = pieces[0][1][0][0].shape
    size = width // 2
    image_spec = pl.BlockSpec((1, 2, size, size), lambda j, o, u, i: (j, 0, 0, 0))
    specs = [
        pl.BlockSpec((1, width, rows), lambda j, o, u, i, n=n: (first + j, 0, o[n])) for n in range(len(pieces))
    ]
    values = [product] * len(pieces)
    begins = []
    for _, parts in pieces:
        inners = [True] * (len(parts) - 1) + [False]
        for (field, begin), is_inner in zip(parts, inners):
            specs.append(part_spec((1, rows, width), first, begin, field.shape[0], is_inner))
            values.append(field)
        begins.append([(begin, is_inner) for (_, begin), is_inner in zip(parts, inners)])
    if before is not None:
        specs.append(pl.BlockSpec((1, 2, size, size), lambda j, o, u, i: (first + j, 0, 0, 0)))
        values.append(before)
    places = jnp.stack([shot for shot, _ in pieces])
    return pl.pallas_call(
        functools.partial(image_kernel, first=first, begins=begins, size=size),
        grid_spec=pltpu.PrefetchScalarGridSpec(
            num_scalar_prefetch=3, grid=(count,), in_specs=specs, out_specs=image_spec
        ),
        out_shape=jax.ShapeDtypeStruct((count, 2, size, size), jnp.float32),
        compiler_params=params(),
        cost_estimate=SMALL,
        name="image",
    )(places, places, inner, *values)


def following(value, *earlier):
    return lax.optimization_barrier((value,) + earlier)[0]


def hand(value, *pairs):
    return lax.ppermute(value, "shot", pairs)


def send_sum(value, pairs):
    pairs = [(4 * a + b, 4 * c + d) for (a, b), (c, d) in pairs]
    return lax.ppermute(value.astype(jnp.bfloat16), ("shot", "freq"), pairs).astype(jnp.float32)


def sum_images(one, two, shot, freq):
    left = shot < 2
    shots = range(4)
    even = freq % 2 == 0
    low = freq < 2
    last = one[4:]
    one = one[:4]
    keep = jnp.where(even, jnp.concatenate([one, last]), jnp.concatenate([two, last]))
    send = jnp.where(even, jnp.concatenate([two, last]), jnp.concatenate([one, last]))
    image = keep + send_sum(send, [((s, f), (s, f ^ 1)) for s in shots for f in range(4)])
    keep = jnp.where(low, image[:2], image[2:4])
    send = jnp.where(low, image[2:4], image[:2])
    last = image[4] + send_sum(image[4], [((s, 1), (s, 3)) for s in (1, 2)])
    image = keep + send_sum(send, [((s, f), (s, f ^ 2)) for s in shots for f in range(4)])
    keep = jnp.where(left, image[0], image[1])
    send = jnp.where(left, image[1], image[0])
    image = keep + send_sum(send, [((s, f), (3 - s, f)) for s in shots for f in range(4) if (s, f) != (0, 3)])
    last = send_sum(last, [((1, 3), (3, 3))]) + send_sum(last, [((2, 3), (3, 3))])
    return jnp.where((shot == 3) & (freq == 3), last, image)


def split_body(source_field, receiver_field, operator, band_offsets, survey_tiles, survey_data):
    tiles = survey_data.shape[1]
    shot = lax.axis_index("shot")
    freq = lax.axis_index("freq")
    inner = ((shot == 1) | (shot == 2)).astype(jnp.int32)[None]
    offsets = band_offsets.T
    make = functools.partial(extrapolate_blocks, operator=operator[0], inner=inner)
    inward = ((0, 1), (3, 2))
    outward = ((1, 0), (2, 3))
    middle = ((1, 2), (2, 1))
    ends = ((0, 3), (3, 0))
    beyond = ((1, 3), (2, 0))

    far_data = hand(survey_data[0], *inward, *outward)
    (r_head,) = make(receiver_field[0], offsets=offsets, sets=[INNER[:HEAD]], listed=True)
    r_1_head = hand(r_head, *inward)
    r_3_head = hand(r_head, *middle)
    r_inner, r_outer, r_swap = make(
        receiver_field[0], offsets=following(offsets, r_head), sets=[INNER[HEAD:], OUTER], swap=True
    )
    r_3_in = hand(r_inner, *middle)
    r_1 = hand(following(r_swap, far_data, r_3_head), *inward, *outward)
    s_inner, s_outer = make(
        source_field[0], offsets=following(offsets, r_outer, r_3_head, r_1_head), sets=[INNER, OUTER]
    )
    s_out = hand(s_outer, *outward)
    s_in = hand(s_inner, *inward)
    forward_head = hand(r_1_head, *middle)
    r_3_out = hand(following(r_outer, r_3_in), *ends)
    forward = hand(r_1[:len(INNER) - HEAD], *middle)
    beyond_1 = hand(following(r_outer, s_out, forward_head)[:LATE], *beyond)
    beyond_2 = hand(r_outer[LATE:], *beyond)

    ids = survey_tiles[:, 1]
    near_ids = lax.dynamic_slice_in_dim(ids, shot * tiles, tiles)
    far_ids = lax.dynamic_slice_in_dim(ids, (shot ^ 1) * tiles, tiles)
    product = product_blocks(
        s_inner, s_outer, s_in, s_out, survey_data[0], far_data, near_ids, far_ids, inner
    )
    early = [
        (shot, [(r_head, 0), (r_inner, HEAD), (r_outer, 0)]),
        (shot ^ 1, [(r_1_head, 0), (r_1, HEAD), (r_1, 0)]),
        (shot ^ 3, [(r_3_head, 0), (r_3_in, HEAD), (r_3_out, 0)]),
    ]
    forwarded = [(forward_head, 0), (forward, HEAD)]
    image = image_blocks(product, 0, len(INNER), early, inner)
    most = image_blocks(product, 0, LATE + 1, [(shot ^ 2, forwarded + [(beyond_1, 0)])], inner, image)
    rest = image_blocks(
        product, LATE + 1, len(INNER) - LATE - 1, [(shot ^ 2, forwarded + [(beyond_2, LATE)])], inner,
        following(image, most),
    )
    one = most[:FIRST]
    two = jnp.concatenate([most[FIRST:], rest])
    image = sum_images(one, two, shot, freq)
    total_freqs = source_field.shape[0] * lax.axis_size("freq")
    return image * (1.0 / math.sqrt(2.0 * NR * total_freqs))


def body(source_field, *rest):
    fits = (
        lax.axis_size("shot") == 4
        and lax.axis_size("freq") == 4
        and source_field.shape[1:] == (512, 16, 2, 128)
    )
    return (split_body if fits else general_body)(source_field, *rest)


def solution(mesh):
    return jax.shard_map(
        body,
        mesh=mesh,
        in_specs=(
            P("freq", ("groups", "shot"), None, None, None),
            P("freq", ("groups", "shot"), None, None, None),
            P("freq", "groups", None, None, None, None),
            P("groups", None),
            P("groups", None),
            P("freq", ("groups", "shot"), None, None, None),
        ),
        out_specs=P(None, ("groups", "shot", "freq"), None),
        check_vma=False,
    )
```

```python
import functools
import math

import jax
import jax.numpy as jnp
from jax import lax
from jax.experimental import pallas as pl
from jax.experimental.pallas import tpu as pltpu
from jax.sharding import PartitionSpec as P

NR = 2048
SMALL = pl.CostEstimate(flops=1000, bytes_accessed=1000, transcendentals=0)


def extrapolate(wavefield, operator, columns):
    row_count, blocks_x, components, block_size = wavefield.shape
    bands = columns.shape[1]
    real_part = operator[:, :, 0]
    imag_part = operator[:, :, 1]
    upper_rows = jnp.concatenate([real_part, imag_part], -1)
    lower_rows = jnp.concatenate([-imag_part, real_part], -1)
    real_block = jnp.concatenate([upper_rows, lower_rows], -2)
    real_block = real_block.reshape(blocks_x, bands, 2 * block_size, 2, block_size)
    chosen = jnp.take(wavefield, columns, axis=1).reshape(
        row_count, blocks_x, bands, 2 * block_size
    )
    result = jnp.einsum("sikc,ikcoy->soiy", chosen, real_block, preferred_element_type=jnp.float32)
    return result.astype(jnp.bfloat16)


def to_owners(wavefield, shot_count, own_cells):
    row_count = wavefield.shape[0]
    return wavefield.reshape(row_count, 2, shot_count, own_cells)


def to_tiles(wavefield, shot_count, own_cells):
    row_count, components, blocks_x, block_size = wavefield.shape
    if own_cells >= block_size:
        return to_owners(wavefield, shot_count, own_cells)
    factor = block_size // own_cells
    copies = jnp.broadcast_to(
        wavefield[:, :, :, None, :], (row_count, components, blocks_x, factor, block_size)
    )
    return copies.reshape(row_count, components, shot_count, block_size)


def data_product(source_cells, data_shard, survey_tiles, block_size, own_cells):
    source_count = source_cells.shape[0]
    receiver_blocks = NR // block_size
    blocks = source_cells.reshape(source_count // block_size, block_size, 2 * own_cells)
    block_ids = jnp.arange(receiver_blocks, dtype=jnp.int32)
    chosen = jnp.take(blocks, survey_tiles[:, 0], axis=0)
    products = jnp.einsum(
        "ncsr,nsk->ncrk",
        lax.all_gather(data_shard, "shot", axis=0, tiled=True),
        chosen,
        preferred_element_type=jnp.float32,
    )
    real_part = products[:, 0, :, :own_cells] - products[:, 1, :, own_cells:]
    imag_part = products[:, 0, :, own_cells:] + products[:, 1, :, :own_cells]
    contribution = jnp.concatenate([real_part, imag_part], -1)
    onehot = (survey_tiles[:, 1][:, None] == block_ids[None, :]).astype(jnp.float32)
    summed = jnp.einsum("nq,nrk->qrk", onehot, contribution, precision=lax.Precision.HIGHEST)
    return summed.reshape(NR, 2, own_cells).astype(jnp.bfloat16)


def image_tile(product, receiver_tile, block_size):
    row_count, components, own_cells = product.shape
    tiles_here = max(own_cells // block_size, 1)
    inner_cells = own_cells // tiles_here
    left = product.reshape(row_count, 2, tiles_here, inner_cells)
    right = receiver_tile.reshape(row_count, 2, tiles_here, block_size)
    turned = jnp.stack([-right[:, 1], right[:, 0]], 1)
    both = jnp.stack([right, turned], 1)
    result = jnp.einsum("rctx,rocty->otxy", left, both, preferred_element_type=jnp.float32)
    return result.reshape(2, own_cells, block_size)


def general_body(source_field, receiver_field, operator, band_offsets, survey_tiles, survey_data):
    shot_count = lax.axis_size("shot")
    freq_local = source_field.shape[0]
    blocks_x = source_field.shape[2]
    block_size = source_field.shape[4]
    own_cells = blocks_x * block_size // shot_count
    block_rows = jnp.arange(blocks_x, dtype=jnp.int32)[:, None]
    columns = (block_rows + band_offsets) % blocks_x
    source_next = extrapolate(source_field[0], operator[0], columns)
    receiver_next = extrapolate(receiver_field[0], operator[0], columns)
    source_send = to_owners(source_next, shot_count, own_cells)
    receiver_send = to_tiles(receiver_next, shot_count, own_cells)
    source_cells = lax.all_to_all(source_send, "shot", split_axis=2, concat_axis=0, tiled=True)
    receiver_tile = lax.all_to_all(receiver_send, "shot", split_axis=2, concat_axis=0, tiled=True)
    source_cells = source_cells.reshape(source_cells.shape[0], 2 * own_cells)
    product = data_product(source_cells, survey_data[0], survey_tiles, block_size, own_cells)
    receiver_tile = receiver_tile.reshape(receiver_tile.shape[0], 2, -1)
    image_sum = image_tile(product, receiver_tile, block_size)
    total_freqs = freq_local * lax.axis_size("freq")
    scaled = image_sum * (1.0 / math.sqrt(2.0 * NR * total_freqs))
    return lax.psum_scatter(scaled, "freq", scatter_dimension=1, tiled=True)


INNER = [4, 8, 6, 10, 15, 5, 9, 7, 11]
HEAD = 3
OUTER = [0, 12, 2, 14, 1, 13, 3]
FIRST = 5
OUTER_FIRST = 4
LATE = 5
SWAP = len(INNER) - HEAD


def outer_place(slot):
    return jnp.where(slot < FIRST, jnp.minimum(slot, OUTER_FIRST - 1), jnp.minimum(slot - 1, len(OUTER) - 1))


def params(limit=24):
    return pltpu.CompilerParams(vmem_limit_bytes=limit * 1024 * 1024)


def extrapolate_kernel(order, offsets, inner, field, operator, *refs, sets, rows, blocks, parts, listed, swap):
    stage, apart, lines, weights, field_sems, weight_sems = refs[-6:]
    outs = refs[:-6]
    sizes = [len(one) for one in sets]
    step = pl.program_id(0)
    bands = operator.shape[1]
    pitch = 2 * blocks + 1
    chunk = stage.shape[0] // pitch
    part_lines = lines.shape[0] // parts

    def column(block, band):
        return lax.rem(block + offsets[band, block] + blocks, blocks)

    def field_copy(part):
        here = pl.ds(part * part_lines, part_lines)
        return pltpu.make_async_copy(field.at[here], lines.at[here], field_sems.at[part])

    def weight_copy(n, block):
        return pltpu.make_async_copy(operator.at[block], weights.at[n], weight_sems.at[n])

    @pl.when(step == 0)
    def _():
        for part in range(parts):
            field_copy(part).start()
        for n, block in enumerate(sum(sets, [])):
            weight_copy(n, block).start()
        if listed:
            wanted = [column(block, band) for block in sum(sets, []) for band in range(bands)]
        else:
            wanted = list(range(blocks))

        def split(n, carry):
            for row in range(chunk):
                here = pl.ds(pl.multiple_of((n * chunk + row) * 2 * blocks, 2 * blocks), 2 * blocks)
                stage[pl.ds(row * pitch, 2 * blocks), :] = lines[here, :].astype(jnp.float32)
            to = pl.ds(pl.multiple_of(n * chunk, chunk), chunk)
            for slot, block in enumerate(wanted):
                for half in range(2):
                    picked = stage[pl.ds(2 * block + half, chunk, stride=pitch), :]
                    apart[slot, to, half * 128:(half + 1) * 128] = picked.astype(jnp.bfloat16)
            return carry

        steps = rows // chunk // parts
        for part in range(parts):
            field_copy(part).wait()
            lax.fori_loop(part * steps, (part + 1) * steps, split, 0)

    block = order[step]
    weight_copy(step, block).wait()
    inputs = []
    factors = []
    for band in range(bands):
        inputs.append(apart[step * bands + band if listed else column(block, band)])
        real = weights[step, band, 0]
        imag = weights[step, band, 1]
        factors.append(jnp.concatenate([real, imag], 1))
        factors.append(jnp.concatenate([-imag, real], 1))
    result = jnp.dot(
        jnp.concatenate(inputs, 1), jnp.concatenate(factors, 0), preferred_element_type=jnp.float32
    ).astype(jnp.bfloat16)
    first = 0
    for out, count in zip(outs, sizes):
        if len(sizes) == 1:
            out[0] = result
        else:
            @pl.when((step >= first) & (step < first + count))
            def _(out=out):
                out[0] = result
        first += count
    if swap:
        @pl.when(jnp.where(inner[0] > 0, (step >= sizes[0]) & (step < 2 * sizes[0]), step < sizes[0]))
        def _():
            outs[-1][0] = result


def extrapolate_blocks(field, operator, offsets, inner, sets, listed=False, swap=False, limit=60):
    rows, blocks, _, size = field.shape
    bands = offsets.shape[0]
    width = 2 * size
    chunk = 32
    parts = 4
    sizes = [len(one) for one in sets]
    count = sum(sizes)
    order = jnp.array(sum(sets, []), jnp.int32)
    firsts = [sum(sizes[:n]) for n in range(len(sizes))]
    flat = field.reshape(rows * blocks * 2, size)

    def out_spec(first, count):
        return pl.BlockSpec((1, rows, width), lambda j, o, c, i: (jnp.clip(j - first, 0, count - 1), 0, 0))

    def swap_place(j, o, c, i):
        return jnp.clip(j - jnp.where(i[0] > 0, sizes[0], 0), 0, sizes[0] - 1), 0, 0

    out_specs = [out_spec(*one) for one in zip(firsts, sizes)]
    if swap:
        out_specs.append(pl.BlockSpec((1, rows, width), swap_place))
    return pl.pallas_call(
        functools.partial(
            extrapolate_kernel, sets=sets, rows=rows, blocks=blocks, parts=parts, listed=listed, swap=swap
        ),
        grid_spec=pltpu.PrefetchScalarGridSpec(
            num_scalar_prefetch=3,
            grid=(count,),
            in_specs=[pl.BlockSpec(memory_space=pltpu.HBM)] * 2,
            out_specs=out_specs,
            scratch_shapes=[
                pltpu.VMEM((chunk * (2 * blocks + 1), size), jnp.float32),
                pltpu.VMEM((count * bands if listed else blocks, rows, width), jnp.bfloat16),
                pltpu.VMEM(flat.shape, jnp.bfloat16),
                pltpu.VMEM((count,) + operator.shape[1:], jnp.bfloat16),
                pltpu.SemaphoreType.DMA((parts,)),
                pltpu.SemaphoreType.DMA((count,)),
            ],
        ),
        out_shape=[jax.ShapeDtypeStruct((n, rows, width), jnp.bfloat16) for n in sizes + sizes[:1] * swap],
        compiler_params=params(limit),
        cost_estimate=SMALL,
        name="extrapolate",
    )(order, offsets, inner, flat, operator)


def product_kernel(near_ids, far_ids, inner, near_in, near_out, far_in, far_out, near_data, far_data, out, turned, total):
    size = near_data.shape[2]
    tiles = near_data.shape[0]
    sources = near_in.shape[1] // size
    per_source = tiles // sources

    @pl.when(pl.program_id(0) == 0)
    def _():
        for side, data in enumerate((near_data, far_data)):
            for tile in range(tiles):
                for part in range(2):
                    turned[side * tiles + tile, :, part * size:(part + 1) * size] = data[tile, part].T

    total[...] = jnp.zeros_like(total)
    sides = ((near_in, near_out, near_ids), (far_in, far_out, far_ids))
    for side, (field_in, field_out, ids) in enumerate(sides):
        for source in range(sources):
            lines = slice(source * size, (source + 1) * size)
            upper = jnp.where(inner[0] > 0, field_in[0, lines, :], field_out[0, lines, :])
            lower = jnp.concatenate([-upper[:, size:], upper[:, :size]], 1)
            both = jnp.concatenate([upper, lower], 0)
            first = side * tiles + source * per_source
            left = turned[first:first + per_source].reshape(per_source * size, 2 * size)
            result = jnp.dot(left, both, preferred_element_type=jnp.float32)
            for tile in range(per_source):
                total[ids[source * per_source + tile]] += result[tile * size:(tile + 1) * size]
    for block in range(total.shape[0]):
        out[0, :, block * size:(block + 1) * size] = total[block].T.astype(jnp.bfloat16)


def part_spec(shape, first, begin, count, is_inner):
    def index(j, a, b, inner):
        place = first + j if is_inner else outer_place(first + j)
        place = jnp.clip(place - begin, 0, count - 1)
        return jnp.where((inner[0] > 0) == is_inner, place, 0), 0, 0

    return pl.BlockSpec(shape, index)


def product_blocks(near_in, near_out, far_in, far_out, near_data, far_data, near_ids, far_ids, inner):
    blocks, rows, width = near_in.shape
    tiles, _, size, _ = near_data.shape
    receivers = NR // size
    shape = (1, rows, width)
    data_spec = pl.BlockSpec(near_data.shape, lambda j, a, b, i: (0, 0, 0, 0))
    return pl.pallas_call(
        product_kernel,
        grid_spec=pltpu.PrefetchScalarGridSpec(
            num_scalar_prefetch=3,
            grid=(blocks,),
            in_specs=[part_spec(shape, 0, 0, len(INNER), True), part_spec(shape, 0, 0, len(OUTER), False)] * 2
            + [data_spec, data_spec],
            out_specs=pl.BlockSpec((1, width, NR), lambda j, a, b, i: (j, 0, 0)),
            scratch_shapes=[
                pltpu.VMEM((2 * tiles, size, width), jnp.bfloat16),
                pltpu.VMEM((receivers, size, width), jnp.float32),
            ],
        ),
        out_shape=jax.ShapeDtypeStruct((blocks, width, NR), jnp.bfloat16),
        compiler_params=params(),
        cost_estimate=SMALL,
        name="product",
    )(near_ids, far_ids, inner, near_in, near_out, far_in, far_out, near_data, far_data)


def image_kernel(places, unused, inner, *refs, first, begins, size):
    out = refs[-1]
    slot = first + pl.program_id(0)
    parts = refs[len(begins):]
    both = None
    for n, piece in enumerate(begins):
        field = parts[0][0]
        for part, (begin, is_inner) in zip(parts[1:], piece[1:]):
            place = slot if is_inner else outer_place(slot)
            field = jnp.where(((inner[0] > 0) == is_inner) & (place >= begin), part[0], field)
        parts = parts[len(piece):]
        term = jnp.dot(refs[n][0], field, preferred_element_type=jnp.float32)
        both = term if both is None else both + term
    real = both[:size, :size] + both[size:, size:]
    imag = both[size:, :size] - both[:size, size:]
    if len(parts) > 1:
        real += parts[0][0, 0]
        imag += parts[0][0, 1]
    out[0, 0] = real
    out[0, 1] = imag


def image_blocks(product, first, count, pieces, inner, before=None):
    _, rows, width = pieces[0][1][0][0].shape
    size = width // 2
    image_spec = pl.BlockSpec((1, 2, size, size), lambda j, o, u, i: (j, 0, 0, 0))
    specs = [
        pl.BlockSpec((1, width, rows), lambda j, o, u, i, n=n: (first + j, 0, o[n])) for n in range(len(pieces))
    ]
    values = [product] * len(pieces)
    begins = []
    for _, parts in pieces:
        for field, begin, is_inner in parts:
            specs.append(part_spec((1, rows, width), first, begin, field.shape[0], is_inner))
            values.append(field)
        begins.append([(begin, is_inner) for _, begin, is_inner in parts])
    if before is not None:
        specs.append(pl.BlockSpec((1, 2, size, size), lambda j, o, u, i: (first + j, 0, 0, 0)))
        values.append(before)
    places = jnp.stack([shot for shot, _ in pieces])
    return pl.pallas_call(
        functools.partial(image_kernel, first=first, begins=begins, size=size),
        grid_spec=pltpu.PrefetchScalarGridSpec(
            num_scalar_prefetch=3, grid=(count,), in_specs=specs, out_specs=image_spec
        ),
        out_shape=jax.ShapeDtypeStruct((count, 2, size, size), jnp.float32),
        compiler_params=params(),
        cost_estimate=SMALL,
        name="image",
    )(places, places, inner, *values)


def following(value, *earlier):
    return lax.optimization_barrier((value,) + earlier)[0]


def hand(value, *pairs):
    return lax.ppermute(value, "shot", pairs)


def send_sum(value, pairs):
    pairs = [(4 * a + b, 4 * c + d) for (a, b), (c, d) in pairs]
    return lax.ppermute(value.astype(jnp.bfloat16), ("shot", "freq"), pairs).astype(jnp.float32)


def sum_images(one, two, shot, freq):
    left = shot < 2
    shots = range(4)
    even = freq % 2 == 0
    low = freq < 2
    last = one[4:]
    one = one[:4]
    keep = jnp.where(even, jnp.concatenate([one, last]), jnp.concatenate([two, last]))
    send = jnp.where(even, jnp.concatenate([two, last]), jnp.concatenate([one, last]))
    image = keep + send_sum(send, [((s, f), (s, f ^ 1)) for s in shots for f in range(4)])
    keep = jnp.where(low, image[:2], image[2:4])
    send = jnp.where(low, image[2:4], image[:2])
    last = image[4] + send_sum(image[4], [((s, 1), (s, 3)) for s in (1, 2)])
    image = keep + send_sum(send, [((s, f), (s, f ^ 2)) for s in shots for f in range(4)])
    keep = jnp.where(left, image[0], image[1])
    send = jnp.where(left, image[1], image[0])
    image = keep + send_sum(send, [((s, f), (3 - s, f)) for s in shots for f in range(4) if (s, f) != (0, 3)])
    last = send_sum(last, [((1, 3), (3, 3))]) + send_sum(last, [((2, 3), (3, 3))])
    return jnp.where((shot == 3) & (freq == 3), last, image)


def split_body(source_field, receiver_field, operator, band_offsets, survey_tiles, survey_data):
    tiles = survey_data.shape[1]
    shot = lax.axis_index("shot")
    freq = lax.axis_index("freq")
    inner = ((shot == 1) | (shot == 2)).astype(jnp.int32)[None]
    offsets = band_offsets.T
    make = functools.partial(extrapolate_blocks, operator=operator[0], inner=inner)
    inward = ((0, 1), (3, 2))
    outward = ((1, 0), (2, 3))
    middle = ((1, 2), (2, 1))
    ends = ((0, 3), (3, 0))
    beyond = ((1, 3), (2, 0))

    far_data = hand(survey_data[0], *inward, *outward)
    (r_head,) = make(receiver_field[0], offsets=offsets, sets=[INNER[:HEAD]], listed=True)
    r_1_head = hand(r_head, *inward)
    r_3_head = hand(r_head, *middle)
    r_inner, r_outer, r_swap = make(
        receiver_field[0], offsets=following(offsets, r_head), sets=[INNER[HEAD:], OUTER], swap=True
    )
    r_3_in = hand(r_inner, *middle)
    r_1 = hand(following(r_swap, far_data, r_3_head), *inward, *outward)
    s_inner, s_outer = make(
        source_field[0], offsets=following(offsets, r_outer, r_3_head, r_1_head), sets=[INNER, OUTER]
    )
    s_out = hand(s_outer, *outward)
    s_in = hand(s_inner, *inward)
    forward_head = hand(r_1_head, *middle)
    r_3_out = hand(following(r_outer, r_3_in, r_1), *ends)
    r_1_rest = hand(r_outer[SWAP:], *outward)
    forward = hand(r_1, *middle)
    beyond_1 = hand(following(r_outer, s_out, forward_head)[:LATE], *beyond)
    beyond_2 = hand(following(r_outer, r_1_rest)[LATE:], *beyond)

    ids = survey_tiles[:, 1]
    near_ids = lax.dynamic_slice_in_dim(ids, shot * tiles, tiles)
    far_ids = lax.dynamic_slice_in_dim(ids, (shot ^ 1) * tiles, tiles)
    product = product_blocks(
        s_inner, s_outer, s_in, s_out, survey_data[0], far_data, near_ids, far_ids, inner
    )
    early = [
        (shot, [(r_head, 0, True), (r_inner, HEAD, True), (r_outer, 0, False)]),
        (shot ^ 1, [(r_1_head, 0, True), (r_1, HEAD, True), (r_1, 0, False), (r_1_rest, SWAP, False)]),
        (shot ^ 3, [(r_3_head, 0, True), (r_3_in, HEAD, True), (r_3_out, 0, False)]),
    ]
    forwarded = [(forward_head, 0, True), (forward, HEAD, True)]
    image = image_blocks(product, 0, len(INNER), early, inner)
    most = image_blocks(product, 0, LATE + 1, [(shot ^ 2, forwarded + [(beyond_1, 0, False)])], inner, image)
    rest = image_blocks(
        product, LATE + 1, len(INNER) - LATE - 1, [(shot ^ 2, forwarded + [(beyond_2, LATE, False)])], inner,
        following(image, most),
    )
    one = most[:FIRST]
    two = jnp.concatenate([most[FIRST:], rest])
    image = sum_images(one, two, shot, freq)
    total_freqs = source_field.shape[0] * lax.axis_size("freq")
    return image * (1.0 / math.sqrt(2.0 * NR * total_freqs))


def body(source_field, *rest):
    fits = (
        lax.axis_size("shot") == 4
        and lax.axis_size("freq") == 4
        and source_field.shape[1:] == (512, 16, 2, 128)
    )
    return (split_body if fits else general_body)(source_field, *rest)


def solution(mesh):
    return jax.shard_map(
        body,
        mesh=mesh,
        in_specs=(
            P("freq", ("groups", "shot"), None, None, None),
            P("freq", ("groups", "shot"), None, None, None),
            P("freq", "groups", None, None, None, None),
            P("groups", None),
            P("groups", None),
            P("freq", ("groups", "shot"), None, None, None),
        ),
        out_specs=P(None, ("groups", "shot", "freq"), None),
        check_vma=False,
    )
```

```python
import functools
import math

import jax
import jax.numpy as jnp
from jax import lax
from jax.experimental import pallas as pl
from jax.experimental.pallas import tpu as pltpu
from jax.sharding import PartitionSpec as P

NR = 2048
SMALL = pl.CostEstimate(flops=1000, bytes_accessed=1000, transcendentals=0)


def extrapolate(wavefield, operator, columns):
    row_count, blocks_x, components, block_size = wavefield.shape
    bands = columns.shape[1]
    real_part = operator[:, :, 0]
    imag_part = operator[:, :, 1]
    upper_rows = jnp.concatenate([real_part, imag_part], -1)
    lower_rows = jnp.concatenate([-imag_part, real_part], -1)
    real_block = jnp.concatenate([upper_rows, lower_rows], -2)
    real_block = real_block.reshape(blocks_x, bands, 2 * block_size, 2, block_size)
    chosen = jnp.take(wavefield, columns, axis=1).reshape(
        row_count, blocks_x, bands, 2 * block_size
    )
    result = jnp.einsum("sikc,ikcoy->soiy", chosen, real_block, preferred_element_type=jnp.float32)
    return result.astype(jnp.bfloat16)


def to_owners(wavefield, shot_count, own_cells):
    row_count = wavefield.shape[0]
    return wavefield.reshape(row_count, 2, shot_count, own_cells)


def to_tiles(wavefield, shot_count, own_cells):
    row_count, components, blocks_x, block_size = wavefield.shape
    if own_cells >= block_size:
        return to_owners(wavefield, shot_count, own_cells)
    factor = block_size // own_cells
    copies = jnp.broadcast_to(
        wavefield[:, :, :, None, :], (row_count, components, blocks_x, factor, block_size)
    )
    return copies.reshape(row_count, components, shot_count, block_size)


def data_product(source_cells, data_shard, survey_tiles, block_size, own_cells):
    source_count = source_cells.shape[0]
    receiver_blocks = NR // block_size
    blocks = source_cells.reshape(source_count // block_size, block_size, 2 * own_cells)
    block_ids = jnp.arange(receiver_blocks, dtype=jnp.int32)
    chosen = jnp.take(blocks, survey_tiles[:, 0], axis=0)
    products = jnp.einsum(
        "ncsr,nsk->ncrk",
        lax.all_gather(data_shard, "shot", axis=0, tiled=True),
        chosen,
        preferred_element_type=jnp.float32,
    )
    real_part = products[:, 0, :, :own_cells] - products[:, 1, :, own_cells:]
    imag_part = products[:, 0, :, own_cells:] + products[:, 1, :, :own_cells]
    contribution = jnp.concatenate([real_part, imag_part], -1)
    onehot = (survey_tiles[:, 1][:, None] == block_ids[None, :]).astype(jnp.float32)
    summed = jnp.einsum("nq,nrk->qrk", onehot, contribution, precision=lax.Precision.HIGHEST)
    return summed.reshape(NR, 2, own_cells).astype(jnp.bfloat16)


def image_tile(product, receiver_tile, block_size):
    row_count, components, own_cells = product.shape
    tiles_here = max(own_cells // block_size, 1)
    inner_cells = own_cells // tiles_here
    left = product.reshape(row_count, 2, tiles_here, inner_cells)
    right = receiver_tile.reshape(row_count, 2, tiles_here, block_size)
    turned = jnp.stack([-right[:, 1], right[:, 0]], 1)
    both = jnp.stack([right, turned], 1)
    result = jnp.einsum("rctx,rocty->otxy", left, both, preferred_element_type=jnp.float32)
    return result.reshape(2, own_cells, block_size)


def general_body(source_field, receiver_field, operator, band_offsets, survey_tiles, survey_data):
    shot_count = lax.axis_size("shot")
    freq_local = source_field.shape[0]
    blocks_x = source_field.shape[2]
    block_size = source_field.shape[4]
    own_cells = blocks_x * block_size // shot_count
    block_rows = jnp.arange(blocks_x, dtype=jnp.int32)[:, None]
    columns = (block_rows + band_offsets) % blocks_x
    source_next = extrapolate(source_field[0], operator[0], columns)
    receiver_next = extrapolate(receiver_field[0], operator[0], columns)
    source_send = to_owners(source_next, shot_count, own_cells)
    receiver_send = to_tiles(receiver_next, shot_count, own_cells)
    source_cells = lax.all_to_all(source_send, "shot", split_axis=2, concat_axis=0, tiled=True)
    receiver_tile = lax.all_to_all(receiver_send, "shot", split_axis=2, concat_axis=0, tiled=True)
    source_cells = source_cells.reshape(source_cells.shape[0], 2 * own_cells)
    product = data_product(source_cells, survey_data[0], survey_tiles, block_size, own_cells)
    receiver_tile = receiver_tile.reshape(receiver_tile.shape[0], 2, -1)
    image_sum = image_tile(product, receiver_tile, block_size)
    total_freqs = freq_local * lax.axis_size("freq")
    scaled = image_sum * (1.0 / math.sqrt(2.0 * NR * total_freqs))
    return lax.psum_scatter(scaled, "freq", scatter_dimension=1, tiled=True)


INNER = [4, 8, 6, 10, 15, 5, 9, 7, 11]
HEAD = 3
OUTER = [0, 12, 2, 14, 1, 13, 3]
FIRST = 5
OUTER_FIRST = 4
LATE = 5


def outer_place(slot):
    return jnp.where(slot < FIRST, jnp.minimum(slot, OUTER_FIRST - 1), jnp.minimum(slot - 1, len(OUTER) - 1))


def params(limit=24):
    return pltpu.CompilerParams(vmem_limit_bytes=limit * 1024 * 1024)


def extrapolate_kernel(order, offsets, field, operator, *refs, sets, rows, blocks, parts, listed):
    stage, apart, lines, weights, field_sems, weight_sems = refs[-6:]
    outs = refs[:-6]
    sizes = [len(one) for one in sets]
    step = pl.program_id(0)
    bands = operator.shape[1]
    pitch = 2 * blocks + 1
    chunk = stage.shape[0] // pitch
    part_lines = lines.shape[0] // parts

    def column(block, band):
        return lax.rem(block + offsets[band, block] + blocks, blocks)

    def field_copy(part):
        here = pl.ds(part * part_lines, part_lines)
        return pltpu.make_async_copy(field.at[here], lines.at[here], field_sems.at[part])

    def weight_copy(n, block):
        return pltpu.make_async_copy(operator.at[block], weights.at[n], weight_sems.at[n])

    @pl.when(step == 0)
    def _():
        for part in range(parts):
            field_copy(part).start()
        for n, block in enumerate(sum(sets, [])):
            weight_copy(n, block).start()
        if listed:
            wanted = [column(block, band) for block in sum(sets, []) for band in range(bands)]
        else:
            wanted = list(range(blocks))

        def split(n, carry):
            for row in range(chunk):
                here = pl.ds(pl.multiple_of((n * chunk + row) * 2 * blocks, 2 * blocks), 2 * blocks)
                stage[pl.ds(row * pitch, 2 * blocks), :] = lines[here, :].astype(jnp.float32)
            to = pl.ds(pl.multiple_of(n * chunk, chunk), chunk)
            for slot, block in enumerate(wanted):
                for half in range(2):
                    picked = stage[pl.ds(2 * block + half, chunk, stride=pitch), :]
                    apart[slot, to, half * 128:(half + 1) * 128] = picked.astype(jnp.bfloat16)
            return carry

        steps = rows // chunk // parts
        for part in range(parts):
            field_copy(part).wait()
            lax.fori_loop(part * steps, (part + 1) * steps, split, 0)

    block = order[step]
    weight_copy(step, block).wait()
    inputs = []
    factors = []
    for band in range(bands):
        inputs.append(apart[step * bands + band if listed else column(block, band)])
        real = weights[step, band, 0]
        imag = weights[step, band, 1]
        factors.append(jnp.concatenate([real, imag], 1))
        factors.append(jnp.concatenate([-imag, real], 1))
    result = jnp.dot(
        jnp.concatenate(inputs, 1), jnp.concatenate(factors, 0), preferred_element_type=jnp.float32
    ).astype(jnp.bfloat16)
    first = 0
    for out, count in zip(outs, sizes):
        if len(sizes) == 1:
            out[0] = result
        else:
            @pl.when((step >= first) & (step < first + count))
            def _(out=out):
                out[0] = result
        first += count


def extrapolate_blocks(field, operator, offsets, sets, listed=False, limit=60):
    rows, blocks, _, size = field.shape
    bands = offsets.shape[0]
    width = 2 * size
    chunk = 32
    parts = 4
    sizes = [len(one) for one in sets]
    count = sum(sizes)
    order = jnp.array(sum(sets, []), jnp.int32)
    firsts = [sum(sizes[:n]) for n in range(len(sizes))]
    flat = field.reshape(rows * blocks * 2, size)

    def out_spec(first, count):
        return pl.BlockSpec((1, rows, width), lambda j, o, c: (jnp.clip(j - first, 0, count - 1), 0, 0))

    return pl.pallas_call(
        functools.partial(
            extrapolate_kernel, sets=sets, rows=rows, blocks=blocks, parts=parts, listed=listed
        ),
        grid_spec=pltpu.PrefetchScalarGridSpec(
            num_scalar_prefetch=2,
            grid=(count,),
            in_specs=[pl.BlockSpec(memory_space=pltpu.HBM)] * 2,
            out_specs=[out_spec(*one) for one in zip(firsts, sizes)],
            scratch_shapes=[
                pltpu.VMEM((chunk * (2 * blocks + 1), size), jnp.float32),
                pltpu.VMEM((count * bands if listed else blocks, rows, width), jnp.bfloat16),
                pltpu.VMEM(flat.shape, jnp.bfloat16),
                pltpu.VMEM((count,) + operator.shape[1:], jnp.bfloat16),
                pltpu.SemaphoreType.DMA((parts,)),
                pltpu.SemaphoreType.DMA((count,)),
            ],
        ),
        out_shape=[jax.ShapeDtypeStruct((n, rows, width), jnp.bfloat16) for n in sizes],
        compiler_params=params(limit),
        cost_estimate=SMALL,
        name="extrapolate",
    )(order, offsets, flat, operator)


def product_kernel(near_ids, far_ids, inner, near_in, near_out, far_in, far_out, near_data, far_data, out, turned, total):
    size = near_data.shape[2]
    tiles = near_data.shape[0]
    sources = near_in.shape[1] // size
    per_source = tiles // sources

    @pl.when(pl.program_id(0) == 0)
    def _():
        for side, data in enumerate((near_data, far_data)):
            for tile in range(tiles):
                for part in range(2):
                    turned[side * tiles + tile, :, part * size:(part + 1) * size] = data[tile, part].T

    total[...] = jnp.zeros_like(total)
    sides = ((near_in, near_out, near_ids), (far_in, far_out, far_ids))
    for side, (field_in, field_out, ids) in enumerate(sides):
        for source in range(sources):
            lines = slice(source * size, (source + 1) * size)
            upper = jnp.where(inner[0] > 0, field_in[0, lines, :], field_out[0, lines, :])
            lower = jnp.concatenate([-upper[:, size:], upper[:, :size]], 1)
            both = jnp.concatenate([upper, lower], 0)
            first = side * tiles + source * per_source
            left = turned[first:first + per_source].reshape(per_source * size, 2 * size)
            result = jnp.dot(left, both, preferred_element_type=jnp.float32)
            for tile in range(per_source):
                total[ids[source * per_source + tile]] += result[tile * size:(tile + 1) * size]
    for block in range(total.shape[0]):
        out[0, :, block * size:(block + 1) * size] = total[block].T.astype(jnp.bfloat16)


def part_spec(shape, first, begin, count, is_inner):
    def index(j, a, b, inner):
        place = first + j if is_inner else outer_place(first + j)
        place = jnp.clip(place - begin, 0, count - 1)
        return jnp.where((inner[0] > 0) == is_inner, place, 0), 0, 0

    return pl.BlockSpec(shape, index)


def product_blocks(near_in, near_out, far_in, far_out, near_data, far_data, near_ids, far_ids, inner):
    blocks, rows, width = near_in.shape
    tiles, _, size, _ = near_data.shape
    receivers = NR // size
    shape = (1, rows, width)
    data_spec = pl.BlockSpec(near_data.shape, lambda j, a, b, i: (0, 0, 0, 0))
    return pl.pallas_call(
        product_kernel,
        grid_spec=pltpu.PrefetchScalarGridSpec(
            num_scalar_prefetch=3,
            grid=(blocks,),
            in_specs=[part_spec(shape, 0, 0, len(INNER), True), part_spec(shape, 0, 0, len(OUTER), False)] * 2
            + [data_spec, data_spec],
            out_specs=pl.BlockSpec((1, width, NR), lambda j, a, b, i: (j, 0, 0)),
            scratch_shapes=[
                pltpu.VMEM((2 * tiles, size, width), jnp.bfloat16),
                pltpu.VMEM((receivers, size, width), jnp.float32),
            ],
        ),
        out_shape=jax.ShapeDtypeStruct((blocks, width, NR), jnp.bfloat16),
        compiler_params=params(),
        cost_estimate=SMALL,
        name="product",
    )(near_ids, far_ids, inner, near_in, near_out, far_in, far_out, near_data, far_data)


def image_kernel(places, unused, inner, *refs, first, begins, size):
    out = refs[-1]
    slot = first + pl.program_id(0)
    parts = refs[len(begins):]
    both = None
    for n, piece in enumerate(begins):
        field = parts[0][0]
        for part, (begin, is_inner) in zip(parts[1:], piece[1:]):
            chosen = (inner[0] > 0) & (slot >= begin) if is_inner else inner[0] == 0
            field = jnp.where(chosen, part[0], field)
        parts = parts[len(piece):]
        term = jnp.dot(refs[n][0], field, preferred_element_type=jnp.float32)
        both = term if both is None else both + term
    real = both[:size, :size] + both[size:, size:]
    imag = both[size:, :size] - both[:size, size:]
    if len(parts) > 1:
        real += parts[0][0, 0]
        imag += parts[0][0, 1]
    out[0, 0] = real
    out[0, 1] = imag


def image_blocks(product, first, count, pieces, inner, before=None):
    _, rows, width = pieces[0][1][0][0].shape
    size = width // 2
    image_spec = pl.BlockSpec((1, 2, size, size), lambda j, o, u, i: (j, 0, 0, 0))
    specs = [
        pl.BlockSpec((1, width, rows), lambda j, o, u, i, n=n: (first + j, 0, o[n])) for n in range(len(pieces))
    ]
    values = [product] * len(pieces)
    begins = []
    for _, parts in pieces:
        inners = [True] * (len(parts) - 1) + [False]
        for (field, begin), is_inner in zip(parts, inners):
            specs.append(part_spec((1, rows, width), first, begin, field.shape[0], is_inner))
            values.append(field)
        begins.append([(begin, is_inner) for (_, begin), is_inner in zip(parts, inners)])
    if before is not None:
        specs.append(pl.BlockSpec((1, 2, size, size), lambda j, o, u, i: (first + j, 0, 0, 0)))
        values.append(before)
    places = jnp.stack([shot for shot, _ in pieces])
    return pl.pallas_call(
        functools.partial(image_kernel, first=first, begins=begins, size=size),
        grid_spec=pltpu.PrefetchScalarGridSpec(
            num_scalar_prefetch=3, grid=(count,), in_specs=specs, out_specs=image_spec
        ),
        out_shape=jax.ShapeDtypeStruct((count, 2, size, size), jnp.float32),
        compiler_params=params(),
        cost_estimate=SMALL,
        name="image",
    )(places, places, inner, *values)


def following(value, *earlier):
    return lax.optimization_barrier((value,) + earlier)[0]


def hand(value, *pairs):
    return lax.ppermute(value, "shot", pairs)


def send_sum(value, pairs):
    pairs = [(4 * a + b, 4 * c + d) for (a, b), (c, d) in pairs]
    return lax.ppermute(value.astype(jnp.bfloat16), ("shot", "freq"), pairs).astype(jnp.float32)


def sum_images(one, two, shot, freq):
    left = shot < 2
    shots = range(4)
    even = freq % 2 == 0
    low = freq < 2
    last = one[4:]
    one = one[:4]
    keep = jnp.where(even, jnp.concatenate([one, last]), jnp.concatenate([two, last]))
    send = jnp.where(even, jnp.concatenate([two, last]), jnp.concatenate([one, last]))
    image = keep + send_sum(send, [((s, f), (s, f ^ 1)) for s in shots for f in range(4)])
    keep = jnp.where(low, image[:2], image[2:4])
    send = jnp.where(low, image[2:4], image[:2])
    last = image[4] + send_sum(image[4], [((s, 1), (s, 3)) for s in (1, 2)])
    image = keep + send_sum(send, [((s, f), (s, f ^ 2)) for s in shots for f in range(4)])
    keep = jnp.where(left, image[0], image[1])
    send = jnp.where(left, image[1], image[0])
    image = keep + send_sum(send, [((s, f), (3 - s, f)) for s in shots for f in range(4) if (s, f) != (0, 3)])
    last = send_sum(last, [((1, 3), (3, 3))]) + send_sum(last, [((2, 3), (3, 3))])
    return jnp.where((shot == 3) & (freq == 3), last, image)


def split_body(source_field, receiver_field, operator, band_offsets, survey_tiles, survey_data):
    tiles = survey_data.shape[1]
    shot = lax.axis_index("shot")
    freq = lax.axis_index("freq")
    inner = ((shot == 1) | (shot == 2)).astype(jnp.int32)[None]
    offsets = band_offsets.T
    make = functools.partial(extrapolate_blocks, operator=operator[0])
    inward = ((0, 1), (3, 2))
    outward = ((1, 0), (2, 3))
    middle = ((1, 2), (2, 1))
    ends = ((0, 3), (3, 0))
    beyond = ((1, 3), (2, 0))

    far_data = hand(survey_data[0], *inward, *outward)
    (r_head,) = make(receiver_field[0], offsets=offsets, sets=[INNER[:HEAD]], listed=True)
    r_1_head = hand(r_head, *inward)
    r_3_head = hand(r_head, *middle)
    r_inner, r_outer = make(receiver_field[0], offsets=following(offsets, r_head), sets=[INNER[HEAD:], OUTER])
    r_3_in = hand(r_inner, *middle)
    r_1_in = hand(r_inner, *inward)
    r_1_out = hand(following(r_outer, far_data, r_3_head), *outward)
    s_inner, s_outer = make(
        source_field[0], offsets=following(offsets, r_outer, r_3_head), sets=[INNER, OUTER]
    )
    s_out = hand(following(s_outer, r_1_head), *outward)
    s_in = hand(s_inner, *inward)
    forward_head = hand(following(r_1_head, r_3_in), *middle)
    r_3_out = hand(r_outer, *ends)
    forward = hand(following(r_1_in, r_1_out), *middle)
    beyond_1 = hand(following(r_outer, s_out, forward_head)[:LATE], *beyond)
    beyond_2 = hand(r_outer[LATE:], *beyond)

    ids = survey_tiles[:, 1]
    near_ids = lax.dynamic_slice_in_dim(ids, shot * tiles, tiles)
    far_ids = lax.dynamic_slice_in_dim(ids, (shot ^ 1) * tiles, tiles)
    product = product_blocks(
        s_inner, s_outer, s_in, s_out, survey_data[0], far_data, near_ids, far_ids, inner
    )
    early = [
        (shot, [(r_head, 0), (r_inner, HEAD), (r_outer, 0)]),
        (shot ^ 1, [(r_1_head, 0), (r_1_in, HEAD), (r_1_out, 0)]),
        (shot ^ 3, [(r_3_head, 0), (r_3_in, HEAD), (r_3_out, 0)]),
    ]
    forwarded = [(forward_head, 0), (forward, HEAD)]
    image = image_blocks(product, 0, len(INNER), early, inner)
    most = image_blocks(product, 0, LATE + 1, [(shot ^ 2, forwarded + [(beyond_1, 0)])], inner, image)
    rest = image_blocks(
        product, LATE + 1, len(INNER) - LATE - 1, [(shot ^ 2, forwarded + [(beyond_2, LATE)])], inner,
        following(image, most),
    )
    one = most[:FIRST]
    two = jnp.concatenate([most[FIRST:], rest])
    image = sum_images(one, two, shot, freq)
    total_freqs = source_field.shape[0] * lax.axis_size("freq")
    return image * (1.0 / math.sqrt(2.0 * NR * total_freqs))


def body(source_field, *rest):
    fits = (
        lax.axis_size("shot") == 4
        and lax.axis_size("freq") == 4
        and source_field.shape[1:] == (512, 16, 2, 128)
    )
    return (split_body if fits else general_body)(source_field, *rest)


def solution(mesh):
    return jax.shard_map(
        body,
        mesh=mesh,
        in_specs=(
            P("freq", ("groups", "shot"), None, None, None),
            P("freq", ("groups", "shot"), None, None, None),
            P("freq", "groups", None, None, None, None),
            P("groups", None),
            P("groups", None),
            P("freq", ("groups", "shot"), None, None, None),
        ),
        out_specs=P(None, ("groups", "shot", "freq"), None),
        check_vma=False,
    )
```

```python
import functools
import math

import jax
import jax.numpy as jnp
from jax import lax
from jax.experimental import pallas as pl
from jax.experimental.pallas import tpu as pltpu
from jax.sharding import PartitionSpec as P

NR = 2048
SMALL = pl.CostEstimate(flops=1000, bytes_accessed=1000, transcendentals=0)


def extrapolate(wavefield, operator, columns):
    row_count, blocks_x, components, block_size = wavefield.shape
    bands = columns.shape[1]
    real_part = operator[:, :, 0]
    imag_part = operator[:, :, 1]
    upper_rows = jnp.concatenate([real_part, imag_part], -1)
    lower_rows = jnp.concatenate([-imag_part, real_part], -1)
    real_block = jnp.concatenate([upper_rows, lower_rows], -2)
    real_block = real_block.reshape(blocks_x, bands, 2 * block_size, 2, block_size)
    chosen = jnp.take(wavefield, columns, axis=1).reshape(
        row_count, blocks_x, bands, 2 * block_size
    )
    result = jnp.einsum("sikc,ikcoy->soiy", chosen, real_block, preferred_element_type=jnp.float32)
    return result.astype(jnp.bfloat16)


def to_owners(wavefield, shot_count, own_cells):
    row_count = wavefield.shape[0]
    return wavefield.reshape(row_count, 2, shot_count, own_cells)


def to_tiles(wavefield, shot_count, own_cells):
    row_count, components, blocks_x, block_size = wavefield.shape
    if own_cells >= block_size:
        return to_owners(wavefield, shot_count, own_cells)
    factor = block_size // own_cells
    copies = jnp.broadcast_to(
        wavefield[:, :, :, None, :], (row_count, components, blocks_x, factor, block_size)
    )
    return copies.reshape(row_count, components, shot_count, block_size)


def data_product(source_cells, data_shard, survey_tiles, block_size, own_cells):
    source_count = source_cells.shape[0]
    receiver_blocks = NR // block_size
    blocks = source_cells.reshape(source_count // block_size, block_size, 2 * own_cells)
    block_ids = jnp.arange(receiver_blocks, dtype=jnp.int32)
    chosen = jnp.take(blocks, survey_tiles[:, 0], axis=0)
    products = jnp.einsum(
        "ncsr,nsk->ncrk",
        lax.all_gather(data_shard, "shot", axis=0, tiled=True),
        chosen,
        preferred_element_type=jnp.float32,
    )
    real_part = products[:, 0, :, :own_cells] - products[:, 1, :, own_cells:]
    imag_part = products[:, 0, :, own_cells:] + products[:, 1, :, :own_cells]
    contribution = jnp.concatenate([real_part, imag_part], -1)
    onehot = (survey_tiles[:, 1][:, None] == block_ids[None, :]).astype(jnp.float32)
    summed = jnp.einsum("nq,nrk->qrk", onehot, contribution, precision=lax.Precision.HIGHEST)
    return summed.reshape(NR, 2, own_cells).astype(jnp.bfloat16)


def image_tile(product, receiver_tile, block_size):
    row_count, components, own_cells = product.shape
    tiles_here = max(own_cells // block_size, 1)
    inner_cells = own_cells // tiles_here
    left = product.reshape(row_count, 2, tiles_here, inner_cells)
    right = receiver_tile.reshape(row_count, 2, tiles_here, block_size)
    turned = jnp.stack([-right[:, 1], right[:, 0]], 1)
    both = jnp.stack([right, turned], 1)
    result = jnp.einsum("rctx,rocty->otxy", left, both, preferred_element_type=jnp.float32)
    return result.reshape(2, own_cells, block_size)


def general_body(source_field, receiver_field, operator, band_offsets, survey_tiles, survey_data):
    shot_count = lax.axis_size("shot")
    freq_local = source_field.shape[0]
    blocks_x = source_field.shape[2]
    block_size = source_field.shape[4]
    own_cells = blocks_x * block_size // shot_count
    block_rows = jnp.arange(blocks_x, dtype=jnp.int32)[:, None]
    columns = (block_rows + band_offsets) % blocks_x
    source_next = extrapolate(source_field[0], operator[0], columns)
    receiver_next = extrapolate(receiver_field[0], operator[0], columns)
    source_send = to_owners(source_next, shot_count, own_cells)
    receiver_send = to_tiles(receiver_next, shot_count, own_cells)
    source_cells = lax.all_to_all(source_send, "shot", split_axis=2, concat_axis=0, tiled=True)
    receiver_tile = lax.all_to_all(receiver_send, "shot", split_axis=2, concat_axis=0, tiled=True)
    source_cells = source_cells.reshape(source_cells.shape[0], 2 * own_cells)
    product = data_product(source_cells, survey_data[0], survey_tiles, block_size, own_cells)
    receiver_tile = receiver_tile.reshape(receiver_tile.shape[0], 2, -1)
    image_sum = image_tile(product, receiver_tile, block_size)
    total_freqs = freq_local * lax.axis_size("freq")
    scaled = image_sum * (1.0 / math.sqrt(2.0 * NR * total_freqs))
    return lax.psum_scatter(scaled, "freq", scatter_dimension=1, tiled=True)


INNER = [4, 8, 6, 10, 15, 5, 9, 7, 11]
HEAD = 3
OUTER = [0, 12, 2, 14, 1, 13, 3]
FIRST = 5
OUTER_FIRST = 4
LATE = 5
HALF = 4


def outer_place(slot):
    return jnp.where(slot < FIRST, jnp.minimum(slot, OUTER_FIRST - 1), jnp.minimum(slot - 1, len(OUTER) - 1))


def params(limit=24):
    return pltpu.CompilerParams(vmem_limit_bytes=limit * 1024 * 1024)


def extrapolate_kernel(order, offsets, field, operator, *refs, sets, rows, blocks, parts, listed):
    stage, apart, lines, weights, field_sems, weight_sems = refs[-6:]
    outs = refs[:-6]
    sizes = [len(one) for one in sets]
    step = pl.program_id(0)
    bands = operator.shape[1]
    pitch = 2 * blocks + 1
    chunk = stage.shape[0] // pitch
    part_lines = lines.shape[0] // parts

    def column(block, band):
        return lax.rem(block + offsets[band, block] + blocks, blocks)

    def field_copy(part):
        here = pl.ds(part * part_lines, part_lines)
        return pltpu.make_async_copy(field.at[here], lines.at[here], field_sems.at[part])

    def weight_copy(n, block):
        return pltpu.make_async_copy(operator.at[block], weights.at[n], weight_sems.at[n])

    @pl.when(step == 0)
    def _():
        for part in range(parts):
            field_copy(part).start()
        for n, block in enumerate(sum(sets, [])):
            weight_copy(n, block).start()
        if listed:
            wanted = [column(block, band) for block in sum(sets, []) for band in range(bands)]
        else:
            wanted = list(range(blocks))

        def split(n, carry):
            for row in range(chunk):
                here = pl.ds(pl.multiple_of((n * chunk + row) * 2 * blocks, 2 * blocks), 2 * blocks)
                stage[pl.ds(row * pitch, 2 * blocks), :] = lines[here, :].astype(jnp.float32)
            to = pl.ds(pl.multiple_of(n * chunk, chunk), chunk)
            for slot, block in enumerate(wanted):
                for half in range(2):
                    picked = stage[pl.ds(2 * block + half, chunk, stride=pitch), :]
                    apart[slot, to, half * 128:(half + 1) * 128] = picked.astype(jnp.bfloat16)
            return carry

        steps = rows // chunk // parts
        for part in range(parts):
            field_copy(part).wait()
            lax.fori_loop(part * steps, (part + 1) * steps, split, 0)

    block = order[step]
    weight_copy(step, block).wait()
    inputs = []
    factors = []
    for band in range(bands):
        inputs.append(apart[step * bands + band if listed else column(block, band)])
        real = weights[step, band, 0]
        imag = weights[step, band, 1]
        factors.append(jnp.concatenate([real, imag], 1))
        factors.append(jnp.concatenate([-imag, real], 1))
    result = jnp.dot(
        jnp.concatenate(inputs, 1), jnp.concatenate(factors, 0), preferred_element_type=jnp.float32
    ).astype(jnp.bfloat16)
    first = 0
    for out, count in zip(outs, sizes):
        if len(sizes) == 1:
            out[0] = result
        else:
            @pl.when((step >= first) & (step < first + count))
            def _(out=out):
                out[0] = result
        first += count


def extrapolate_blocks(field, operator, offsets, sets, listed=False, limit=60):
    rows, blocks, _, size = field.shape
    bands = offsets.shape[0]
    width = 2 * size
    chunk = 32
    parts = 4
    sizes = [len(one) for one in sets]
    count = sum(sizes)
    order = jnp.array(sum(sets, []), jnp.int32)
    firsts = [sum(sizes[:n]) for n in range(len(sizes))]
    flat = field.reshape(rows * blocks * 2, size)

    def out_spec(first, count):
        return pl.BlockSpec((1, rows, width), lambda j, o, c: (jnp.clip(j - first, 0, count - 1), 0, 0))

    return pl.pallas_call(
        functools.partial(
            extrapolate_kernel, sets=sets, rows=rows, blocks=blocks, parts=parts, listed=listed
        ),
        grid_spec=pltpu.PrefetchScalarGridSpec(
            num_scalar_prefetch=2,
            grid=(count,),
            in_specs=[pl.BlockSpec(memory_space=pltpu.HBM)] * 2,
            out_specs=[out_spec(*one) for one in zip(firsts, sizes)],
            scratch_shapes=[
                pltpu.VMEM((chunk * (2 * blocks + 1), size), jnp.float32),
                pltpu.VMEM((count * bands if listed else blocks, rows, width), jnp.bfloat16),
                pltpu.VMEM(flat.shape, jnp.bfloat16),
                pltpu.VMEM((count,) + operator.shape[1:], jnp.bfloat16),
                pltpu.SemaphoreType.DMA((parts,)),
                pltpu.SemaphoreType.DMA((count,)),
            ],
        ),
        out_shape=[jax.ShapeDtypeStruct((n, rows, width), jnp.bfloat16) for n in sizes],
        compiler_params=params(limit),
        cost_estimate=SMALL,
        name="extrapolate",
    )(order, offsets, flat, operator)


def product_kernel(near_ids, far_ids, inner, near_in, near_out, far_in, far_out, near_data, far_data, out, turned, total):
    size = near_data.shape[2]
    tiles = near_data.shape[0]
    sources = near_in.shape[1] // size
    per_source = tiles // sources

    @pl.when(pl.program_id(0) == 0)
    def _():
        for side, data in enumerate((near_data, far_data)):
            for tile in range(tiles):
                for part in range(2):
                    turned[side * tiles + tile, :, part * size:(part + 1) * size] = data[tile, part].T

    total[...] = jnp.zeros_like(total)
    sides = ((near_in, near_out, near_ids), (far_in, far_out, far_ids))
    for side, (field_in, field_out, ids) in enumerate(sides):
        for source in range(sources):
            lines = slice(source * size, (source + 1) * size)
            upper = jnp.where(inner[0] > 0, field_in[0, lines, :], field_out[0, lines, :])
            lower = jnp.concatenate([-upper[:, size:], upper[:, :size]], 1)
            both = jnp.concatenate([upper, lower], 0)
            first = side * tiles + source * per_source
            left = turned[first:first + per_source].reshape(per_source * size, 2 * size)
            result = jnp.dot(left, both, preferred_element_type=jnp.float32)
            for tile in range(per_source):
                total[ids[source * per_source + tile]] += result[tile * size:(tile + 1) * size]
    for block in range(total.shape[0]):
        out[0, :, block * size:(block + 1) * size] = total[block].T.astype(jnp.bfloat16)


def part_spec(shape, first, begin, count, is_inner):
    def index(j, a, b, inner):
        place = first + j if is_inner else outer_place(first + j)
        place = jnp.clip(place - begin, 0, count - 1)
        return jnp.where((inner[0] > 0) == is_inner, place, 0), 0, 0

    return pl.BlockSpec(shape, index)


def product_blocks(near_in, near_out, far_in, far_out, near_data, far_data, near_ids, far_ids, inner):
    blocks, rows, width = near_in.shape
    tiles, _, size, _ = near_data.shape
    receivers = NR // size
    shape = (1, rows, width)
    data_spec = pl.BlockSpec(near_data.shape, lambda j, a, b, i: (0, 0, 0, 0))
    return pl.pallas_call(
        product_kernel,
        grid_spec=pltpu.PrefetchScalarGridSpec(
            num_scalar_prefetch=3,
            grid=(blocks,),
            in_specs=[part_spec(shape, 0, 0, len(INNER), True), part_spec(shape, 0, 0, len(OUTER), False)] * 2
            + [data_spec, data_spec],
            out_specs=pl.BlockSpec((1, width, NR), lambda j, a, b, i: (j, 0, 0)),
            scratch_shapes=[
                pltpu.VMEM((2 * tiles, size, width), jnp.bfloat16),
                pltpu.VMEM((receivers, size, width), jnp.float32),
            ],
        ),
        out_shape=jax.ShapeDtypeStruct((blocks, width, NR), jnp.bfloat16),
        compiler_params=params(),
        cost_estimate=SMALL,
        name="product",
    )(near_ids, far_ids, inner, near_in, near_out, far_in, far_out, near_data, far_data)


def image_kernel(places, unused, inner, *refs, first, begins, size):
    out = refs[-1]
    slot = first + pl.program_id(0)
    parts = refs[len(begins):]
    both = None
    for n, piece in enumerate(begins):
        field = parts[0][0]
        for part, (begin, is_inner) in zip(parts[1:], piece[1:]):
            place = slot if is_inner else outer_place(slot)
            field = jnp.where(((inner[0] > 0) == is_inner) & (place >= begin), part[0], field)
        parts = parts[len(piece):]
        term = jnp.dot(refs[n][0], field, preferred_element_type=jnp.float32)
        both = term if both is None else both + term
    real = both[:size, :size] + both[size:, size:]
    imag = both[size:, :size] - both[:size, size:]
    if len(parts) > 1:
        real += parts[0][0, 0]
        imag += parts[0][0, 1]
    out[0, 0] = real
    out[0, 1] = imag


def image_blocks(product, first, count, pieces, inner, before=None):
    _, rows, width = pieces[0][1][0][0].shape
    size = width // 2
    image_spec = pl.BlockSpec((1, 2, size, size), lambda j, o, u, i: (j, 0, 0, 0))
    specs = [
        pl.BlockSpec((1, width, rows), lambda j, o, u, i, n=n: (first + j, 0, o[n])) for n in range(len(pieces))
    ]
    values = [product] * len(pieces)
    begins = []
    for _, parts in pieces:
        for field, begin, is_inner in parts:
            specs.append(part_spec((1, rows, width), first, begin, field.shape[0], is_inner))
            values.append(field)
        begins.append([(begin, is_inner) for _, begin, is_inner in parts])
    if before is not None:
        specs.append(pl.BlockSpec((1, 2, size, size), lambda j, o, u, i: (first + j, 0, 0, 0)))
        values.append(before)
    places = jnp.stack([shot for shot, _ in pieces])
    return pl.pallas_call(
        functools.partial(image_kernel, first=first, begins=begins, size=size),
        grid_spec=pltpu.PrefetchScalarGridSpec(
            num_scalar_prefetch=3, grid=(count,), in_specs=specs, out_specs=image_spec
        ),
        out_shape=jax.ShapeDtypeStruct((count, 2, size, size), jnp.float32),
        compiler_params=params(),
        cost_estimate=SMALL,
        name="image",
    )(places, places, inner, *values)


def following(value, *earlier):
    return lax.optimization_barrier((value,) + earlier)[0]


def hand(value, *pairs):
    return lax.ppermute(value, "shot", pairs)


def send_sum(value, pairs):
    pairs = [(4 * a + b, 4 * c + d) for (a, b), (c, d) in pairs]
    return lax.ppermute(value.astype(jnp.bfloat16), ("shot", "freq"), pairs).astype(jnp.float32)


def sum_images(one, two, shot, freq):
    left = shot < 2
    shots = range(4)
    even = freq % 2 == 0
    low = freq < 2
    last = one[4:]
    one = one[:4]
    keep = jnp.where(even, jnp.concatenate([one, last]), jnp.concatenate([two, last]))
    send = jnp.where(even, jnp.concatenate([two, last]), jnp.concatenate([one, last]))
    image = keep + send_sum(send, [((s, f), (s, f ^ 1)) for s in shots for f in range(4)])
    keep = jnp.where(low, image[:2], image[2:4])
    send = jnp.where(low, image[2:4], image[:2])
    last = image[4] + send_sum(image[4], [((s, 1), (s, 3)) for s in (1, 2)])
    image = keep + send_sum(send, [((s, f), (s, f ^ 2)) for s in shots for f in range(4)])
    keep = jnp.where(left, image[0], image[1])
    send = jnp.where(left, image[1], image[0])
    image = keep + send_sum(send, [((s, f), (3 - s, f)) for s in shots for f in range(4) if (s, f) != (0, 3)])
    last = send_sum(last, [((1, 3), (3, 3))]) + send_sum(last, [((2, 3), (3, 3))])
    return jnp.where((shot == 3) & (freq == 3), last, image)


def split_body(source_field, receiver_field, operator, band_offsets, survey_tiles, survey_data):
    tiles = survey_data.shape[1]
    shot = lax.axis_index("shot")
    freq = lax.axis_index("freq")
    inner = ((shot == 1) | (shot == 2)).astype(jnp.int32)[None]
    offsets = band_offsets.T
    make = functools.partial(extrapolate_blocks, operator=operator[0])
    inward = ((0, 1), (3, 2))
    outward = ((1, 0), (2, 3))
    middle = ((1, 2), (2, 1))
    ends = ((0, 3), (3, 0))
    beyond = ((1, 3), (2, 0))

    far_data = hand(survey_data[0], *inward, *outward)
    (r_head,) = make(receiver_field[0], offsets=offsets, sets=[INNER[:HEAD]], listed=True)
    r_1_head = hand(r_head, *inward)
    r_3_head = hand(r_head, *middle)
    r_inner, r_outer = make(receiver_field[0], offsets=following(offsets, r_head), sets=[INNER[HEAD:], OUTER])
    r_3_in = hand(r_inner, *middle)
    r_1_in = hand(r_inner, *inward)
    r_1_out = hand(following(r_outer, far_data, r_3_head), *outward)
    s_inner, s_outer = make(
        source_field[0], offsets=following(offsets, r_outer, r_3_head), sets=[INNER, OUTER]
    )
    s_out = hand(following(s_outer, r_1_head), *outward)
    s_in = hand(s_inner, *inward)
    forward_head = hand(following(r_1_head, r_3_in), *middle)
    forward = hand(following(r_1_in, r_1_out), *middle)
    beyond_1 = hand(r_outer[:LATE], *beyond)
    r_3_out_1 = hand(following(r_outer, s_out, forward_head)[:HALF], *ends)
    r_3_out_2 = hand(r_outer[HALF:], *ends)
    beyond_2 = hand(r_outer[LATE:], *beyond)

    ids = survey_tiles[:, 1]
    near_ids = lax.dynamic_slice_in_dim(ids, shot * tiles, tiles)
    far_ids = lax.dynamic_slice_in_dim(ids, (shot ^ 1) * tiles, tiles)
    product = product_blocks(
        s_inner, s_outer, s_in, s_out, survey_data[0], far_data, near_ids, far_ids, inner
    )
    early = [
        (shot, [(r_head, 0, True), (r_inner, HEAD, True), (r_outer, 0, False)]),
        (shot ^ 1, [(r_1_head, 0, True), (r_1_in, HEAD, True), (r_1_out, 0, False)]),
        (shot ^ 3, [(r_3_head, 0, True), (r_3_in, HEAD, True), (r_3_out_1, 0, False), (r_3_out_2, HALF, False)]),
    ]
    forwarded = [(forward_head, 0, True), (forward, HEAD, True)]
    image = image_blocks(product, 0, len(INNER), early, inner)
    most = image_blocks(product, 0, LATE + 1, [(shot ^ 2, forwarded + [(beyond_1, 0, False)])], inner, image)
    rest = image_blocks(
        product, LATE + 1, len(INNER) - LATE - 1, [(shot ^ 2, forwarded + [(beyond_2, LATE, False)])], inner,
        following(image, most),
    )
    one = most[:FIRST]
    two = jnp.concatenate([most[FIRST:], rest])
    image = sum_images(one, two, shot, freq)
    total_freqs = source_field.shape[0] * lax.axis_size("freq")
    return image * (1.0 / math.sqrt(2.0 * NR * total_freqs))


def body(source_field, *rest):
    fits = (
        lax.axis_size("shot") == 4
        and lax.axis_size("freq") == 4
        and source_field.shape[1:] == (512, 16, 2, 128)
    )
    return (split_body if fits else general_body)(source_field, *rest)


def solution(mesh):
    return jax.shard_map(
        body,
        mesh=mesh,
        in_specs=(
            P("freq", ("groups", "shot"), None, None, None),
            P("freq", ("groups", "shot"), None, None, None),
            P("freq", "groups", None, None, None, None),
            P("groups", None),
            P("groups", None),
            P("freq", ("groups", "shot"), None, None, None),
        ),
        out_specs=P(None, ("groups", "shot", "freq"), None),
        check_vma=False,
    )
```

```python
import functools
import math

import jax
import jax.numpy as jnp
from jax import lax
from jax.experimental import pallas as pl
from jax.experimental.pallas import tpu as pltpu
from jax.sharding import PartitionSpec as P

NR = 2048
SMALL = pl.CostEstimate(flops=1000, bytes_accessed=1000, transcendentals=0)


def extrapolate(wavefield, operator, columns):
    row_count, blocks_x, components, block_size = wavefield.shape
    bands = columns.shape[1]
    real_part = operator[:, :, 0]
    imag_part = operator[:, :, 1]
    upper_rows = jnp.concatenate([real_part, imag_part], -1)
    lower_rows = jnp.concatenate([-imag_part, real_part], -1)
    real_block = jnp.concatenate([upper_rows, lower_rows], -2)
    real_block = real_block.reshape(blocks_x, bands, 2 * block_size, 2, block_size)
    chosen = jnp.take(wavefield, columns, axis=1).reshape(
        row_count, blocks_x, bands, 2 * block_size
    )
    result = jnp.einsum("sikc,ikcoy->soiy", chosen, real_block, preferred_element_type=jnp.float32)
    return result.astype(jnp.bfloat16)


def to_owners(wavefield, shot_count, own_cells):
    row_count = wavefield.shape[0]
    return wavefield.reshape(row_count, 2, shot_count, own_cells)


def to_tiles(wavefield, shot_count, own_cells):
    row_count, components, blocks_x, block_size = wavefield.shape
    if own_cells >= block_size:
        return to_owners(wavefield, shot_count, own_cells)
    factor = block_size // own_cells
    copies = jnp.broadcast_to(
        wavefield[:, :, :, None, :], (row_count, components, blocks_x, factor, block_size)
    )
    return copies.reshape(row_count, components, shot_count, block_size)


def data_product(source_cells, data_shard, survey_tiles, block_size, own_cells):
    source_count = source_cells.shape[0]
    receiver_blocks = NR // block_size
    blocks = source_cells.reshape(source_count // block_size, block_size, 2 * own_cells)
    block_ids = jnp.arange(receiver_blocks, dtype=jnp.int32)
    chosen = jnp.take(blocks, survey_tiles[:, 0], axis=0)
    products = jnp.einsum(
        "ncsr,nsk->ncrk",
        lax.all_gather(data_shard, "shot", axis=0, tiled=True),
        chosen,
        preferred_element_type=jnp.float32,
    )
    real_part = products[:, 0, :, :own_cells] - products[:, 1, :, own_cells:]
    imag_part = products[:, 0, :, own_cells:] + products[:, 1, :, :own_cells]
    contribution = jnp.concatenate([real_part, imag_part], -1)
    onehot = (survey_tiles[:, 1][:, None] == block_ids[None, :]).astype(jnp.float32)
    summed = jnp.einsum("nq,nrk->qrk", onehot, contribution, precision=lax.Precision.HIGHEST)
    return summed.reshape(NR, 2, own_cells).astype(jnp.bfloat16)


def image_tile(product, receiver_tile, block_size):
    row_count, components, own_cells = product.shape
    tiles_here = max(own_cells // block_size, 1)
    inner_cells = own_cells // tiles_here
    left = product.reshape(row_count, 2, tiles_here, inner_cells)
    right = receiver_tile.reshape(row_count, 2, tiles_here, block_size)
    turned = jnp.stack([-right[:, 1], right[:, 0]], 1)
    both = jnp.stack([right, turned], 1)
    result = jnp.einsum("rctx,rocty->otxy", left, both, preferred_element_type=jnp.float32)
    return result.reshape(2, own_cells, block_size)


def general_body(source_field, receiver_field, operator, band_offsets, survey_tiles, survey_data):
    shot_count = lax.axis_size("shot")
    freq_local = source_field.shape[0]
    blocks_x = source_field.shape[2]
    block_size = source_field.shape[4]
    own_cells = blocks_x * block_size // shot_count
    block_rows = jnp.arange(blocks_x, dtype=jnp.int32)[:, None]
    columns = (block_rows + band_offsets) % blocks_x
    source_next = extrapolate(source_field[0], operator[0], columns)
    receiver_next = extrapolate(receiver_field[0], operator[0], columns)
    source_send = to_owners(source_next, shot_count, own_cells)
    receiver_send = to_tiles(receiver_next, shot_count, own_cells)
    source_cells = lax.all_to_all(source_send, "shot", split_axis=2, concat_axis=0, tiled=True)
    receiver_tile = lax.all_to_all(receiver_send, "shot", split_axis=2, concat_axis=0, tiled=True)
    source_cells = source_cells.reshape(source_cells.shape[0], 2 * own_cells)
    product = data_product(source_cells, survey_data[0], survey_tiles, block_size, own_cells)
    receiver_tile = receiver_tile.reshape(receiver_tile.shape[0], 2, -1)
    image_sum = image_tile(product, receiver_tile, block_size)
    total_freqs = freq_local * lax.axis_size("freq")
    scaled = image_sum * (1.0 / math.sqrt(2.0 * NR * total_freqs))
    return lax.psum_scatter(scaled, "freq", scatter_dimension=1, tiled=True)


INNER = [4, 8, 6, 10, 15, 5, 9, 7, 11]
HEAD = 3
OUTER = [0, 12, 2, 14, 1, 13, 3]
FIRST = 5
OUTER_FIRST = 4
LATE = 6
HALF = 4


def outer_place(slot):
    return jnp.where(slot < FIRST, jnp.minimum(slot, OUTER_FIRST - 1), jnp.minimum(slot - 1, len(OUTER) - 1))


def params(limit=24):
    return pltpu.CompilerParams(vmem_limit_bytes=limit * 1024 * 1024)


def extrapolate_kernel(order, offsets, field, operator, *refs, sets, rows, blocks, parts, listed):
    stage, apart, lines, weights, field_sems, weight_sems = refs[-6:]
    outs = refs[:-6]
    sizes = [len(one) for one in sets]
    step = pl.program_id(0)
    bands = operator.shape[1]
    pitch = 2 * blocks + 1
    chunk = stage.shape[0] // pitch
    part_lines = lines.shape[0] // parts

    def column(block, band):
        return lax.rem(block + offsets[band, block] + blocks, blocks)

    def field_copy(part):
        here = pl.ds(part * part_lines, part_lines)
        return pltpu.make_async_copy(field.at[here], lines.at[here], field_sems.at[part])

    def weight_copy(n, block):
        return pltpu.make_async_copy(operator.at[block], weights.at[n], weight_sems.at[n])

    @pl.when(step == 0)
    def _():
        for part in range(parts):
            field_copy(part).start()
        for n, block in enumerate(sum(sets, [])):
            weight_copy(n, block).start()
        if listed:
            wanted = [column(block, band) for block in sum(sets, []) for band in range(bands)]
        else:
            wanted = list(range(blocks))

        def split(n, carry):
            for row in range(chunk):
                here = pl.ds(pl.multiple_of((n * chunk + row) * 2 * blocks, 2 * blocks), 2 * blocks)
                stage[pl.ds(row * pitch, 2 * blocks), :] = lines[here, :].astype(jnp.float32)
            to = pl.ds(pl.multiple_of(n * chunk, chunk), chunk)
            for slot, block in enumerate(wanted):
                for half in range(2):
                    picked = stage[pl.ds(2 * block + half, chunk, stride=pitch), :]
                    apart[slot, to, half * 128:(half + 1) * 128] = picked.astype(jnp.bfloat16)
            return carry

        steps = rows // chunk // parts
        for part in range(parts):
            field_copy(part).wait()
            lax.fori_loop(part * steps, (part + 1) * steps, split, 0)

    block = order[step]
    weight_copy(step, block).wait()
    inputs = []
    factors = []
    for band in range(bands):
        inputs.append(apart[step * bands + band if listed else column(block, band)])
        real = weights[step, band, 0]
        imag = weights[step, band, 1]
        factors.append(jnp.concatenate([real, imag], 1))
        factors.append(jnp.concatenate([-imag, real], 1))
    result = jnp.dot(
        jnp.concatenate(inputs, 1), jnp.concatenate(factors, 0), preferred_element_type=jnp.float32
    ).astype(jnp.bfloat16)
    first = 0
    for out, count in zip(outs, sizes):
        if len(sizes) == 1:
            out[0] = result
        else:
            @pl.when((step >= first) & (step < first + count))
            def _(out=out):
                out[0] = result
        first += count


def extrapolate_blocks(field, operator, offsets, sets, listed=False, limit=60):
    rows, blocks, _, size = field.shape
    bands = offsets.shape[0]
    width = 2 * size
    chunk = 32
    parts = 4
    sizes = [len(one) for one in sets]
    count = sum(sizes)
    order = jnp.array(sum(sets, []), jnp.int32)
    firsts = [sum(sizes[:n]) for n in range(len(sizes))]
    flat = field.reshape(rows * blocks * 2, size)

    def out_spec(first, count):
        return pl.BlockSpec((1, rows, width), lambda j, o, c: (jnp.clip(j - first, 0, count - 1), 0, 0))

    return pl.pallas_call(
        functools.partial(
            extrapolate_kernel, sets=sets, rows=rows, blocks=blocks, parts=parts, listed=listed
        ),
        grid_spec=pltpu.PrefetchScalarGridSpec(
            num_scalar_prefetch=2,
            grid=(count,),
            in_specs=[pl.BlockSpec(memory_space=pltpu.HBM)] * 2,
            out_specs=[out_spec(*one) for one in zip(firsts, sizes)],
            scratch_shapes=[
                pltpu.VMEM((chunk * (2 * blocks + 1), size), jnp.float32),
                pltpu.VMEM((count * bands if listed else blocks, rows, width), jnp.bfloat16),
                pltpu.VMEM(flat.shape, jnp.bfloat16),
                pltpu.VMEM((count,) + operator.shape[1:], jnp.bfloat16),
                pltpu.SemaphoreType.DMA((parts,)),
                pltpu.SemaphoreType.DMA((count,)),
            ],
        ),
        out_shape=[jax.ShapeDtypeStruct((n, rows, width), jnp.bfloat16) for n in sizes],
        compiler_params=params(limit),
        cost_estimate=SMALL,
        name="extrapolate",
    )(order, offsets, flat, operator)


def product_kernel(near_ids, far_ids, inner, near_in, near_out, far_in, far_out, near_data, far_data, out, turned, total):
    size = near_data.shape[2]
    tiles = near_data.shape[0]
    sources = near_in.shape[1] // size
    per_source = tiles // sources

    @pl.when(pl.program_id(0) == 0)
    def _():
        for side, data in enumerate((near_data, far_data)):
            for tile in range(tiles):
                for part in range(2):
                    turned[side * tiles + tile, :, part * size:(part + 1) * size] = data[tile, part].T

    total[...] = jnp.zeros_like(total)
    sides = ((near_in, near_out, near_ids), (far_in, far_out, far_ids))
    for side, (field_in, field_out, ids) in enumerate(sides):
        for source in range(sources):
            lines = slice(source * size, (source + 1) * size)
            upper = jnp.where(inner[0] > 0, field_in[0, lines, :], field_out[0, lines, :])
            lower = jnp.concatenate([-upper[:, size:], upper[:, :size]], 1)
            both = jnp.concatenate([upper, lower], 0)
            first = side * tiles + source * per_source
            left = turned[first:first + per_source].reshape(per_source * size, 2 * size)
            result = jnp.dot(left, both, preferred_element_type=jnp.float32)
            for tile in range(per_source):
                total[ids[source * per_source + tile]] += result[tile * size:(tile + 1) * size]
    for block in range(total.shape[0]):
        out[0, :, block * size:(block + 1) * size] = total[block].T.astype(jnp.bfloat16)


def part_spec(shape, first, begin, count, is_inner):
    def index(j, a, b, inner):
        place = first + j if is_inner else outer_place(first + j)
        place = jnp.clip(place - begin, 0, count - 1)
        return jnp.where((inner[0] > 0) == is_inner, place, 0), 0, 0

    return pl.BlockSpec(shape, index)


def product_blocks(near_in, near_out, far_in, far_out, near_data, far_data, near_ids, far_ids, inner):
    blocks, rows, width = near_in.shape
    tiles, _, size, _ = near_data.shape
    receivers = NR // size
    shape = (1, rows, width)
    data_spec = pl.BlockSpec(near_data.shape, lambda j, a, b, i: (0, 0, 0, 0))
    return pl.pallas_call(
        product_kernel,
        grid_spec=pltpu.PrefetchScalarGridSpec(
            num_scalar_prefetch=3,
            grid=(blocks,),
            in_specs=[part_spec(shape, 0, 0, len(INNER), True), part_spec(shape, 0, 0, len(OUTER), False)] * 2
            + [data_spec, data_spec],
            out_specs=pl.BlockSpec((1, width, NR), lambda j, a, b, i: (j, 0, 0)),
            scratch_shapes=[
                pltpu.VMEM((2 * tiles, size, width), jnp.bfloat16),
                pltpu.VMEM((receivers, size, width), jnp.float32),
            ],
        ),
        out_shape=jax.ShapeDtypeStruct((blocks, width, NR), jnp.bfloat16),
        compiler_params=params(),
        cost_estimate=SMALL,
        name="product",
    )(near_ids, far_ids, inner, near_in, near_out, far_in, far_out, near_data, far_data)


def image_kernel(places, unused, inner, *refs, first, begins, size):
    out = refs[-1]
    slot = first + pl.program_id(0)
    parts = refs[len(begins):]
    both = None
    for n, piece in enumerate(begins):
        field = parts[0][0]
        for part, (begin, is_inner) in zip(parts[1:], piece[1:]):
            place = slot if is_inner else outer_place(slot)
            field = jnp.where(((inner[0] > 0) == is_inner) & (place >= begin), part[0], field)
        parts = parts[len(piece):]
        term = jnp.dot(refs[n][0], field, preferred_element_type=jnp.float32)
        both = term if both is None else both + term
    real = both[:size, :size] + both[size:, size:]
    imag = both[size:, :size] - both[:size, size:]
    if len(parts) > 1:
        real += parts[0][0, 0]
        imag += parts[0][0, 1]
    out[0, 0] = real
    out[0, 1] = imag


def image_blocks(product, first, count, pieces, inner, before=None):
    _, rows, width = pieces[0][1][0][0].shape
    size = width // 2
    image_spec = pl.BlockSpec((1, 2, size, size), lambda j, o, u, i: (j, 0, 0, 0))
    specs = [
        pl.BlockSpec((1, width, rows), lambda j, o, u, i, n=n: (first + j, 0, o[n])) for n in range(len(pieces))
    ]
    values = [product] * len(pieces)
    begins = []
    for _, parts in pieces:
        for field, begin, is_inner in parts:
            specs.append(part_spec((1, rows, width), first, begin, field.shape[0], is_inner))
            values.append(field)
        begins.append([(begin, is_inner) for _, begin, is_inner in parts])
    if before is not None:
        specs.append(pl.BlockSpec((1, 2, size, size), lambda j, o, u, i: (first + j, 0, 0, 0)))
        values.append(before)
    places = jnp.stack([shot for shot, _ in pieces])
    return pl.pallas_call(
        functools.partial(image_kernel, first=first, begins=begins, size=size),
        grid_spec=pltpu.PrefetchScalarGridSpec(
            num_scalar_prefetch=3, grid=(count,), in_specs=specs, out_specs=image_spec
        ),
        out_shape=jax.ShapeDtypeStruct((count, 2, size, size), jnp.float32),
        compiler_params=params(),
        cost_estimate=SMALL,
        name="image",
    )(places, places, inner, *values)


def following(value, *earlier):
    return lax.optimization_barrier((value,) + earlier)[0]


def hand(value, *pairs):
    return lax.ppermute(value, "shot", pairs)


def send_sum(value, pairs):
    pairs = [(4 * a + b, 4 * c + d) for (a, b), (c, d) in pairs]
    return lax.ppermute(value.astype(jnp.bfloat16), ("shot", "freq"), pairs).astype(jnp.float32)


def sum_images(one, two, shot, freq):
    left = shot < 2
    shots = range(4)
    even = freq % 2 == 0
    low = freq < 2
    last = one[4:]
    one = one[:4]
    keep = jnp.where(even, jnp.concatenate([one, last]), jnp.concatenate([two, last]))
    send = jnp.where(even, jnp.concatenate([two, last]), jnp.concatenate([one, last]))
    image = keep + send_sum(send, [((s, f), (s, f ^ 1)) for s in shots for f in range(4)])
    keep = jnp.where(low, image[:2], image[2:4])
    send = jnp.where(low, image[2:4], image[:2])
    last = image[4] + send_sum(image[4], [((s, 1), (s, 3)) for s in (1, 2)])
    image = keep + send_sum(send, [((s, f), (s, f ^ 2)) for s in shots for f in range(4)])
    keep = jnp.where(left, image[0], image[1])
    send = jnp.where(left, image[1], image[0])
    image = keep + send_sum(send, [((s, f), (3 - s, f)) for s in shots for f in range(4) if (s, f) != (0, 3)])
    last = send_sum(last, [((1, 3), (3, 3))]) + send_sum(last, [((2, 3), (3, 3))])
    return jnp.where((shot == 3) & (freq == 3), last, image)


def split_body(source_field, receiver_field, operator, band_offsets, survey_tiles, survey_data):
    tiles = survey_data.shape[1]
    shot = lax.axis_index("shot")
    freq = lax.axis_index("freq")
    inner = ((shot == 1) | (shot == 2)).astype(jnp.int32)[None]
    offsets = band_offsets.T
    make = functools.partial(extrapolate_blocks, operator=operator[0])
    inward = ((0, 1), (3, 2))
    outward = ((1, 0), (2, 3))
    middle = ((1, 2), (2, 1))
    ends = ((0, 3), (3, 0))
    beyond = ((1, 3), (2, 0))

    far_data = hand(survey_data[0], *inward, *outward)
    (r_head,) = make(receiver_field[0], offsets=offsets, sets=[INNER[:HEAD]], listed=True)
    r_1_head = hand(r_head, *inward)
    r_3_head = hand(r_head, *middle)
    r_inner, r_outer = make(receiver_field[0], offsets=following(offsets, r_head), sets=[INNER[HEAD:], OUTER])
    r_3_in = hand(r_inner, *middle)
    r_1_in = hand(r_inner, *inward)
    r_1_out = hand(following(r_outer, far_data, r_3_head), *outward)
    s_inner, s_outer = make(
        source_field[0], offsets=following(offsets, r_outer, r_3_head), sets=[INNER, OUTER]
    )
    s_out = hand(following(s_outer, r_1_head), *outward)
    s_in = hand(s_inner, *inward)
    forward_head = hand(following(r_1_head, r_3_in), *middle)
    beyond_1 = hand(r_outer[:LATE], *beyond)
    forward = hand(following(r_1_in, r_1_out, beyond_1), *middle)
    r_3_out_1 = hand(following(r_outer, forward_head)[:HALF], *ends)
    r_3_out_2 = hand(r_outer[HALF:], *ends)
    beyond_2 = hand(r_outer[LATE:], *beyond)

    ids = survey_tiles[:, 1]
    near_ids = lax.dynamic_slice_in_dim(ids, shot * tiles, tiles)
    far_ids = lax.dynamic_slice_in_dim(ids, (shot ^ 1) * tiles, tiles)
    product = product_blocks(
        s_inner, s_outer, s_in, s_out, survey_data[0], far_data, near_ids, far_ids, inner
    )
    early = [
        (shot, [(r_head, 0, True), (r_inner, HEAD, True), (r_outer, 0, False)]),
        (shot ^ 1, [(r_1_head, 0, True), (r_1_in, HEAD, True), (r_1_out, 0, False)]),
        (shot ^ 3, [(r_3_head, 0, True), (r_3_in, HEAD, True), (r_3_out_1, 0, False), (r_3_out_2, HALF, False)]),
    ]
    forwarded = [(forward_head, 0, True), (forward, HEAD, True)]
    image = image_blocks(product, 0, len(INNER), early, inner)
    most = image_blocks(product, 0, LATE + 1, [(shot ^ 2, forwarded + [(beyond_1, 0, False)])], inner, image)
    rest = image_blocks(
        product, LATE + 1, len(INNER) - LATE - 1, [(shot ^ 2, forwarded + [(beyond_2, LATE, False)])], inner,
        following(image, most),
    )
    one = most[:FIRST]
    two = jnp.concatenate([most[FIRST:], rest])
    image = sum_images(one, two, shot, freq)
    total_freqs = source_field.shape[0] * lax.axis_size("freq")
    return image * (1.0 / math.sqrt(2.0 * NR * total_freqs))


def body(source_field, *rest):
    fits = (
        lax.axis_size("shot") == 4
        and lax.axis_size("freq") == 4
        and source_field.shape[1:] == (512, 16, 2, 128)
    )
    return (split_body if fits else general_body)(source_field, *rest)


def solution(mesh):
    return jax.shard_map(
        body,
        mesh=mesh,
        in_specs=(
            P("freq", ("groups", "shot"), None, None, None),
            P("freq", ("groups", "shot"), None, None, None),
            P("freq", "groups", None, None, None, None),
            P("groups", None),
            P("groups", None),
            P("freq", ("groups", "shot"), None, None, None),
        ),
        out_specs=P(None, ("groups", "shot", "freq"), None),
        check_vma=False,
    )
```

```python
import functools
import math

import jax
import jax.numpy as jnp
from jax import lax
from jax.experimental import pallas as pl
from jax.experimental.pallas import tpu as pltpu
from jax.sharding import PartitionSpec as P

NR = 2048
SMALL = pl.CostEstimate(flops=1000, bytes_accessed=1000, transcendentals=0)


def extrapolate(wavefield, operator, columns):
    row_count, blocks_x, components, block_size = wavefield.shape
    bands = columns.shape[1]
    real_part = operator[:, :, 0]
    imag_part = operator[:, :, 1]
    upper_rows = jnp.concatenate([real_part, imag_part], -1)
    lower_rows = jnp.concatenate([-imag_part, real_part], -1)
    real_block = jnp.concatenate([upper_rows, lower_rows], -2)
    real_block = real_block.reshape(blocks_x, bands, 2 * block_size, 2, block_size)
    chosen = jnp.take(wavefield, columns, axis=1).reshape(
        row_count, blocks_x, bands, 2 * block_size
    )
    result = jnp.einsum("sikc,ikcoy->soiy", chosen, real_block, preferred_element_type=jnp.float32)
    return result.astype(jnp.bfloat16)


def to_owners(wavefield, shot_count, own_cells):
    row_count = wavefield.shape[0]
    return wavefield.reshape(row_count, 2, shot_count, own_cells)


def to_tiles(wavefield, shot_count, own_cells):
    row_count, components, blocks_x, block_size = wavefield.shape
    if own_cells >= block_size:
        return to_owners(wavefield, shot_count, own_cells)
    factor = block_size // own_cells
    copies = jnp.broadcast_to(
        wavefield[:, :, :, None, :], (row_count, components, blocks_x, factor, block_size)
    )
    return copies.reshape(row_count, components, shot_count, block_size)


def data_product(source_cells, data_shard, survey_tiles, block_size, own_cells):
    source_count = source_cells.shape[0]
    receiver_blocks = NR // block_size
    blocks = source_cells.reshape(source_count // block_size, block_size, 2 * own_cells)
    block_ids = jnp.arange(receiver_blocks, dtype=jnp.int32)
    chosen = jnp.take(blocks, survey_tiles[:, 0], axis=0)
    products = jnp.einsum(
        "ncsr,nsk->ncrk",
        lax.all_gather(data_shard, "shot", axis=0, tiled=True),
        chosen,
        preferred_element_type=jnp.float32,
    )
    real_part = products[:, 0, :, :own_cells] - products[:, 1, :, own_cells:]
    imag_part = products[:, 0, :, own_cells:] + products[:, 1, :, :own_cells]
    contribution = jnp.concatenate([real_part, imag_part], -1)
    onehot = (survey_tiles[:, 1][:, None] == block_ids[None, :]).astype(jnp.float32)
    summed = jnp.einsum("nq,nrk->qrk", onehot, contribution, precision=lax.Precision.HIGHEST)
    return summed.reshape(NR, 2, own_cells).astype(jnp.bfloat16)


def image_tile(product, receiver_tile, block_size):
    row_count, components, own_cells = product.shape
    tiles_here = max(own_cells // block_size, 1)
    inner_cells = own_cells // tiles_here
    left = product.reshape(row_count, 2, tiles_here, inner_cells)
    right = receiver_tile.reshape(row_count, 2, tiles_here, block_size)
    turned = jnp.stack([-right[:, 1], right[:, 0]], 1)
    both = jnp.stack([right, turned], 1)
    result = jnp.einsum("rctx,rocty->otxy", left, both, preferred_element_type=jnp.float32)
    return result.reshape(2, own_cells, block_size)


def general_body(source_field, receiver_field, operator, band_offsets, survey_tiles, survey_data):
    shot_count = lax.axis_size("shot")
    freq_local = source_field.shape[0]
    blocks_x = source_field.shape[2]
    block_size = source_field.shape[4]
    own_cells = blocks_x * block_size // shot_count
    block_rows = jnp.arange(blocks_x, dtype=jnp.int32)[:, None]
    columns = (block_rows + band_offsets) % blocks_x
    source_next = extrapolate(source_field[0], operator[0], columns)
    receiver_next = extrapolate(receiver_field[0], operator[0], columns)
    source_send = to_owners(source_next, shot_count, own_cells)
    receiver_send = to_tiles(receiver_next, shot_count, own_cells)
    source_cells = lax.all_to_all(source_send, "shot", split_axis=2, concat_axis=0, tiled=True)
    receiver_tile = lax.all_to_all(receiver_send, "shot", split_axis=2, concat_axis=0, tiled=True)
    source_cells = source_cells.reshape(source_cells.shape[0], 2 * own_cells)
    product = data_product(source_cells, survey_data[0], survey_tiles, block_size, own_cells)
    receiver_tile = receiver_tile.reshape(receiver_tile.shape[0], 2, -1)
    image_sum = image_tile(product, receiver_tile, block_size)
    total_freqs = freq_local * lax.axis_size("freq")
    scaled = image_sum * (1.0 / math.sqrt(2.0 * NR * total_freqs))
    return lax.psum_scatter(scaled, "freq", scatter_dimension=1, tiled=True)


INNER = [4, 8, 6, 10, 15, 5, 9, 7, 11]
HEAD = 3
OUTER = [0, 12, 2, 14, 1, 13, 3]
FIRST = 5
OUTER_FIRST = 4
LATE = 5
SWAP = len(OUTER)
HALF = 4


def outer_place(slot):
    return jnp.where(slot < FIRST, jnp.minimum(slot, OUTER_FIRST - 1), jnp.minimum(slot - 1, len(OUTER) - 1))


def params(limit=24):
    return pltpu.CompilerParams(vmem_limit_bytes=limit * 1024 * 1024)


def extrapolate_kernel(order, offsets, inner, field, operator, *refs, sets, rows, blocks, parts, listed, swap):
    stage, apart, lines, weights, field_sems, weight_sems = refs[-6:]
    outs = refs[:-6]
    sizes = [len(one) for one in sets]
    step = pl.program_id(0)
    bands = operator.shape[1]
    pitch = 2 * blocks + 1
    chunk = stage.shape[0] // pitch
    part_lines = lines.shape[0] // parts

    def column(block, band):
        return lax.rem(block + offsets[band, block] + blocks, blocks)

    def field_copy(part):
        here = pl.ds(part * part_lines, part_lines)
        return pltpu.make_async_copy(field.at[here], lines.at[here], field_sems.at[part])

    def weight_copy(n, block):
        return pltpu.make_async_copy(operator.at[block], weights.at[n], weight_sems.at[n])

    @pl.when(step == 0)
    def _():
        for part in range(parts):
            field_copy(part).start()
        for n, block in enumerate(sum(sets, [])):
            weight_copy(n, block).start()
        if listed:
            wanted = [column(block, band) for block in sum(sets, []) for band in range(bands)]
        else:
            wanted = list(range(blocks))

        def split(n, carry):
            for row in range(chunk):
                here = pl.ds(pl.multiple_of((n * chunk + row) * 2 * blocks, 2 * blocks), 2 * blocks)
                stage[pl.ds(row * pitch, 2 * blocks), :] = lines[here, :].astype(jnp.float32)
            to = pl.ds(pl.multiple_of(n * chunk, chunk), chunk)
            for slot, block in enumerate(wanted):
                for half in range(2):
                    picked = stage[pl.ds(2 * block + half, chunk, stride=pitch), :]
                    apart[slot, to, half * 128:(half + 1) * 128] = picked.astype(jnp.bfloat16)
            return carry

        steps = rows // chunk // parts
        for part in range(parts):
            field_copy(part).wait()
            lax.fori_loop(part * steps, (part + 1) * steps, split, 0)

    block = order[step]
    weight_copy(step, block).wait()
    inputs = []
    factors = []
    for band in range(bands):
        inputs.append(apart[step * bands + band if listed else column(block, band)])
        real = weights[step, band, 0]
        imag = weights[step, band, 1]
        factors.append(jnp.concatenate([real, imag], 1))
        factors.append(jnp.concatenate([-imag, real], 1))
    result = jnp.dot(
        jnp.concatenate(inputs, 1), jnp.concatenate(factors, 0), preferred_element_type=jnp.float32
    ).astype(jnp.bfloat16)
    first = 0
    for out, count in zip(outs, sizes):
        if len(sizes) == 1:
            out[0] = result
        else:
            @pl.when((step >= first) & (step < first + count))
            def _(out=out):
                out[0] = result
        first += count
    if swap:
        @pl.when(jnp.where(inner[0] > 0, (step >= sizes[0]) & (step < 2 * sizes[0]), step < sizes[0]))
        def _():
            outs[-1][0] = result


def extrapolate_blocks(field, operator, offsets, inner, sets, listed=False, swap=False, limit=60):
    rows, blocks, _, size = field.shape
    bands = offsets.shape[0]
    width = 2 * size
    chunk = 32
    parts = 4
    sizes = [len(one) for one in sets]
    count = sum(sizes)
    order = jnp.array(sum(sets, []), jnp.int32)
    firsts = [sum(sizes[:n]) for n in range(len(sizes))]
    flat = field.reshape(rows * blocks * 2, size)

    def out_spec(first, count):
        return pl.BlockSpec((1, rows, width), lambda j, o, c, i: (jnp.clip(j - first, 0, count - 1), 0, 0))

    def swap_place(j, o, c, i):
        return jnp.clip(j - jnp.where(i[0] > 0, sizes[0], 0), 0, sizes[0] - 1), 0, 0

    out_specs = [out_spec(*one) for one in zip(firsts, sizes)]
    if swap:
        out_specs.append(pl.BlockSpec((1, rows, width), swap_place))
    return pl.pallas_call(
        functools.partial(
            extrapolate_kernel, sets=sets, rows=rows, blocks=blocks, parts=parts, listed=listed, swap=swap
        ),
        grid_spec=pltpu.PrefetchScalarGridSpec(
            num_scalar_prefetch=3,
            grid=(count,),
            in_specs=[pl.BlockSpec(memory_space=pltpu.HBM)] * 2,
            out_specs=out_specs,
            scratch_shapes=[
                pltpu.VMEM((chunk * (2 * blocks + 1), size), jnp.float32),
                pltpu.VMEM((count * bands if listed else blocks, rows, width), jnp.bfloat16),
                pltpu.VMEM(flat.shape, jnp.bfloat16),
                pltpu.VMEM((count,) + operator.shape[1:], jnp.bfloat16),
                pltpu.SemaphoreType.DMA((parts,)),
                pltpu.SemaphoreType.DMA((count,)),
            ],
        ),
        out_shape=[jax.ShapeDtypeStruct((n, rows, width), jnp.bfloat16) for n in sizes + sizes[:1] * swap],
        compiler_params=params(limit),
        cost_estimate=SMALL,
        name="extrapolate",
    )(order, offsets, inner, flat, operator)


def chosen(refs, begins, slot, inner):
    field = refs[0][0]
    for part, (begin, is_inner) in zip(refs[1:], begins[1:]):
        place = slot if is_inner else outer_place(slot)
        field = jnp.where(((inner[0] > 0) == is_inner) & (place >= begin), part[0], field)
    return field


def product_kernel(near_ids, far_ids, inner, *refs, begins):
    near_data, far_data, out, turned, total = refs[-5:]
    size = near_data.shape[2]
    tiles = near_data.shape[0]
    sources = refs[0].shape[1] // size
    per_source = tiles // sources

    @pl.when(pl.program_id(0) == 0)
    def _():
        for side, data in enumerate((near_data, far_data)):
            for tile in range(tiles):
                for part in range(2):
                    turned[side * tiles + tile, :, part * size:(part + 1) * size] = data[tile, part].T

    total[...] = jnp.zeros_like(total)
    for side, ids in enumerate((near_ids, far_ids)):
        first = len(begins[0]) * side
        field = chosen(refs[first:first + len(begins[side])], begins[side], pl.program_id(0), inner)
        for source in range(sources):
            upper = field[source * size:(source + 1) * size, :]
            lower = jnp.concatenate([-upper[:, size:], upper[:, :size]], 1)
            both = jnp.concatenate([upper, lower], 0)
            first = side * tiles + source * per_source
            left = turned[first:first + per_source].reshape(per_source * size, 2 * size)
            result = jnp.dot(left, both, preferred_element_type=jnp.float32)
            for tile in range(per_source):
                total[ids[source * per_source + tile]] += result[tile * size:(tile + 1) * size]
    for block in range(total.shape[0]):
        out[0, :, block * size:(block + 1) * size] = total[block].T.astype(jnp.bfloat16)


def part_spec(shape, first, begin, count, is_inner):
    def index(j, a, b, inner):
        place = first + j if is_inner else outer_place(first + j)
        place = jnp.clip(place - begin, 0, count - 1)
        return jnp.where((inner[0] > 0) == is_inner, place, 0), 0, 0

    return pl.BlockSpec(shape, index)


def product_blocks(near, far, near_data, far_data, near_ids, far_ids, inner):
    blocks = len(INNER)
    _, rows, width = near[0][0].shape
    tiles, _, size, _ = near_data.shape
    receivers = NR // size
    parts = near + far
    begins = [[part[1:] for part in side] for side in (near, far)]
    data_spec = pl.BlockSpec(near_data.shape, lambda j, a, b, i: (0, 0, 0, 0))
    return pl.pallas_call(
        functools.partial(product_kernel, begins=begins),
        grid_spec=pltpu.PrefetchScalarGridSpec(
            num_scalar_prefetch=3,
            grid=(blocks,),
            in_specs=[
                part_spec((1, rows, width), 0, begin, field.shape[0], is_inner) for field, begin, is_inner in parts
            ]
            + [data_spec, data_spec],
            out_specs=pl.BlockSpec((1, width, NR), lambda j, a, b, i: (j, 0, 0)),
            scratch_shapes=[
                pltpu.VMEM((2 * tiles, size, width), jnp.bfloat16),
                pltpu.VMEM((receivers, size, width), jnp.float32),
            ],
        ),
        out_shape=jax.ShapeDtypeStruct((blocks, width, NR), jnp.bfloat16),
        compiler_params=params(),
        cost_estimate=SMALL,
        name="product",
    )(near_ids, far_ids, inner, *[field for field, _, _ in parts], near_data, far_data)


def image_kernel(places, unused, inner, *refs, first, begins, size):
    out = refs[-1]
    slot = first + pl.program_id(0)
    parts = refs[len(begins):]
    both = None
    for n, piece in enumerate(begins):
        field = parts[0][0]
        for part, (begin, is_inner) in zip(parts[1:], piece[1:]):
            place = slot if is_inner else outer_place(slot)
            field = jnp.where(((inner[0] > 0) == is_inner) & (place >= begin), part[0], field)
        parts = parts[len(piece):]
        term = jnp.dot(refs[n][0], field, preferred_element_type=jnp.float32)
        both = term if both is None else both + term
    real = both[:size, :size] + both[size:, size:]
    imag = both[size:, :size] - both[:size, size:]
    if len(parts) > 1:
        real += parts[0][0, 0]
        imag += parts[0][0, 1]
    out[0, 0] = real
    out[0, 1] = imag


def image_blocks(product, first, count, pieces, inner, before=None):
    _, rows, width = pieces[0][1][0][0].shape
    size = width // 2
    image_spec = pl.BlockSpec((1, 2, size, size), lambda j, o, u, i: (j, 0, 0, 0))
    specs = [
        pl.BlockSpec((1, width, rows), lambda j, o, u, i, n=n: (first + j, 0, o[n])) for n in range(len(pieces))
    ]
    values = [product] * len(pieces)
    begins = []
    for _, parts in pieces:
        for field, begin, is_inner in parts:
            specs.append(part_spec((1, rows, width), first, begin, field.shape[0], is_inner))
            values.append(field)
        begins.append([(begin, is_inner) for _, begin, is_inner in parts])
    if before is not None:
        specs.append(pl.BlockSpec((1, 2, size, size), lambda j, o, u, i: (first + j, 0, 0, 0)))
        values.append(before)
    places = jnp.stack([shot for shot, _ in pieces])
    return pl.pallas_call(
        functools.partial(image_kernel, first=first, begins=begins, size=size),
        grid_spec=pltpu.PrefetchScalarGridSpec(
            num_scalar_prefetch=3, grid=(count,), in_specs=specs, out_specs=image_spec
        ),
        out_shape=jax.ShapeDtypeStruct((count, 2, size, size), jnp.float32),
        compiler_params=params(),
        cost_estimate=SMALL,
        name="image",
    )(places, places, inner, *values)


def following(value, *earlier):
    return lax.optimization_barrier((value,) + earlier)[0]


def hand(value, *pairs):
    return lax.ppermute(value, "shot", pairs)


def send_sum(value, pairs):
    pairs = [(4 * a + b, 4 * c + d) for (a, b), (c, d) in pairs]
    return lax.ppermute(value.astype(jnp.bfloat16), ("shot", "freq"), pairs).astype(jnp.float32)


def sum_images(one, two, shot, freq):
    left = shot < 2
    shots = range(4)
    even = freq % 2 == 0
    low = freq < 2
    last = one[4:]
    one = one[:4]
    keep = jnp.where(even, jnp.concatenate([one, last]), jnp.concatenate([two, last]))
    send = jnp.where(even, jnp.concatenate([two, last]), jnp.concatenate([one, last]))
    image = keep + send_sum(send, [((s, f), (s, f ^ 1)) for s in shots for f in range(4)])
    keep = jnp.where(low, image[:2], image[2:4])
    send = jnp.where(low, image[2:4], image[:2])
    last = image[4] + send_sum(image[4], [((s, 1), (s, 3)) for s in (1, 2)])
    image = keep + send_sum(send, [((s, f), (s, f ^ 2)) for s in shots for f in range(4)])
    keep = jnp.where(left, image[0], image[1])
    send = jnp.where(left, image[1], image[0])
    image = keep + send_sum(send, [((s, f), (3 - s, f)) for s in shots for f in range(4) if (s, f) != (0, 3)])
    last = send_sum(last, [((1, 3), (3, 3))]) + send_sum(last, [((2, 3), (3, 3))])
    return jnp.where((shot == 3) & (freq == 3), last, image)


def split_body(source_field, receiver_field, operator, band_offsets, survey_tiles, survey_data):
    tiles = survey_data.shape[1]
    shot = lax.axis_index("shot")
    freq = lax.axis_index("freq")
    inner = ((shot == 1) | (shot == 2)).astype(jnp.int32)[None]
    offsets = band_offsets.T
    make = functools.partial(extrapolate_blocks, operator=operator[0], inner=inner)
    inward = ((0, 1), (3, 2))
    outward = ((1, 0), (2, 3))
    middle = ((1, 2), (2, 1))
    ends = ((0, 3), (3, 0))
    beyond = ((1, 3), (2, 0))

    far_data = hand(survey_data[0], *inward, *outward)
    (r_head,) = make(receiver_field[0], offsets=offsets, sets=[INNER[:HEAD]], listed=True)
    r_1_head = hand(r_head, *inward)
    r_3_head = hand(r_head, *middle)
    r_inner, r_outer = make(receiver_field[0], offsets=following(offsets, r_head), sets=[INNER[HEAD:], OUTER])
    r_3_in = hand(r_inner, *middle)
    r_1_in = hand(r_inner, *inward)
    r_1_out = hand(following(r_outer, far_data, r_3_head), *outward)
    s_inner, s_outer, s_rest, s_swap = make(
        source_field[0],
        offsets=following(offsets, r_outer, r_3_head),
        sets=[INNER[:SWAP], OUTER, INNER[SWAP:]],
        swap=True,
    )
    s_far = hand(following(s_swap, r_1_head), *inward, *outward)
    forward_head = hand(r_1_head, *middle)
    s_rest_far = hand(following(s_rest, r_3_in), *inward)
    forward = hand(r_1_in, *middle)
    beyond_1 = hand(following(r_outer, r_1_out)[:LATE], *beyond)
    r_3_out_1 = hand(following(r_outer, s_far, s_rest_far, forward_head)[:HALF], *ends)
    r_3_out_2 = hand(r_outer[HALF:], *ends)
    beyond_2 = hand(r_outer[LATE:], *beyond)

    ids = survey_tiles[:, 1]
    near_ids = lax.dynamic_slice_in_dim(ids, shot * tiles, tiles)
    far_ids = lax.dynamic_slice_in_dim(ids, (shot ^ 1) * tiles, tiles)
    near = [(s_inner, 0, True), (s_rest, SWAP, True), (s_outer, 0, False)]
    far = [(s_far, 0, True), (s_rest_far, SWAP, True), (s_far, 0, False)]
    product = product_blocks(near, far, survey_data[0], far_data, near_ids, far_ids, inner)
    early = [
        (shot, [(r_head, 0, True), (r_inner, HEAD, True), (r_outer, 0, False)]),
        (shot ^ 1, [(r_1_head, 0, True), (r_1_in, HEAD, True), (r_1_out, 0, False)]),
        (shot ^ 3, [(r_3_head, 0, True), (r_3_in, HEAD, True), (r_3_out_1, 0, False), (r_3_out_2, HALF, False)]),
    ]
    forwarded = [(forward_head, 0, True), (forward, HEAD, True)]
    image = image_blocks(product, 0, len(INNER), early, inner)
    most = image_blocks(product, 0, LATE + 1, [(shot ^ 2, forwarded + [(beyond_1, 0, False)])], inner, image)
    rest = image_blocks(
        product, LATE + 1, len(INNER) - LATE - 1, [(shot ^ 2, forwarded + [(beyond_2, LATE, False)])], inner,
        following(image, most),
    )
    one = most[:FIRST]
    two = jnp.concatenate([most[FIRST:], rest])
    image = sum_images(one, two, shot, freq)
    total_freqs = source_field.shape[0] * lax.axis_size("freq")
    return image * (1.0 / math.sqrt(2.0 * NR * total_freqs))


def body(source_field, *rest):
    fits = (
        lax.axis_size("shot") == 4
        and lax.axis_size("freq") == 4
        and source_field.shape[1:] == (512, 16, 2, 128)
    )
    return (split_body if fits else general_body)(source_field, *rest)


def solution(mesh):
    return jax.shard_map(
        body,
        mesh=mesh,
        in_specs=(
            P("freq", ("groups", "shot"), None, None, None),
            P("freq", ("groups", "shot"), None, None, None),
            P("freq", "groups", None, None, None, None),
            P("groups", None),
            P("groups", None),
            P("freq", ("groups", "shot"), None, None, None),
        ),
        out_specs=P(None, ("groups", "shot", "freq"), None),
        check_vma=False,
    )
```

```python
import functools
import math

import jax
import jax.numpy as jnp
from jax import lax
from jax.experimental import pallas as pl
from jax.experimental.pallas import tpu as pltpu
from jax.sharding import PartitionSpec as P

NR = 2048
SMALL = pl.CostEstimate(flops=1000, bytes_accessed=1000, transcendentals=0)


def extrapolate(wavefield, operator, columns):
    row_count, blocks_x, components, block_size = wavefield.shape
    bands = columns.shape[1]
    real_part = operator[:, :, 0]
    imag_part = operator[:, :, 1]
    upper_rows = jnp.concatenate([real_part, imag_part], -1)
    lower_rows = jnp.concatenate([-imag_part, real_part], -1)
    real_block = jnp.concatenate([upper_rows, lower_rows], -2)
    real_block = real_block.reshape(blocks_x, bands, 2 * block_size, 2, block_size)
    chosen = jnp.take(wavefield, columns, axis=1).reshape(
        row_count, blocks_x, bands, 2 * block_size
    )
    result = jnp.einsum("sikc,ikcoy->soiy", chosen, real_block, preferred_element_type=jnp.float32)
    return result.astype(jnp.bfloat16)


def to_owners(wavefield, shot_count, own_cells):
    row_count = wavefield.shape[0]
    return wavefield.reshape(row_count, 2, shot_count, own_cells)


def to_tiles(wavefield, shot_count, own_cells):
    row_count, components, blocks_x, block_size = wavefield.shape
    if own_cells >= block_size:
        return to_owners(wavefield, shot_count, own_cells)
    factor = block_size // own_cells
    copies = jnp.broadcast_to(
        wavefield[:, :, :, None, :], (row_count, components, blocks_x, factor, block_size)
    )
    return copies.reshape(row_count, components, shot_count, block_size)


def data_product(source_cells, data_shard, survey_tiles, block_size, own_cells):
    source_count = source_cells.shape[0]
    receiver_blocks = NR // block_size
    blocks = source_cells.reshape(source_count // block_size, block_size, 2 * own_cells)
    block_ids = jnp.arange(receiver_blocks, dtype=jnp.int32)
    chosen = jnp.take(blocks, survey_tiles[:, 0], axis=0)
    products = jnp.einsum(
        "ncsr,nsk->ncrk",
        lax.all_gather(data_shard, "shot", axis=0, tiled=True),
        chosen,
        preferred_element_type=jnp.float32,
    )
    real_part = products[:, 0, :, :own_cells] - products[:, 1, :, own_cells:]
    imag_part = products[:, 0, :, own_cells:] + products[:, 1, :, :own_cells]
    contribution = jnp.concatenate([real_part, imag_part], -1)
    onehot = (survey_tiles[:, 1][:, None] == block_ids[None, :]).astype(jnp.float32)
    summed = jnp.einsum("nq,nrk->qrk", onehot, contribution, precision=lax.Precision.HIGHEST)
    return summed.reshape(NR, 2, own_cells).astype(jnp.bfloat16)


def image_tile(product, receiver_tile, block_size):
    row_count, components, own_cells = product.shape
    tiles_here = max(own_cells // block_size, 1)
    inner_cells = own_cells // tiles_here
    left = product.reshape(row_count, 2, tiles_here, inner_cells)
    right = receiver_tile.reshape(row_count, 2, tiles_here, block_size)
    turned = jnp.stack([-right[:, 1], right[:, 0]], 1)
    both = jnp.stack([right, turned], 1)
    result = jnp.einsum("rctx,rocty->otxy", left, both, preferred_element_type=jnp.float32)
    return result.reshape(2, own_cells, block_size)


def general_body(source_field, receiver_field, operator, band_offsets, survey_tiles, survey_data):
    shot_count = lax.axis_size("shot")
    freq_local = source_field.shape[0]
    blocks_x = source_field.shape[2]
    block_size = source_field.shape[4]
    own_cells = blocks_x * block_size // shot_count
    block_rows = jnp.arange(blocks_x, dtype=jnp.int32)[:, None]
    columns = (block_rows + band_offsets) % blocks_x
    source_next = extrapolate(source_field[0], operator[0], columns)
    receiver_next = extrapolate(receiver_field[0], operator[0], columns)
    source_send = to_owners(source_next, shot_count, own_cells)
    receiver_send = to_tiles(receiver_next, shot_count, own_cells)
    source_cells = lax.all_to_all(source_send, "shot", split_axis=2, concat_axis=0, tiled=True)
    receiver_tile = lax.all_to_all(receiver_send, "shot", split_axis=2, concat_axis=0, tiled=True)
    source_cells = source_cells.reshape(source_cells.shape[0], 2 * own_cells)
    product = data_product(source_cells, survey_data[0], survey_tiles, block_size, own_cells)
    receiver_tile = receiver_tile.reshape(receiver_tile.shape[0], 2, -1)
    image_sum = image_tile(product, receiver_tile, block_size)
    total_freqs = freq_local * lax.axis_size("freq")
    scaled = image_sum * (1.0 / math.sqrt(2.0 * NR * total_freqs))
    return lax.psum_scatter(scaled, "freq", scatter_dimension=1, tiled=True)


INNER = [4, 8, 6, 10, 15, 5, 9, 7, 11]
HEAD = 3
OUTER = [0, 12, 2, 14, 1, 13, 3]
FIRST = 5
OUTER_FIRST = 4
LATE = 5
SWAP = len(OUTER)
HALF = 4


def outer_place(slot):
    return jnp.where(slot < FIRST, jnp.minimum(slot, OUTER_FIRST - 1), jnp.minimum(slot - 1, len(OUTER) - 1))


def params(limit=24):
    return pltpu.CompilerParams(vmem_limit_bytes=limit * 1024 * 1024)


def extrapolate_kernel(order, offsets, inner, field, operator, *refs, sets, rows, blocks, parts, listed, swap):
    stage, apart, lines, weights, field_sems, weight_sems = refs[-6:]
    outs = refs[:-6]
    sizes = [len(one) for one in sets]
    step = pl.program_id(0)
    bands = operator.shape[1]
    pitch = 2 * blocks + 1
    chunk = stage.shape[0] // pitch - 1
    part_lines = lines.shape[0] // parts

    def column(block, band):
        return lax.rem(block + offsets[band, block] + blocks, blocks)

    def field_copy(part):
        here = pl.ds(part * part_lines, part_lines)
        return pltpu.make_async_copy(field.at[here], lines.at[here], field_sems.at[part])

    def weight_copy(n, block):
        return pltpu.make_async_copy(operator.at[block], weights.at[n], weight_sems.at[n])

    @pl.when(step == 0)
    def _():
        for part in range(parts):
            field_copy(part).start()
        for n, block in enumerate(sum(sets, [])):
            weight_copy(n, block).start()
        if listed:
            wanted = [column(block, band) for block in sum(sets, []) for band in range(bands)]
        else:
            wanted = list(range(blocks))

        def split(n, carry):
            for row in range(chunk):
                here = pl.ds(pl.multiple_of((n * chunk + row) * 2 * blocks, 2 * blocks), 2 * blocks)
                stage[pl.ds(row * pitch, 2 * blocks), :] = lines[here, :].astype(jnp.float32)
            to = pl.ds(pl.multiple_of(n * chunk, chunk), chunk)
            for slot, block in enumerate(wanted):
                for half in range(2):
                    picked = stage[pl.ds(2 * block + half, chunk, stride=pitch), :]
                    apart[slot, to, half * 128:(half + 1) * 128] = picked.astype(jnp.bfloat16)
            return carry

        steps = rows // chunk // parts
        for part in range(parts):
            field_copy(part).wait()
            lax.fori_loop(part * steps, (part + 1) * steps, split, 0)

    block = order[step]
    weight_copy(step, block).wait()
    inputs = []
    factors = []
    for band in range(bands):
        inputs.append(apart[step * bands + band if listed else column(block, band)])
        real = weights[step, band, 0]
        imag = weights[step, band, 1]
        factors.append(jnp.concatenate([real, imag], 1))
        factors.append(jnp.concatenate([-imag, real], 1))
    result = jnp.dot(
        jnp.concatenate(inputs, 1), jnp.concatenate(factors, 0), preferred_element_type=jnp.float32
    ).astype(jnp.bfloat16)
    first = 0
    for out, count in zip(outs, sizes):
        if len(sizes) == 1:
            out[0] = result
        else:
            @pl.when((step >= first) & (step < first + count))
            def _(out=out):
                out[0] = result
        first += count
    if swap:
        @pl.when(jnp.where(inner[0] > 0, (step >= sizes[0]) & (step < 2 * sizes[0]), step < sizes[0]))
        def _():
            outs[-1][0] = result


def extrapolate_blocks(field, operator, offsets, inner, sets, listed=False, swap=False, limit=60):
    rows, blocks, _, size = field.shape
    bands = offsets.shape[0]
    width = 2 * size
    chunk = 32
    parts = 4
    sizes = [len(one) for one in sets]
    count = sum(sizes)
    order = jnp.array(sum(sets, []), jnp.int32)
    firsts = [sum(sizes[:n]) for n in range(len(sizes))]
    flat = field.reshape(rows * blocks * 2, size)

    def out_spec(first, count):
        return pl.BlockSpec((1, rows, width), lambda j, o, c, i: (jnp.clip(j - first, 0, count - 1), 0, 0))

    def swap_place(j, o, c, i):
        return jnp.clip(j - jnp.where(i[0] > 0, sizes[0], 0), 0, sizes[0] - 1), 0, 0

    out_specs = [out_spec(*one) for one in zip(firsts, sizes)]
    if swap:
        out_specs.append(pl.BlockSpec((1, rows, width), swap_place))
    return pl.pallas_call(
        functools.partial(
            extrapolate_kernel, sets=sets, rows=rows, blocks=blocks, parts=parts, listed=listed, swap=swap
        ),
        grid_spec=pltpu.PrefetchScalarGridSpec(
            num_scalar_prefetch=3,
            grid=(count,),
            in_specs=[pl.BlockSpec(memory_space=pltpu.HBM)] * 2,
            out_specs=out_specs,
            scratch_shapes=[
                pltpu.VMEM(((chunk + 1) * (2 * blocks + 1), size), jnp.float32),
                pltpu.VMEM((count * bands if listed else blocks, rows, width), jnp.bfloat16),
                pltpu.VMEM(flat.shape, jnp.bfloat16),
                pltpu.VMEM((count,) + operator.shape[1:], jnp.bfloat16),
                pltpu.SemaphoreType.DMA((parts,)),
                pltpu.SemaphoreType.DMA((count,)),
            ],
        ),
        out_shape=[jax.ShapeDtypeStruct((n, rows, width), jnp.bfloat16) for n in sizes + sizes[:1] * swap],
        compiler_params=params(limit),
        cost_estimate=SMALL,
        name="extrapolate",
    )(order, offsets, inner, flat, operator)


def chosen(refs, begins, slot, inner):
    field = refs[0][0]
    for part, (begin, is_inner) in zip(refs[1:], begins[1:]):
        place = slot if is_inner else outer_place(slot)
        field = jnp.where(((inner[0] > 0) == is_inner) & (place >= begin), part[0], field)
    return field


def product_kernel(near_ids, far_ids, inner, *refs, begins):
    near_data, far_data, out, turned, total = refs[-5:]
    size = near_data.shape[2]
    tiles = near_data.shape[0]
    sources = refs[0].shape[1] // size
    per_source = tiles // sources

    @pl.when(pl.program_id(0) == 0)
    def _():
        for side, data in enumerate((near_data, far_data)):
            for tile in range(tiles):
                for part in range(2):
                    turned[side * tiles + tile, :, part * size:(part + 1) * size] = data[tile, part].T

    total[...] = jnp.zeros_like(total)
    for side, ids in enumerate((near_ids, far_ids)):
        first = len(begins[0]) * side
        field = chosen(refs[first:first + len(begins[side])], begins[side], pl.program_id(0), inner)
        for source in range(sources):
            upper = field[source * size:(source + 1) * size, :]
            lower = jnp.concatenate([-upper[:, size:], upper[:, :size]], 1)
            both = jnp.concatenate([upper, lower], 0)
            first = side * tiles + source * per_source
            left = turned[first:first + per_source].reshape(per_source * size, 2 * size)
            result = jnp.dot(left, both, preferred_element_type=jnp.float32)
            for tile in range(per_source):
                total[ids[source * per_source + tile]] += result[tile * size:(tile + 1) * size]
    for block in range(total.shape[0]):
        out[0, :, block * size:(block + 1) * size] = total[block].T.astype(jnp.bfloat16)


def part_spec(shape, first, begin, count, is_inner):
    def index(j, a, b, inner):
        place = first + j if is_inner else outer_place(first + j)
        place = jnp.clip(place - begin, 0, count - 1)
        return jnp.where((inner[0] > 0) == is_inner, place, 0), 0, 0

    return pl.BlockSpec(shape, index)


def product_blocks(near, far, near_data, far_data, near_ids, far_ids, inner):
    blocks = len(INNER)
    _, rows, width = near[0][0].shape
    tiles, _, size, _ = near_data.shape
    receivers = NR // size
    parts = near + far
    begins = [[part[1:] for part in side] for side in (near, far)]
    data_spec = pl.BlockSpec(near_data.shape, lambda j, a, b, i: (0, 0, 0, 0))
    return pl.pallas_call(
        functools.partial(product_kernel, begins=begins),
        grid_spec=pltpu.PrefetchScalarGridSpec(
            num_scalar_prefetch=3,
            grid=(blocks,),
            in_specs=[
                part_spec((1, rows, width), 0, begin, field.shape[0], is_inner) for field, begin, is_inner in parts
            ]
            + [data_spec, data_spec],
            out_specs=pl.BlockSpec((1, width, NR), lambda j, a, b, i: (j, 0, 0)),
            scratch_shapes=[
                pltpu.VMEM((2 * tiles, size, width), jnp.bfloat16),
                pltpu.VMEM((receivers, size, width), jnp.float32),
            ],
        ),
        out_shape=jax.ShapeDtypeStruct((blocks, width, NR), jnp.bfloat16),
        compiler_params=params(),
        cost_estimate=SMALL,
        name="product",
    )(near_ids, far_ids, inner, *[field for field, _, _ in parts], near_data, far_data)


def image_kernel(places, unused, inner, *refs, first, begins, size):
    out = refs[-1]
    slot = first + pl.program_id(0)
    parts = refs[len(begins):]
    both = None
    for n, piece in enumerate(begins):
        field = parts[0][0]
        for part, (begin, is_inner) in zip(parts[1:], piece[1:]):
            place = slot if is_inner else outer_place(slot)
            field = jnp.where(((inner[0] > 0) == is_inner) & (place >= begin), part[0], field)
        parts = parts[len(piece):]
        term = jnp.dot(refs[n][0], field, preferred_element_type=jnp.float32)
        both = term if both is None else both + term
    real = both[:size, :size] + both[size:, size:]
    imag = both[size:, :size] - both[:size, size:]
    if len(parts) > 1:
        real += parts[0][0, 0]
        imag += parts[0][0, 1]
    out[0, 0] = real
    out[0, 1] = imag


def image_blocks(product, first, count, pieces, inner, before=None):
    _, rows, width = pieces[0][1][0][0].shape
    size = width // 2
    image_spec = pl.BlockSpec((1, 2, size, size), lambda j, o, u, i: (j, 0, 0, 0))
    specs = [
        pl.BlockSpec((1, width, rows), lambda j, o, u, i, n=n: (first + j, 0, o[n])) for n in range(len(pieces))
    ]
    values = [product] * len(pieces)
    begins = []
    for _, parts in pieces:
        for field, begin, is_inner in parts:
            specs.append(part_spec((1, rows, width), first, begin, field.shape[0], is_inner))
            values.append(field)
        begins.append([(begin, is_inner) for _, begin, is_inner in parts])
    if before is not None:
        specs.append(pl.BlockSpec((1, 2, size, size), lambda j, o, u, i: (first + j, 0, 0, 0)))
        values.append(before)
    places = jnp.stack([shot for shot, _ in pieces])
    return pl.pallas_call(
        functools.partial(image_kernel, first=first, begins=begins, size=size),
        grid_spec=pltpu.PrefetchScalarGridSpec(
            num_scalar_prefetch=3, grid=(count,), in_specs=specs, out_specs=image_spec
        ),
        out_shape=jax.ShapeDtypeStruct((count, 2, size, size), jnp.float32),
        compiler_params=params(),
        cost_estimate=SMALL,
        name="image",
    )(places, places, inner, *values)


def following(value, *earlier):
    return lax.optimization_barrier((value,) + earlier)[0]


def hand(value, *pairs):
    return lax.ppermute(value, "shot", pairs)


def send_sum(value, pairs):
    pairs = [(4 * a + b, 4 * c + d) for (a, b), (c, d) in pairs]
    return lax.ppermute(value.astype(jnp.bfloat16), ("shot", "freq"), pairs).astype(jnp.float32)


def sum_images(one, two, shot, freq):
    left = shot < 2
    shots = range(4)
    even = freq % 2 == 0
    low = freq < 2
    last = one[4:]
    one = one[:4]
    keep = jnp.where(even, jnp.concatenate([one, last]), jnp.concatenate([two, last]))
    send = jnp.where(even, jnp.concatenate([two, last]), jnp.concatenate([one, last]))
    image = keep + send_sum(send, [((s, f), (s, f ^ 1)) for s in shots for f in range(4)])
    keep = jnp.where(low, image[:2], image[2:4])
    send = jnp.where(low, image[2:4], image[:2])
    last = image[4] + send_sum(image[4], [((s, 1), (s, 3)) for s in (1, 2)])
    image = keep + send_sum(send, [((s, f), (s, f ^ 2)) for s in shots for f in range(4)])
    keep = jnp.where(left, image[0], image[1])
    send = jnp.where(left, image[1], image[0])
    image = keep + send_sum(send, [((s, f), (3 - s, f)) for s in shots for f in range(4) if (s, f) != (0, 3)])
    last = send_sum(last, [((1, 3), (3, 3))]) + send_sum(last, [((2, 3), (3, 3))])
    return jnp.where((shot == 3) & (freq == 3), last, image)


def split_body(source_field, receiver_field, operator, band_offsets, survey_tiles, survey_data):
    tiles = survey_data.shape[1]
    shot = lax.axis_index("shot")
    freq = lax.axis_index("freq")
    inner = ((shot == 1) | (shot == 2)).astype(jnp.int32)[None]
    offsets = band_offsets.T
    make = functools.partial(extrapolate_blocks, operator=operator[0], inner=inner)
    inward = ((0, 1), (3, 2))
    outward = ((1, 0), (2, 3))
    middle = ((1, 2), (2, 1))
    ends = ((0, 3), (3, 0))
    beyond = ((1, 3), (2, 0))

    far_data = hand(survey_data[0], *inward, *outward)
    (r_head,) = make(receiver_field[0], offsets=offsets, sets=[INNER[:HEAD]], listed=True)
    r_1_head = hand(r_head, *inward)
    r_3_head = hand(r_head, *middle)
    r_inner, r_outer = make(receiver_field[0], offsets=following(offsets, r_head), sets=[INNER[HEAD:], OUTER])
    r_3_in = hand(r_inner, *middle)
    r_1_in = hand(r_inner, *inward)
    r_1_out = hand(following(r_outer, far_data, r_3_head), *outward)
    s_inner, s_outer, s_rest, s_swap = make(
        source_field[0],
        offsets=following(offsets, r_outer, r_3_head),
        sets=[INNER[:SWAP], OUTER, INNER[SWAP:]],
        swap=True,
    )
    s_far = hand(following(s_swap, r_1_head), *inward, *outward)
    forward_head = hand(r_1_head, *middle)
    s_rest_far = hand(following(s_rest, r_3_in), *inward)
    forward = hand(r_1_in, *middle)
    beyond_1 = hand(following(r_outer, r_1_out)[:LATE], *beyond)
    r_3_out_1 = hand(following(r_outer, s_far, s_rest_far, forward_head)[:HALF], *ends)
    r_3_out_2 = hand(r_outer[HALF:], *ends)
    beyond_2 = hand(r_outer[LATE:], *beyond)

    ids = survey_tiles[:, 1]
    near_ids = lax.dynamic_slice_in_dim(ids, shot * tiles, tiles)
    far_ids = lax.dynamic_slice_in_dim(ids, (shot ^ 1) * tiles, tiles)
    near = [(s_inner, 0, True), (s_rest, SWAP, True), (s_outer, 0, False)]
    far = [(s_far, 0, True), (s_rest_far, SWAP, True), (s_far, 0, False)]
    product = product_blocks(near, far, survey_data[0], far_data, near_ids, far_ids, inner)
    early = [
        (shot, [(r_head, 0, True), (r_inner, HEAD, True), (r_outer, 0, False)]),
        (shot ^ 1, [(r_1_head, 0, True), (r_1_in, HEAD, True), (r_1_out, 0, False)]),
        (shot ^ 3, [(r_3_head, 0, True), (r_3_in, HEAD, True), (r_3_out_1, 0, False), (r_3_out_2, HALF, False)]),
    ]
    forwarded = [(forward_head, 0, True), (forward, HEAD, True)]
    image = image_blocks(product, 0, len(INNER), early, inner)
    most = image_blocks(product, 0, LATE + 1, [(shot ^ 2, forwarded + [(beyond_1, 0, False)])], inner, image)
    rest = image_blocks(
        product, LATE + 1, len(INNER) - LATE - 1, [(shot ^ 2, forwarded + [(beyond_2, LATE, False)])], inner,
        following(image, most),
    )
    one = most[:FIRST]
    two = jnp.concatenate([most[FIRST:], rest])
    image = sum_images(one, two, shot, freq)
    total_freqs = source_field.shape[0] * lax.axis_size("freq")
    return image * (1.0 / math.sqrt(2.0 * NR * total_freqs))


def body(source_field, *rest):
    fits = (
        lax.axis_size("shot") == 4
        and lax.axis_size("freq") == 4
        and source_field.shape[1:] == (512, 16, 2, 128)
    )
    return (split_body if fits else general_body)(source_field, *rest)


def solution(mesh):
    return jax.shard_map(
        body,
        mesh=mesh,
        in_specs=(
            P("freq", ("groups", "shot"), None, None, None),
            P("freq", ("groups", "shot"), None, None, None),
            P("freq", "groups", None, None, None, None),
            P("groups", None),
            P("groups", None),
            P("freq", ("groups", "shot"), None, None, None),
        ),
        out_specs=P(None, ("groups", "shot", "freq"), None),
        check_vma=False,
    )
```

```python
import functools
import math

import jax
import jax.numpy as jnp
from jax import lax
from jax.experimental import pallas as pl
from jax.experimental.pallas import tpu as pltpu
from jax.sharding import PartitionSpec as P

NR = 2048
SMALL = pl.CostEstimate(flops=1000, bytes_accessed=1000, transcendentals=0)


def extrapolate(wavefield, operator, columns):
    row_count, blocks_x, components, block_size = wavefield.shape
    bands = columns.shape[1]
    real_part = operator[:, :, 0]
    imag_part = operator[:, :, 1]
    upper_rows = jnp.concatenate([real_part, imag_part], -1)
    lower_rows = jnp.concatenate([-imag_part, real_part], -1)
    real_block = jnp.concatenate([upper_rows, lower_rows], -2)
    real_block = real_block.reshape(blocks_x, bands, 2 * block_size, 2, block_size)
    chosen = jnp.take(wavefield, columns, axis=1).reshape(
        row_count, blocks_x, bands, 2 * block_size
    )
    result = jnp.einsum("sikc,ikcoy->soiy", chosen, real_block, preferred_element_type=jnp.float32)
    return result.astype(jnp.bfloat16)


def to_owners(wavefield, shot_count, own_cells):
    row_count = wavefield.shape[0]
    return wavefield.reshape(row_count, 2, shot_count, own_cells)


def to_tiles(wavefield, shot_count, own_cells):
    row_count, components, blocks_x, block_size = wavefield.shape
    if own_cells >= block_size:
        return to_owners(wavefield, shot_count, own_cells)
    factor = block_size // own_cells
    copies = jnp.broadcast_to(
        wavefield[:, :, :, None, :], (row_count, components, blocks_x, factor, block_size)
    )
    return copies.reshape(row_count, components, shot_count, block_size)


def data_product(source_cells, data_shard, survey_tiles, block_size, own_cells):
    source_count = source_cells.shape[0]
    receiver_blocks = NR // block_size
    blocks = source_cells.reshape(source_count // block_size, block_size, 2 * own_cells)
    block_ids = jnp.arange(receiver_blocks, dtype=jnp.int32)
    chosen = jnp.take(blocks, survey_tiles[:, 0], axis=0)
    products = jnp.einsum(
        "ncsr,nsk->ncrk",
        lax.all_gather(data_shard, "shot", axis=0, tiled=True),
        chosen,
        preferred_element_type=jnp.float32,
    )
    real_part = products[:, 0, :, :own_cells] - products[:, 1, :, own_cells:]
    imag_part = products[:, 0, :, own_cells:] + products[:, 1, :, :own_cells]
    contribution = jnp.concatenate([real_part, imag_part], -1)
    onehot = (survey_tiles[:, 1][:, None] == block_ids[None, :]).astype(jnp.float32)
    summed = jnp.einsum("nq,nrk->qrk", onehot, contribution, precision=lax.Precision.HIGHEST)
    return summed.reshape(NR, 2, own_cells).astype(jnp.bfloat16)


def image_tile(product, receiver_tile, block_size):
    row_count, components, own_cells = product.shape
    tiles_here = max(own_cells // block_size, 1)
    inner_cells = own_cells // tiles_here
    left = product.reshape(row_count, 2, tiles_here, inner_cells)
    right = receiver_tile.reshape(row_count, 2, tiles_here, block_size)
    turned = jnp.stack([-right[:, 1], right[:, 0]], 1)
    both = jnp.stack([right, turned], 1)
    result = jnp.einsum("rctx,rocty->otxy", left, both, preferred_element_type=jnp.float32)
    return result.reshape(2, own_cells, block_size)


def general_body(source_field, receiver_field, operator, band_offsets, survey_tiles, survey_data):
    shot_count = lax.axis_size("shot")
    freq_local = source_field.shape[0]
    blocks_x = source_field.shape[2]
    block_size = source_field.shape[4]
    own_cells = blocks_x * block_size // shot_count
    block_rows = jnp.arange(blocks_x, dtype=jnp.int32)[:, None]
    columns = (block_rows + band_offsets) % blocks_x
    source_next = extrapolate(source_field[0], operator[0], columns)
    receiver_next = extrapolate(receiver_field[0], operator[0], columns)
    source_send = to_owners(source_next, shot_count, own_cells)
    receiver_send = to_tiles(receiver_next, shot_count, own_cells)
    source_cells = lax.all_to_all(source_send, "shot", split_axis=2, concat_axis=0, tiled=True)
    receiver_tile = lax.all_to_all(receiver_send, "shot", split_axis=2, concat_axis=0, tiled=True)
    source_cells = source_cells.reshape(source_cells.shape[0], 2 * own_cells)
    product = data_product(source_cells, survey_data[0], survey_tiles, block_size, own_cells)
    receiver_tile = receiver_tile.reshape(receiver_tile.shape[0], 2, -1)
    image_sum = image_tile(product, receiver_tile, block_size)
    total_freqs = freq_local * lax.axis_size("freq")
    scaled = image_sum * (1.0 / math.sqrt(2.0 * NR * total_freqs))
    return lax.psum_scatter(scaled, "freq", scatter_dimension=1, tiled=True)


INNER = [4, 8, 6, 10, 15, 5, 9, 7, 11]
HEAD = 3
OUTER = [0, 12, 2, 14, 1, 13, 3]
FIRST = 5
OUTER_FIRST = 4
LATE = 5
SWAP = len(OUTER)
HALF = 4


def outer_place(slot):
    return jnp.where(slot < FIRST, jnp.minimum(slot, OUTER_FIRST - 1), jnp.minimum(slot - 1, len(OUTER) - 1))


def params(limit=24):
    return pltpu.CompilerParams(vmem_limit_bytes=limit * 1024 * 1024)


def extrapolate_kernel(order, offsets, inner, field, operator, *refs, sets, rows, blocks, parts, listed, swap):
    stage, spare, apart, lines, weights, field_sems, weight_sems = refs[-7:]
    outs = refs[:-7]
    sizes = [len(one) for one in sets]
    step = pl.program_id(0)
    bands = operator.shape[1]
    pitch = 2 * blocks + 1
    chunk = stage.shape[0] // pitch - 1
    part_lines = lines.shape[0] // parts

    def column(block, band):
        return lax.rem(block + offsets[band, block] + blocks, blocks)

    def field_copy(part):
        here = pl.ds(part * part_lines, part_lines)
        return pltpu.make_async_copy(field.at[here], lines.at[here], field_sems.at[part])

    def weight_copy(n, block):
        return pltpu.make_async_copy(operator.at[block], weights.at[n], weight_sems.at[n])

    @pl.when(step == 0)
    def _():
        for part in range(parts):
            field_copy(part).start()
        for n, block in enumerate(sum(sets, [])):
            weight_copy(n, block).start()
        if listed:
            wanted = [column(block, band) for block in sum(sets, []) for band in range(bands)]
        else:
            wanted = list(range(blocks))

        def split(pair, carry):
            stages = [(2 * pair, stage), (2 * pair + 1, spare)]
            for n, held in stages:
                for row in range(chunk):
                    here = pl.ds(pl.multiple_of((n * chunk + row) * 2 * blocks, 2 * blocks), 2 * blocks)
                    held[pl.ds(row * pitch, 2 * blocks), :] = lines[here, :].astype(jnp.float32)
            for n, held in stages:
                to = pl.ds(pl.multiple_of(n * chunk, chunk), chunk)
                for slot, block in enumerate(wanted):
                    for half in range(2):
                        picked = held[pl.ds(2 * block + half, chunk, stride=pitch), :]
                        apart[slot, to, half * 128:(half + 1) * 128] = picked.astype(jnp.bfloat16)
            return carry

        steps = rows // (2 * chunk) // parts
        for part in range(parts):
            field_copy(part).wait()
            lax.fori_loop(part * steps, (part + 1) * steps, split, 0)

    block = order[step]
    weight_copy(step, block).wait()
    inputs = []
    factors = []
    for band in range(bands):
        inputs.append(apart[step * bands + band if listed else column(block, band)])
        real = weights[step, band, 0]
        imag = weights[step, band, 1]
        factors.append(jnp.concatenate([real, imag], 1))
        factors.append(jnp.concatenate([-imag, real], 1))
    result = jnp.dot(
        jnp.concatenate(inputs, 1), jnp.concatenate(factors, 0), preferred_element_type=jnp.float32
    ).astype(jnp.bfloat16)
    first = 0
    for out, count in zip(outs, sizes):
        if len(sizes) == 1:
            out[0] = result
        else:
            @pl.when((step >= first) & (step < first + count))
            def _(out=out):
                out[0] = result
        first += count
    if swap:
        @pl.when(jnp.where(inner[0] > 0, (step >= sizes[0]) & (step < 2 * sizes[0]), step < sizes[0]))
        def _():
            outs[-1][0] = result


def extrapolate_blocks(field, operator, offsets, inner, sets, listed=False, swap=False, limit=60):
    rows, blocks, _, size = field.shape
    bands = offsets.shape[0]
    width = 2 * size
    chunk = 32
    parts = 4
    sizes = [len(one) for one in sets]
    count = sum(sizes)
    order = jnp.array(sum(sets, []), jnp.int32)
    firsts = [sum(sizes[:n]) for n in range(len(sizes))]
    flat = field.reshape(rows * blocks * 2, size)

    def out_spec(first, count):
        return pl.BlockSpec((1, rows, width), lambda j, o, c, i: (jnp.clip(j - first, 0, count - 1), 0, 0))

    def swap_place(j, o, c, i):
        return jnp.clip(j - jnp.where(i[0] > 0, sizes[0], 0), 0, sizes[0] - 1), 0, 0

    out_specs = [out_spec(*one) for one in zip(firsts, sizes)]
    if swap:
        out_specs.append(pl.BlockSpec((1, rows, width), swap_place))
    return pl.pallas_call(
        functools.partial(
            extrapolate_kernel, sets=sets, rows=rows, blocks=blocks, parts=parts, listed=listed, swap=swap
        ),
        grid_spec=pltpu.PrefetchScalarGridSpec(
            num_scalar_prefetch=3,
            grid=(count,),
            in_specs=[pl.BlockSpec(memory_space=pltpu.HBM)] * 2,
            out_specs=out_specs,
            scratch_shapes=[
                pltpu.VMEM(((chunk + 1) * (2 * blocks + 1), size), jnp.float32),
                pltpu.VMEM(((chunk + 1) * (2 * blocks + 1), size), jnp.float32),
                pltpu.VMEM((count * bands if listed else blocks, rows, width), jnp.bfloat16),
                pltpu.VMEM(flat.shape, jnp.bfloat16),
                pltpu.VMEM((count,) + operator.shape[1:], jnp.bfloat16),
                pltpu.SemaphoreType.DMA((parts,)),
                pltpu.SemaphoreType.DMA((count,)),
            ],
        ),
        out_shape=[jax.ShapeDtypeStruct((n, rows, width), jnp.bfloat16) for n in sizes + sizes[:1] * swap],
        compiler_params=params(limit),
        cost_estimate=SMALL,
        name="extrapolate",
    )(order, offsets, inner, flat, operator)


def chosen(refs, begins, slot, inner):
    field = refs[0][0]
    for part, (begin, is_inner) in zip(refs[1:], begins[1:]):
        place = slot if is_inner else outer_place(slot)
        field = jnp.where(((inner[0] > 0) == is_inner) & (place >= begin), part[0], field)
    return field


def product_kernel(near_ids, far_ids, inner, *refs, begins):
    near_data, far_data, out, turned, total = refs[-5:]
    size = near_data.shape[2]
    tiles = near_data.shape[0]
    sources = refs[0].shape[1] // size
    per_source = tiles // sources

    @pl.when(pl.program_id(0) == 0)
    def _():
        for side, data in enumerate((near_data, far_data)):
            for tile in range(tiles):
                for part in range(2):
                    turned[side * tiles + tile, :, part * size:(part + 1) * size] = data[tile, part].T

    total[...] = jnp.zeros_like(total)
    for side, ids in enumerate((near_ids, far_ids)):
        first = len(begins[0]) * side
        field = chosen(refs[first:first + len(begins[side])], begins[side], pl.program_id(0), inner)
        for source in range(sources):
            upper = field[source * size:(source + 1) * size, :]
            lower = jnp.concatenate([-upper[:, size:], upper[:, :size]], 1)
            both = jnp.concatenate([upper, lower], 0)
            first = side * tiles + source * per_source
            left = turned[first:first + per_source].reshape(per_source * size, 2 * size)
            result = jnp.dot(left, both, preferred_element_type=jnp.float32)
            for tile in range(per_source):
                total[ids[source * per_source + tile]] += result[tile * size:(tile + 1) * size]
    for block in range(total.shape[0]):
        out[0, :, block * size:(block + 1) * size] = total[block].T.astype(jnp.bfloat16)


def part_spec(shape, first, begin, count, is_inner):
    def index(j, a, b, inner):
        place = first + j if is_inner else outer_place(first + j)
        place = jnp.clip(place - begin, 0, count - 1)
        return jnp.where((inner[0] > 0) == is_inner, place, 0), 0, 0

    return pl.BlockSpec(shape, index)


def product_blocks(near, far, near_data, far_data, near_ids, far_ids, inner):
    blocks = len(INNER)
    _, rows, width = near[0][0].shape
    tiles, _, size, _ = near_data.shape
    receivers = NR // size
    parts = near + far
    begins = [[part[1:] for part in side] for side in (near, far)]
    data_spec = pl.BlockSpec(near_data.shape, lambda j, a, b, i: (0, 0, 0, 0))
    return pl.pallas_call(
        functools.partial(product_kernel, begins=begins),
        grid_spec=pltpu.PrefetchScalarGridSpec(
            num_scalar_prefetch=3,
            grid=(blocks,),
            in_specs=[
                part_spec((1, rows, width), 0, begin, field.shape[0], is_inner) for field, begin, is_inner in parts
            ]
            + [data_spec, data_spec],
            out_specs=pl.BlockSpec((1, width, NR), lambda j, a, b, i: (j, 0, 0)),
            scratch_shapes=[
                pltpu.VMEM((2 * tiles, size, width), jnp.bfloat16),
                pltpu.VMEM((receivers, size, width), jnp.float32),
            ],
        ),
        out_shape=jax.ShapeDtypeStruct((blocks, width, NR), jnp.bfloat16),
        compiler_params=params(),
        cost_estimate=SMALL,
        name="product",
    )(near_ids, far_ids, inner, *[field for field, _, _ in parts], near_data, far_data)


def image_kernel(places, unused, inner, *refs, first, begins, size):
    out = refs[-1]
    slot = first + pl.program_id(0)
    parts = refs[len(begins):]
    both = None
    for n, piece in enumerate(begins):
        field = parts[0][0]
        for part, (begin, is_inner) in zip(parts[1:], piece[1:]):
            place = slot if is_inner else outer_place(slot)
            field = jnp.where(((inner[0] > 0) == is_inner) & (place >= begin), part[0], field)
        parts = parts[len(piece):]
        term = jnp.dot(refs[n][0], field, preferred_element_type=jnp.float32)
        both = term if both is None else both + term
    real = both[:size, :size] + both[size:, size:]
    imag = both[size:, :size] - both[:size, size:]
    if len(parts) > 1:
        real += parts[0][0, 0]
        imag += parts[0][0, 1]
    out[0, 0] = real
    out[0, 1] = imag


def image_blocks(product, first, count, pieces, inner, before=None):
    _, rows, width = pieces[0][1][0][0].shape
    size = width // 2
    image_spec = pl.BlockSpec((1, 2, size, size), lambda j, o, u, i: (j, 0, 0, 0))
    specs = [
        pl.BlockSpec((1, width, rows), lambda j, o, u, i, n=n: (first + j, 0, o[n])) for n in range(len(pieces))
    ]
    values = [product] * len(pieces)
    begins = []
    for _, parts in pieces:
        for field, begin, is_inner in parts:
            specs.append(part_spec((1, rows, width), first, begin, field.shape[0], is_inner))
            values.append(field)
        begins.append([(begin, is_inner) for _, begin, is_inner in parts])
    if before is not None:
        specs.append(pl.BlockSpec((1, 2, size, size), lambda j, o, u, i: (first + j, 0, 0, 0)))
        values.append(before)
    places = jnp.stack([shot for shot, _ in pieces])
    return pl.pallas_call(
        functools.partial(image_kernel, first=first, begins=begins, size=size),
        grid_spec=pltpu.PrefetchScalarGridSpec(
            num_scalar_prefetch=3, grid=(count,), in_specs=specs, out_specs=image_spec
        ),
        out_shape=jax.ShapeDtypeStruct((count, 2, size, size), jnp.float32),
        compiler_params=params(),
        cost_estimate=SMALL,
        name="image",
    )(places, places, inner, *values)


def following(value, *earlier):
    return lax.optimization_barrier((value,) + earlier)[0]


def hand(value, *pairs):
    return lax.ppermute(value, "shot", pairs)


def send_sum(value, pairs):
    pairs = [(4 * a + b, 4 * c + d) for (a, b), (c, d) in pairs]
    return lax.ppermute(value.astype(jnp.bfloat16), ("shot", "freq"), pairs).astype(jnp.float32)


def sum_images(one, two, shot, freq):
    left = shot < 2
    shots = range(4)
    even = freq % 2 == 0
    low = freq < 2
    last = one[4:]
    one = one[:4]
    keep = jnp.where(even, jnp.concatenate([one, last]), jnp.concatenate([two, last]))
    send = jnp.where(even, jnp.concatenate([two, last]), jnp.concatenate([one, last]))
    image = keep + send_sum(send, [((s, f), (s, f ^ 1)) for s in shots for f in range(4)])
    keep = jnp.where(low, image[:2], image[2:4])
    send = jnp.where(low, image[2:4], image[:2])
    last = image[4] + send_sum(image[4], [((s, 1), (s, 3)) for s in (1, 2)])
    image = keep + send_sum(send, [((s, f), (s, f ^ 2)) for s in shots for f in range(4)])
    keep = jnp.where(left, image[0], image[1])
    send = jnp.where(left, image[1], image[0])
    image = keep + send_sum(send, [((s, f), (3 - s, f)) for s in shots for f in range(4) if (s, f) != (0, 3)])
    last = send_sum(last, [((1, 3), (3, 3))]) + send_sum(last, [((2, 3), (3, 3))])
    return jnp.where((shot == 3) & (freq == 3), last, image)


def split_body(source_field, receiver_field, operator, band_offsets, survey_tiles, survey_data):
    tiles = survey_data.shape[1]
    shot = lax.axis_index("shot")
    freq = lax.axis_index("freq")
    inner = ((shot == 1) | (shot == 2)).astype(jnp.int32)[None]
    offsets = band_offsets.T
    make = functools.partial(extrapolate_blocks, operator=operator[0], inner=inner)
    inward = ((0, 1), (3, 2))
    outward = ((1, 0), (2, 3))
    middle = ((1, 2), (2, 1))
    ends = ((0, 3), (3, 0))
    beyond = ((1, 3), (2, 0))

    far_data = hand(survey_data[0], *inward, *outward)
    (r_head,) = make(receiver_field[0], offsets=offsets, sets=[INNER[:HEAD]], listed=True)
    r_1_head = hand(r_head, *inward)
    r_3_head = hand(r_head, *middle)
    r_inner, r_outer = make(receiver_field[0], offsets=following(offsets, r_head), sets=[INNER[HEAD:], OUTER])
    r_3_in = hand(r_inner, *middle)
    r_1_in = hand(r_inner, *inward)
    r_1_out = hand(following(r_outer, far_data, r_3_head), *outward)
    s_inner, s_outer, s_rest, s_swap = make(
        source_field[0],
        offsets=following(offsets, r_outer, r_3_head),
        sets=[INNER[:SWAP], OUTER, INNER[SWAP:]],
        swap=True,
    )
    s_far = hand(following(s_swap, r_1_head), *inward, *outward)
    forward_head = hand(r_1_head, *middle)
    s_rest_far = hand(following(s_rest, r_3_in), *inward)
    forward = hand(r_1_in, *middle)
    beyond_1 = hand(following(r_outer, r_1_out)[:LATE], *beyond)
    r_3_out_1 = hand(following(r_outer, s_far, s_rest_far, forward_head)[:HALF], *ends)
    r_3_out_2 = hand(r_outer[HALF:], *ends)
    beyond_2 = hand(r_outer[LATE:], *beyond)

    ids = survey_tiles[:, 1]
    near_ids = lax.dynamic_slice_in_dim(ids, shot * tiles, tiles)
    far_ids = lax.dynamic_slice_in_dim(ids, (shot ^ 1) * tiles, tiles)
    near = [(s_inner, 0, True), (s_rest, SWAP, True), (s_outer, 0, False)]
    far = [(s_far, 0, True), (s_rest_far, SWAP, True), (s_far, 0, False)]
    product = product_blocks(near, far, survey_data[0], far_data, near_ids, far_ids, inner)
    early = [
        (shot, [(r_head, 0, True), (r_inner, HEAD, True), (r_outer, 0, False)]),
        (shot ^ 1, [(r_1_head, 0, True), (r_1_in, HEAD, True), (r_1_out, 0, False)]),
        (shot ^ 3, [(r_3_head, 0, True), (r_3_in, HEAD, True), (r_3_out_1, 0, False), (r_3_out_2, HALF, False)]),
    ]
    forwarded = [(forward_head, 0, True), (forward, HEAD, True)]
    image = image_blocks(product, 0, len(INNER), early, inner)
    most = image_blocks(product, 0, LATE + 1, [(shot ^ 2, forwarded + [(beyond_1, 0, False)])], inner, image)
    rest = image_blocks(
        product, LATE + 1, len(INNER) - LATE - 1, [(shot ^ 2, forwarded + [(beyond_2, LATE, False)])], inner,
        following(image, most),
    )
    one = most[:FIRST]
    two = jnp.concatenate([most[FIRST:], rest])
    image = sum_images(one, two, shot, freq)
    total_freqs = source_field.shape[0] * lax.axis_size("freq")
    return image * (1.0 / math.sqrt(2.0 * NR * total_freqs))


def body(source_field, *rest):
    fits = (
        lax.axis_size("shot") == 4
        and lax.axis_size("freq") == 4
        and source_field.shape[1:] == (512, 16, 2, 128)
    )
    return (split_body if fits else general_body)(source_field, *rest)


def solution(mesh):
    return jax.shard_map(
        body,
        mesh=mesh,
        in_specs=(
            P("freq", ("groups", "shot"), None, None, None),
            P("freq", ("groups", "shot"), None, None, None),
            P("freq", "groups", None, None, None, None),
            P("groups", None),
            P("groups", None),
            P("freq", ("groups", "shot"), None, None, None),
        ),
        out_specs=P(None, ("groups", "shot", "freq"), None),
        check_vma=False,
    )
```
